32 devices in a mesh: dp: 4 (over y, x), fsdp: 8 (over z, core).
Axes of the slice: x: 2, y: 2, z: 4, core: 2. Of those that a mesh axis runs over, the one named last changes fastest.
Arguments:
- tokens: bfloat16 [384, 256, 512], P(('dp', 'fsdp')), may hold values from -6 to 6
- lengths: int32 [384], P(('dp', 'fsdp')), may hold values from 64 to 250, as said below
- cotangent: bfloat16 [384, 256, 512], P(('dp', 'fsdp')), may hold values from -6 to 6
- qkv_weight: float32 [512, 1536], P(('dp', 'fsdp')), may hold values from -0.25 to 0.25
- out_weight: float32 [512, 512], P(('dp', 'fsdp')), may hold values from -2 to 2
- up_weight: float32 [512, 2048], P(('dp', 'fsdp')), may hold values from -0.25 to 0.25
- down_weight: float32 [2048, 512], P(('dp', 'fsdp')), may hold values from -0.125 to 0.125
- gains: float32 [2, 512], P(None, ('dp', 'fsdp')), may hold values from 0.1 to 1.9
- biases: float32 [6, 512], P(None, ('dp', 'fsdp')), may hold values from -1 to 1
- up_bias: float32 [2048], P(('dp', 'fsdp')), may hold values from -1 to 1
Outputs:
- output: bfloat16 [384, 256, 512], P(('dp', 'fsdp'))
- tokens_grad: bfloat16 [384, 256, 512], P(('dp', 'fsdp'))
- qkv_grad: float32 [512, 1536], P(('dp', 'fsdp'))
- out_grad: float32 [512, 512], P(('dp', 'fsdp'))
- up_grad: float32 [512, 2048], P(('dp', 'fsdp'))
- down_grad: float32 [2048, 512], P(('dp', 'fsdp'))
- gains_grad: float32 [2, 512], P(None, ('dp', 'fsdp'))
- biases_grad: float32 [6, 512], P(None, ('dp', 'fsdp'))
- up_bias_grad: float32 [2048], P(('dp', 'fsdp'))
The draws below stay inside these ranges and needn't reach their ends.
Inputs may be any that keep to these rules, and one draw needn't show every extreme that they name: `lengths`: each length is 64, 128 or 250, and each of the three occurs.
All inputs are finite; a program needn't handle non-finite values.
Results may differ from the reference program's by a relative error of at most 0.012.
The reference program's roundings to bfloat16 on the way count: a program that leaves them out, or rounds other values in their place, can miss the bound.
Values may be sent and summed in bfloat16 or wider, within the bound.
A program may use at most 128 MiB of HBM per device.

```python
import math
import jax
import jax.numpy as jnp
from jax import lax

D = 512
FF = 2048
HEADS = 8
SEQ = 256
SEQS = 384


def draw_lengths(key, part):
    key = jax.random.fold_in(key, 7)
    table = jnp.array([SEQ // 4, SEQ // 2, SEQ - SEQ // 42], jnp.int32)
    picks = jax.random.randint(key, (SEQS,), 0, 3)
    positions = jnp.arange(SEQS, dtype=jnp.int32)
    picks = jnp.where(positions < 3, positions, picks)
    return table[picks]


def levels(rng, shape, pieces, least, largest):
    loudness, own = 1.0, jax.random.fold_in(rng, 6)
    for axis_at, blocks in pieces:
        heights = jnp.exp(jax.random.uniform(jax.random.fold_in(own, axis_at), (blocks,), jnp.float32, least / len(pieces), largest / len(pieces)))
        loudness = loudness * jnp.repeat(heights, shape[axis_at] // blocks).reshape([-1 if axis == axis_at else 1 for axis in range(len(shape))])
    return loudness


def normal_values(stream_key, extent, scale, reach, cuts=(), kind=jnp.bfloat16):
    level = levels(stream_key, extent, cuts, -0.22, 0.18) if cuts else 1.0
    drawn = jax.random.normal(stream_key, extent, jnp.float32) * scale * level
    return jnp.minimum(jnp.maximum(drawn, -reach), reach).astype(kind)


def setup_inputs(seed: int = 0) -> dict:
    streams_of = jax.random.split(jax.random.key(seed), 11)
    tokens = normal_values(streams_of[0], (SEQS, SEQ, D), 1.0, 6.0, ((0, 32),))
    lengths = draw_lengths(jax.random.fold_in(streams_of[10], 71), 0)
    cotangent = normal_values(streams_of[2], (SEQS, SEQ, D), 1.0, 6.0, ((0, 32),))
    qkv_weight = normal_values(streams_of[3], (D, 3 * D), D ** -0.5, 0.25, ((0, 32),), jnp.float32)
    out_weight = normal_values(streams_of[4], (D, D), (D // 64) ** -0.5, 2.0, ((0, 32),), jnp.float32)
    up_weight = normal_values(streams_of[5], (D, FF), D ** -0.5, 0.25, ((0, 32),), jnp.float32)
    down_weight = normal_values(streams_of[6], (FF, D), FF ** -0.5, 0.125, ((0, 32),), jnp.float32)
    gains = jnp.clip(1.0 + 0.18 * jax.random.normal(streams_of[7], (2, D), jnp.float32), 0.1, 1.9)
    biases = normal_values(streams_of[8], (6, D), 0.2, 1.0, ((1, 32),), jnp.float32)
    up_bias = normal_values(streams_of[9], (FF,), 0.2, 1.0, ((0, 32),), jnp.float32)
    return {"tokens": tokens, "lengths": lengths, "cotangent": cotangent, "qkv_weight": qkv_weight, "out_weight": out_weight, "up_weight": up_weight, "down_weight": down_weight, "gains": gains, "biases": biases, "up_bias": up_bias}


@jax.custom_vjp
def low(v):
    return lax.optimization_barrier(v.astype(jnp.bfloat16)).astype(jnp.float32)

@jax.custom_vjp
def low_back(v):
    return v

def low_keep(v):
    return (low(v), None)

def low_pass(kept, grad):
    return (grad,)

def back_keep(v):
    return (v, None)

def back_low(kept, grad):
    return (low(grad),)
low.defvjp(low_keep, low_pass)
low_back.defvjp(back_keep, back_low)

def product(left, right):
    return jnp.matmul(left, right, precision=lax.Precision.HIGHEST)

def layer_norm(values, gain, shift):
    center = values - lax.optimization_barrier(jnp.mean(values, -1, keepdims=True))
    spread = lax.optimization_barrier(jnp.mean(center * center, -1, keepdims=True))
    return center * lax.rsqrt(spread + 1e-05) * gain + shift

def block_layer(inputs, length_part, qkv_weight, out_weight, up_weight, down_weight, gains, biases, up_bias):
    qkv_weight = low(qkv_weight)
    out_weight = low(out_weight)
    up_weight = low(up_weight)
    down_weight = low(down_weight)
    gains = low(gains)
    biases = low(biases)
    up_bias = low(up_bias)
    seq_count, seq_len, model_width = inputs.shape
    head_size = model_width // HEADS
    score_scale = head_size ** (-0.5)
    normed = low(layer_norm(inputs, gains[0], biases[0]))
    joined = product(normed, qkv_weight)
    queries = low(low_back(joined[..., :model_width] + biases[1])).reshape(seq_count, seq_len, HEADS, head_size)
    key_rows = low(low_back(joined[..., model_width:2 * model_width])).reshape(seq_count, seq_len, HEADS, head_size)
    values = low(low_back(joined[..., 2 * model_width:] + biases[2])).reshape(seq_count, seq_len, HEADS, head_size)
    scores = low_back(jnp.einsum('bqhd,bkhd->bhqk', queries, key_rows, precision=lax.Precision.HIGHEST) * score_scale)
    positions = jnp.arange(seq_len)
    key_valid = (positions[None, :] < length_part[:, None])[:, None, None, :]
    logits = jnp.where(key_valid, scores, -1e+30)
    highest = lax.optimization_barrier(jnp.max(logits, -1, keepdims=True))
    exponent = jnp.exp(logits - highest)
    attn_probs = exponent / lax.optimization_barrier(jnp.sum(exponent, -1, keepdims=True))
    context = jnp.einsum('bhqk,bkhd->bqhd', low(attn_probs), values, precision=lax.Precision.HIGHEST)
    context = low(low_back(context.reshape(seq_count, seq_len, model_width)))
    attention = low_back(product(context, out_weight) + biases[3])
    residual = inputs + attention
    normed_two = low(layer_norm(residual, gains[1], biases[4]))
    preact = low_back(product(normed_two, up_weight) + up_bias)
    hidden = low(jax.nn.gelu(preact, approximate=True))
    return residual + product(hidden, down_weight) + biases[5]

def reference(tokens, lengths, cotangent, qkv_weight, out_weight, up_weight, down_weight, gains, biases, up_bias):
    masters = tuple((weight.astype(jnp.float32) for weight in (qkv_weight, out_weight, up_weight, down_weight, gains, biases, up_bias)))
    group = math.gcd(SEQS, 16)
    blocks = SEQS // group
    token_blocks = tokens.reshape(blocks, group, SEQ, D)
    length_blocks = lengths.reshape(blocks, group)
    grad_blocks = cotangent.reshape(blocks, group, SEQ, D)

    def advance(totals, element):
        token_part, length_part, grad_part = element
        inputs = token_part.astype(jnp.float32)

        def applied(inputs_in, *params):
            return block_layer(inputs_in, length_part, *params)
        result, pullback = jax.vjp(applied, inputs, *masters)
        gradients = pullback(grad_part.astype(jnp.float32))
        totals = tuple((total + extra for total, extra in zip(totals, gradients[1:])))
        return (totals, (result.astype(jnp.bfloat16), gradients[0].astype(jnp.bfloat16)))
    zero_grads = tuple((jnp.zeros(master.shape, jnp.float32) for master in masters))
    totals, (results, token_grads) = lax.scan(advance, zero_grads, (token_blocks, length_blocks, grad_blocks))
    return (results.reshape(SEQS, SEQ, D), token_grads.reshape(SEQS, SEQ, D), totals[0], totals[1], totals[2], totals[3], totals[4], totals[5], totals[6])
```

```python
import functools

import jax
import jax.numpy as jnp
from jax import lax
from jax.experimental import pallas as pl
from jax.experimental.pallas import tpu as pltpu
from jax.sharding import PartitionSpec as P

F32, BF = jnp.float32, jnp.bfloat16
MESH = pl.DeviceIdType.MESH
HEADS = 8
EPS = 1e-5
C0 = 0.7978845608028654
C1 = C0 * 0.044715
LANES = 128
NN = (((1,), (0,)), ((), ()))
NT = (((1,), (1,)), ((), ()))
TN = (((0,), (0,)), ((), ()))
VMEM_LIMIT = 60 * 2**20


def dot(a, b, dims=NN):
    return lax.dot_general(a, b, dims, preferred_element_type=F32)


def lane_sums(v):
    total = v[:, :LANES]
    for at in range(LANES, v.shape[1], LANES):
        total = total + v[:, at : at + LANES]
    return total


def normalize(v):
    center = v - jnp.mean(v, 0, keepdims=True)
    inverse = lax.rsqrt(jnp.mean(center * center, 0, keepdims=True) + EPS)
    return center * inverse, inverse


def normalize_back(grad, normed, inverse, gain):
    scaled = grad * gain
    return inverse * (
        scaled
        - jnp.mean(scaled, 0, keepdims=True)
        - normed * jnp.mean(scaled * normed, 0, keepdims=True)
    )


class Place:
    def __init__(self, n_dp, n_z):
        self.n_dp, self.n_z = n_dp, n_z
        self.dp = lax.axis_index("dp")
        fsdp = lax.axis_index("fsdp")
        self.fsdp, self.z, self.core = fsdp, fsdp // 2, fsdp % 2
        self.slot = self.dp * n_z + self.z
        self.mate = (self.dp, self.z * 2 + 1 - self.core)

    def z_of(self, k):
        return lax.rem(self.z + k, self.n_z)

    def dp_of(self, k):
        return lax.rem(self.dp + k, self.n_dp)

    def z_peer(self, k):
        return (self.dp, self.z_of(k) * 2 + self.core)

    def dp_peer(self, k):
        return (self.dp_of(k), self.fsdp)

    def greet(self):
        barrier = pltpu.get_barrier_semaphore()
        peers = [self.mate]
        peers += [self.z_peer(k) for k in range(1, self.n_z)]
        peers += [self.dp_peer(k) for k in range(1, self.n_dp)]
        for peer in peers:
            pl.semaphore_signal(barrier, inc=1, device_id=peer, device_id_type=MESH)
        pl.semaphore_wait(barrier, len(peers))


class Gather:
    def __init__(self, place, own, whole, send, recv):
        self.p, self.own, self.whole, self.send, self.recv = place, own, whole, send, recv

    def put(self, src, slot, core, peer, at):
        pltpu.make_async_remote_copy(
            src_ref=src,
            dst_ref=self.whole.at[slot, core],
            send_sem=self.send.at[at],
            recv_sem=self.recv.at[slot, core],
            device_id=peer,
            device_id_type=MESH,
        ).start()

    def landed(self, slot, core):
        there = self.whole.at[slot, core]
        pltpu.make_async_copy(there, there, self.recv.at[slot, core]).wait()

    def start(self):
        p, at = self.p, 0
        peers = [p.z_peer(k) for k in range(1, p.n_z)]
        peers += [p.dp_peer(k) for k in range(1, p.n_dp)]
        for peer in peers + [p.mate]:
            self.put(self.own, p.slot, p.core, peer, at)
            at += 1

    def along_z(self):
        p = self.p
        at = p.n_z + p.n_dp - 1
        for k in range(1, p.n_z):
            slot = p.dp * p.n_z + p.z_of(k)
            self.landed(slot, p.core)
            for peer in [p.dp_peer(m) for m in range(1, p.n_dp)] + [p.mate]:
                self.put(self.whole.at[slot, p.core], slot, p.core, peer, at)
                at += 1

    def over_dp(self):
        p = self.p
        at = p.n_z + p.n_dp - 1 + (p.n_z - 1) * p.n_dp
        for k in range(0, p.n_z):
            for m in range(1, p.n_dp):
                slot = p.dp_of(m) * p.n_z + p.z_of(k)
                self.landed(slot, p.core)
                self.put(self.whole.at[slot, p.core], slot, p.core, p.mate, at)
                at += 1

    def finish(self):
        p = self.p
        for k in range(0, p.n_z):
            for m in range(0, p.n_dp):
                self.landed(p.dp_of(m) * p.n_z + p.z_of(k), 1 - p.core)
        for at in range(self.sends(p.n_dp, p.n_z)):
            pltpu.make_async_copy(self.own, self.own, self.send.at[at]).wait()

    @staticmethod
    def sends(n_dp, n_z):
        return 2 * n_dp * n_z - 1


def attention_kernel(
    mesh_sizes, gathers, lengths, x_ref, *refs
):
    n_dp, n_z = mesh_sizes
    if gathers:
        (qkv_s, wo_s, wu_s, wd_s, gains_s, biases_s, upb_s,
         qkv_ref, probs_ref, ct_ref, r1_ref, a1_ref, xt_ref, early_ref, wu_ref, wd_ref,
         wqkv_t, wo_t, early, early_own, wu_own, wd_own, small, sems, rems, local) = refs
    else:
        (early_in,
         qkv_ref, probs_ref, ct_ref, r1_ref, a1_ref, xt_ref,
         wqkv_t, wo_t, early) = refs
    step = pl.program_id(0)
    d = x_ref.shape[2]

    if gathers:
        place = Place(n_dp, n_z)
        first = Gather(place, early_own, early, sems.at[0], rems.at[0])
        up = Gather(place, wu_own, wu_ref, sems.at[1], rems.at[1])
        down = Gather(place, wd_own, wd_ref, sems.at[2], rems.at[2])
        own_up = pltpu.make_async_copy(wu_own, wu_ref.at[place.slot, place.core], local.at[0])
        own_down = pltpu.make_async_copy(wd_own, wd_ref.at[place.slot, place.core], local.at[1])
        out_early = pltpu.make_async_copy(early, early_ref, local.at[2])

        @pl.when(step == 0)
        def _():
            place.greet()
            rows = qkv_s.shape[0]
            small[...] = jnp.zeros_like(small)
            small[0:2, :rows] = gains_s[...]
            small[2:8, :rows] = biases_s[...]
            small[8:12, :rows] = upb_s[...]
            early_own[:, : 3 * d] = qkv_s[...].astype(BF)
            early_own[:, 3 * d : 4 * d] = wo_s[...].astype(BF)
            early_own[:, 4 * d :] = small[...].T[:rows].astype(BF)
            wu_own[...] = wu_s[...].astype(BF)
            wd_own[...] = wd_s[...].astype(BF)
            first.start()
            early[place.slot, place.core] = early_own[...]
            first.along_z()
            first.over_dp()
            first.finish()
            own_up.start()
            own_down.start()
            out_early.start()

        for each, at in ((up, 1), (down, 2)):
            pl.when(step == at)(each.start)
            pl.when(step == at + 2)(each.along_z)
            pl.when(step == at + 4)(each.over_dp)
            pl.when(step == at + 6)(each.finish)

        @pl.when(step == 10)
        def _():
            own_up.wait()
            own_down.wait()
            out_early.wait()
    else:

        @pl.when(step == 0)
        def _():
            early[...] = early_in[...].reshape(early.shape)

    @pl.when(step == 0)
    def _():
        whole = early[...].reshape(d, 4 * d + LANES)
        wqkv_t[...] = whole[:, : 3 * d].T
        wo_t[...] = whole[:, 3 * d : 4 * d].T

    column = early[..., 4 * d :].reshape(d, LANES).astype(F32)
    xt = x_ref[0].T
    xt_ref[...] = xt
    x = xt.astype(F32)
    seq = x.shape[1]
    head = d // HEADS
    normed, _ = normalize(x)
    a1 = (normed * column[:, 0:1] + column[:, 2:3]).astype(BF)
    a1_ref[...] = a1
    scale = head**-0.5
    query = (dot(wqkv_t[0:d], a1) + column[:, 3:4]).astype(BF)
    qkv_ref[0:d] = (query.astype(F32) * scale).astype(BF)
    qkv_ref[d : 2 * d] = dot(wqkv_t[d : 2 * d], a1).astype(BF)
    qkv_ref[2 * d :] = (dot(wqkv_t[2 * d :], a1) + column[:, 4:5]).astype(BF)
    valid = lax.broadcasted_iota(jnp.int32, (seq, seq), 0) < lengths[step]
    for h in range(HEADS):
        at = h * head
        scores = dot(qkv_ref[d + at : d + at + head], qkv_ref[at : at + head], TN)
        scores = jnp.where(valid, scores, -1e30)
        exponent = jnp.exp(scores - jnp.max(scores, 0, keepdims=True))
        probs = (exponent * (1.0 / jnp.sum(exponent, 0, keepdims=True))).astype(BF)
        probs_ref[0, h] = probs
        ct_ref[at : at + head] = dot(qkv_ref[2 * d + at : 2 * d + at + head], probs).astype(BF)
    r1_ref[...] = x + dot(wo_t[...], ct_ref[...]) + column[:, 5:6]


def forward_kernel(
    r1_ref, g_ref, column_ref, wu_ref, wd_ref, out_ref, dr1_ref, dwu_ref, dwd_ref, small_ref,
    wu_t, wd_t, gt, a2, total_out, total_a2, total_wu, total_wd, sums, sums_up, up_bias, *, block,
):
    step = pl.program_id(0)
    d, tokens = r1_ref.shape
    hidden = wd_ref.shape[0]
    n_dev = dwd_ref.shape[0] * 2
    rows = d // n_dev
    seqs, seq = g_ref.shape[:2]
    column = column_ref[...].astype(F32)

    @pl.when(step == 0)
    def _():
        wu_t[...] = wu_ref[...].T
        wd_t[...] = wd_ref[...].T
        total_wu[...] = jnp.zeros_like(total_wu)
        total_wd[...] = jnp.zeros_like(total_wd)
        sums[...] = jnp.zeros_like(sums)
        sums_up[...] = jnp.zeros_like(sums_up)
        for r in range(hidden // d):
            up_bias[:, r * rows : (r + 1) * rows, :] = jnp.broadcast_to(
                column[:, 8 + r : 9 + r].reshape(n_dev, rows, 1), (n_dev, rows, LANES)
            )

    for s in range(seqs):
        gt[:, seq * s : seq * (s + 1)] = g_ref[s].T
    r1 = r1_ref[...]
    normed, inverse = normalize(r1)
    a2[...] = (normed * column[:, 1:2] + column[:, 6:7]).astype(BF)
    total_out[...] = r1 + column[:, 7:8]
    total_a2[...] = jnp.zeros_like(total_a2)
    per = block // (hidden // n_dev)

    def body(j, _):
        at = pl.ds(pl.multiple_of(j * block, block), block)
        bias = up_bias[pl.ds(j * per, per)].reshape(block, LANES)[:, 0:1]
        u = dot(wu_t[at, :], a2[...]) + bias
        dh = dot(wd_ref[at, :], gt[...])
        square = u * u
        half = 0.5 + 0.5 * jnp.tanh(u * (C0 + C1 * square))
        h = u * half
        h_low = h.astype(BF)
        slope = half + h * (1.0 - half) * (2 * C0 + 6 * C1 * square)
        du = (dh * slope).astype(BF)
        total_out[...] += dot(wd_t[:, at], h_low)
        total_a2[...] += dot(wu_ref[:, at], du)
        total_wd[at, :] += dot(h_low, gt[...], NT)
        total_wu[:, at] += dot(a2[...], du, NT)
        sums_up[at, :] += lane_sums(du.astype(F32))
        return 0

    lax.fori_loop(0, hidden // block, body, 0)
    for s in range(seqs):
        out_ref[s] = total_out[:, seq * s : seq * (s + 1)].astype(BF).T
    da2 = total_a2[...]
    g = gt[...].astype(F32)
    dr1_ref[...] = g + normalize_back(da2, normed, inverse, column[:, 1:2])
    sums[0] += lane_sums(da2 * normed)
    sums[1] += lane_sums(da2)
    sums[2] += lane_sums(g)

    @pl.when(step == pl.num_programs(0) - 1)
    def _():
        dwu_ref[...] = total_wu[...].astype(BF).reshape(dwu_ref.shape)
        dwd_ref[...] = total_wd[...].astype(BF).reshape(dwd_ref.shape)
        lane = lax.broadcasted_iota(jnp.int32, (d, LANES), 1)
        small = jnp.zeros((d, LANES), F32)
        for s, at in ((0, 1), (1, 6), (2, 7)):
            small = jnp.where(lane == at, jnp.sum(sums[s], 1, keepdims=True), small)
        up = jnp.sum(sums_up[...], 1, keepdims=True).reshape(n_dev, hidden // n_dev, 1)
        for r in range(hidden // d):
            part = up[:, r * rows : (r + 1) * rows].reshape(d, 1)
            small = jnp.where(lane == 8 + r, part, small)
        small_ref[...] = small


class Scatter:
    def __init__(self, place, part, result, bufs, send, recv):
        self.p, self.part, self.result = place, part, result
        self.mine, self.got1, self.sum1, self.got2, self.sum2, self.got3 = bufs
        self.send, self.recv = send, recv

    @staticmethod
    def scratch(n_dp, n_z, rows, width, kind):
        return [
            pltpu.VMEM((n_dp * n_z, rows, width), kind),
            pltpu.VMEM((n_dp * n_z, rows, width), kind),
            pltpu.VMEM((n_dp * n_z, rows, width), kind),
            pltpu.VMEM((n_dp - 1, n_z, rows, width), kind),
            pltpu.VMEM((n_z, rows, width), kind),
            pltpu.VMEM((n_z - 1, rows, width), kind),
        ]

    @staticmethod
    def sems(n_dp, n_z):
        return n_dp + n_z

    def copy(self, src, dst, at, peer):
        return pltpu.make_async_remote_copy(
            src_ref=src,
            dst_ref=dst,
            send_sem=self.send.at[at],
            recv_sem=self.recv.at[at],
            device_id=peer,
            device_id_type=MESH,
        )

    def to_mate(self):
        p = self.p
        return self.copy(self.part.at[:, 1 - p.core], self.got1, 0, p.mate)

    def own(self):
        p = self.p
        return pltpu.make_async_copy(
            self.part.at[:, p.core], self.mine, self.send.at[p.n_dp + p.n_z - 1]
        )

    def over_dp(self):
        p = self.p
        return [
            self.copy(
                self.sum1.at[pl.ds(p.dp_of(k) * p.n_z, p.n_z)], self.got2.at[k - 1], k, p.dp_peer(k)
            )
            for k in range(1, p.n_dp)
        ]

    def along_z(self):
        p = self.p
        return [
            self.copy(
                self.sum2.at[p.z_of(k)], self.got3.at[k - 1], p.n_dp - 1 + k, p.z_peer(k)
            )
            for k in range(1, p.n_z)
        ]

    def step1(self):
        self.to_mate().start()
        self.own().start()

    def step2(self):
        self.own().wait()
        self.to_mate().wait()

        def add(s, _):
            self.sum1[s] = (self.mine[s].astype(F32) + self.got1[s].astype(F32)).astype(
                self.sum1.dtype
            )
            return 0

        lax.fori_loop(0, self.p.n_dp * self.p.n_z, add, 0)
        for copy in self.over_dp():
            copy.start()

    def step3(self):
        for copy in self.over_dp():
            copy.wait()

        def add(s, _):
            total = self.sum1[self.p.dp * self.p.n_z + s].astype(F32)
            for k in range(self.p.n_dp - 1):
                total = total + self.got2[k, s].astype(F32)
            self.sum2[s] = total.astype(self.sum2.dtype)
            return 0

        lax.fori_loop(0, self.p.n_z, add, 0)
        for copy in self.along_z():
            copy.start()

    def step4(self):
        for copy in self.along_z():
            copy.wait()
        total = self.sum2[self.p.z].astype(F32)
        for k in range(self.p.n_z - 1):
            total = total + self.got3[k].astype(F32)
        self.result[...] = total


def backward_kernel(mesh_sizes, scatters, *refs):
    n_dp, n_z = mesh_sizes
    (dr1_ref, xt_ref, a1_ref, ct_ref, qkv_ref, probs_ref, early_ref, part_ref) = refs[:8]
    refs = refs[8:]
    if scatters:
        (dwu_ref, dwd_ref, tg_ref,
         gqkv_ref, gout_ref, gup_ref, gdown_ref, ggains_ref, gbiases_ref, gupb_ref,
         total_qkv, total_out, dp_s, dc_s, sums, part_qkv, part_out, part_small, turn, small_own) = refs[:20]
        buffers, (send, recv) = refs[20:-2], refs[-2:]
    else:
        tg_ref, gqkv_ref, gout_ref, gsmall_ref, total_qkv, total_out, dp_s, dc_s, sums = refs
    step = pl.program_id(0)
    last = pl.num_programs(0) - 1
    d, seq = dr1_ref.shape
    head = d // HEADS
    column = early_ref[:, 4 * d :].astype(F32)

    if scatters:
        place = Place(n_dp, n_z)
        pieces = [
            Scatter(place, part, result, buffers[6 * i : 6 * i + 6], send.at[i], recv.at[i])
            for i, (part, result) in enumerate(
                (
                    (dwd_ref, gdown_ref),
                    (dwu_ref, gup_ref),
                    (part_qkv, gqkv_ref),
                    (part_out, gout_ref),
                    (part_small, small_own),
                )
            )
        ]
        pl.when(step == 0)(place.greet)
        for piece, at in ((pieces[0], 0), (pieces[1], 1)):
            pl.when(step == at)(piece.step1)
            pl.when(step == at + 2)(piece.step2)
            pl.when(step == at + 5)(piece.step3)
            pl.when(step == at + 8)(piece.step4)

    @pl.when(step == 0)
    def _():
        total_qkv[...] = jnp.zeros_like(total_qkv)
        total_out[...] = jnp.zeros_like(total_out)
        sums[...] = jnp.zeros_like(sums)

    dr1 = dr1_ref[...]
    do = dr1.astype(BF)
    total_out[...] += dot(ct_ref[...], do, NT)
    dc_s[...] = dot(early_ref[:, 3 * d : 4 * d], do).astype(BF)
    scale = head**-0.5
    for h in range(HEADS):
        q = slice(h * head, (h + 1) * head)
        k = slice(d + h * head, d + (h + 1) * head)
        v = slice(2 * d + h * head, 2 * d + (h + 1) * head)
        dc = dc_s[q]
        probs = probs_ref[0, h]
        delta = jnp.sum(dc.astype(F32) * ct_ref[q].astype(F32), 0, keepdims=True)
        ds = (probs.astype(F32) * (dot(qkv_ref[v], dc, TN) - delta)).astype(BF)
        dp_s[v] = dot(dc, probs, NT).astype(BF)
        dp_s[k] = dot(qkv_ref[q], ds, NT).astype(BF)
        dp_s[q] = (dot(qkv_ref[k], ds) * scale).astype(BF)
    total_qkv[...] += dot(a1_ref[...], dp_s[...], NT)
    da1 = dot(early_ref[:, : 3 * d], dp_s[...])
    normed, inverse = normalize(xt_ref[...].astype(F32))
    tg_ref[0] = (dr1 + normalize_back(da1, normed, inverse, column[:, 0:1])).astype(BF).T
    sums[0] += lane_sums(da1 * normed)
    sums[1] += lane_sums(da1)
    sums[2] += lane_sums(dp_s[0:d].astype(F32))
    sums[3] += lane_sums(dp_s[2 * d :].astype(F32))
    sums[4] += lane_sums(do.astype(F32))

    @pl.when(step == last)
    def _():
        lane = lax.broadcasted_iota(jnp.int32, (d, LANES), 1)
        small = part_ref[...]
        for s, at in enumerate((0, 2, 3, 4, 5)):
            small = jnp.where(lane == at, jnp.sum(sums[s], 1, keepdims=True), small)
        if not scatters:
            gqkv_ref[...] = total_qkv[...]
            gout_ref[...] = total_out[...]
            gsmall_ref[...] = small
            return
        part_qkv[...] = total_qkv[...].astype(BF).reshape(part_qkv.shape)
        part_out[...] = total_out[...].astype(BF).reshape(part_out.shape)
        part_small[...] = small.reshape(part_small.shape)
        for piece in pieces[2:]:
            piece.step1()
        for piece in pieces[2:]:
            piece.step2()
        for piece in pieces[2:]:
            piece.step3()
        for piece in pieces[2:]:
            piece.step4()
        rows = small_own.shape[0]
        turn[...] = jnp.zeros_like(turn)
        turn[:rows] = small_own[...]
        turned = turn[...].T
        ggains_ref[...] = turned[0:2, :rows]
        gbiases_ref[...] = turned[2:8, :rows]
        gupb_ref[...] = turned[8:12, :rows]


def per_device(n_dp, n_fsdp, tokens, lengths, cotangent, qkv_w, out_w, up_w, down_w, gains, biases, up_bias):
    seqs, seq, d = tokens.shape
    n_z, n_dev = n_fsdp // 2, n_dp * n_fsdp
    rows, rows_down = qkv_w.shape[0], down_w.shape[0]
    hidden = up_w.shape[1]
    slots = n_dp * n_z
    count = seqs * seq
    wide = 4 * d + LANES
    direct = rows % 16 == 0
    axes = ("dp", "fsdp")
    cut = n_dev if direct else 32
    quarter = hidden // d
    up_rows = up_bias.reshape(quarter, rows)

    def whole(shape):
        return pl.BlockSpec(shape, lambda i: (0,) * len(shape), pipeline_mode=pl.Buffered(1))

    def lanes(height, width=seq):
        return pl.BlockSpec((height, width), lambda i: (0, i))

    anywhere = pl.BlockSpec(memory_space=pl.ANY)
    smem = pl.BlockSpec(memory_space=pltpu.SMEM)
    seq_block = pl.BlockSpec((1, seq, d), lambda i: (i, 0, 0))
    probs_block = pl.BlockSpec((1, HEADS, seq, seq), lambda i: (i, 0, 0, 0))

    def shape(dims, kind):
        return jax.ShapeDtypeStruct(dims, kind)

    acts_specs = [lanes(3 * d), probs_block, lanes(d), lanes(d), lanes(d), lanes(d)]
    acts_shapes = [
        shape((3 * d, count), BF),
        shape((seqs, HEADS, seq, seq), BF),
        shape((d, count), BF),
        shape((d, count), F32),
        shape((d, count), BF),
        shape((d, count), BF),
    ]
    turned = [pltpu.VMEM((3 * d, d), BF), pltpu.VMEM((d, d), BF), pltpu.VMEM((slots, 2, rows, wide), BF)]
    if direct:
        n_sends = Gather.sends(n_dp, n_z)
        shards = (qkv_w, out_w, up_w, down_w, gains, biases, up_rows)
        acts = pl.pallas_call(
            functools.partial(attention_kernel, (n_dp, n_z), True),
            grid=(seqs,),
            in_specs=[smem, seq_block] + [whole(s.shape) for s in shards],
            out_specs=acts_specs + [anywhere] * 3,
            out_shape=acts_shapes
            + [
                shape((slots, 2, rows, wide), BF),
                shape((slots, 2, rows, hidden), BF),
                shape((slots, 2, rows_down, d), BF),
            ],
            scratch_shapes=turned
            + [
                pltpu.VMEM((rows, wide), BF),
                pltpu.VMEM((rows, hidden), BF),
                pltpu.VMEM((rows_down, d), BF),
                pltpu.VMEM((LANES, LANES), F32),
                pltpu.SemaphoreType.DMA((3, n_sends)),
                pltpu.SemaphoreType.DMA((3, slots, 2)),
                pltpu.SemaphoreType.DMA((3,)),
            ],
            compiler_params=pltpu.CompilerParams(
                vmem_limit_bytes=VMEM_LIMIT, collective_id=0, has_side_effects=True
            ),
            name="attention_forward",
        )(lengths, tokens, *shards)
        qkv, probs, ct, r1, a1, xt, early, wu, wd = acts
        early = early.reshape(d, wide)
        wu, wd = wu.reshape(d, hidden), wd.reshape(hidden, d)
    else:
        early = jnp.concatenate([qkv_w, out_w, gains.T, biases.T], 1).astype(BF)
        early = lax.all_gather(early, axes, axis=0, tiled=True)
        up_all = lax.all_gather(up_bias.astype(BF), axes, axis=0, tiled=True)
        up_all = up_all.reshape(cut, quarter, d // cut).swapaxes(1, 2).reshape(d, quarter)
        early = jnp.concatenate([early, up_all], 1)
        early = jnp.pad(early, ((0, 0), (0, wide - early.shape[1])))
        wu = lax.all_gather(up_w.astype(BF), axes, axis=0, tiled=True)
        wd = lax.all_gather(down_w.astype(BF), axes, axis=0, tiled=True)
        turned[2] = pltpu.VMEM((d, wide), BF)
        qkv, probs, ct, r1, a1, xt = pl.pallas_call(
            functools.partial(attention_kernel, (n_dp, n_z), False),
            grid=(seqs,),
            in_specs=[smem, seq_block, whole(early.shape)],
            out_specs=acts_specs,
            out_shape=acts_shapes,
            scratch_shapes=turned,
            compiler_params=pltpu.CompilerParams(vmem_limit_bytes=VMEM_LIMIT),
            name="attention_forward",
        )(lengths, tokens, early)

    group = 2 if seqs % 2 == 0 else 1
    chunk = group * seq
    block = 512
    tail = 4 * d // LANES
    out, dr1, dwu, dwd, small = pl.pallas_call(
        functools.partial(forward_kernel, block=block),
        grid=(count // chunk,),
        in_specs=[
            lanes(d, chunk),
            pl.BlockSpec((group, seq, d), lambda i: (i, 0, 0)),
            pl.BlockSpec((d, LANES), lambda i: (0, tail), pipeline_mode=pl.Buffered(1)),
            whole((d, hidden)),
            whole((hidden, d)),
        ],
        out_specs=[
            pl.BlockSpec((group, seq, d), lambda i: (i, 0, 0)),
            lanes(d, chunk),
            whole((cut // 2, 2, d // cut, hidden)),
            whole((cut // 2, 2, hidden // cut, d)),
            whole((d, LANES)),
        ],
        out_shape=[
            shape(tokens.shape, BF),
            shape((d, count), F32),
            shape((cut // 2, 2, d // cut, hidden), BF),
            shape((cut // 2, 2, hidden // cut, d), BF),
            shape((d, LANES), F32),
        ],
        scratch_shapes=[
            pltpu.VMEM((hidden, d), BF),
            pltpu.VMEM((d, hidden), BF),
            pltpu.VMEM((d, chunk), BF),
            pltpu.VMEM((d, chunk), BF),
            pltpu.VMEM((d, chunk), F32),
            pltpu.VMEM((d, chunk), F32),
            pltpu.VMEM((d, hidden), F32),
            pltpu.VMEM((hidden, d), F32),
            pltpu.VMEM((3, d, LANES), F32),
            pltpu.VMEM((hidden, LANES), F32),
            pltpu.VMEM((cut, hidden // cut, LANES), F32),
        ],
        compiler_params=pltpu.CompilerParams(vmem_limit_bytes=VMEM_LIMIT),
        name="feed_forward",
    )(r1, cotangent, early, wu, wd)

    acts_in = [lanes(d), lanes(d), lanes(d), lanes(d), lanes(3 * d), probs_block, whole((d, wide)), whole((d, LANES))]
    base = [
        pltpu.VMEM((d, 3 * d), F32),
        pltpu.VMEM((d, d), F32),
        pltpu.VMEM((3 * d, seq), BF),
        pltpu.VMEM((d, seq), BF),
        pltpu.VMEM((5, d, LANES), F32),
    ]
    if direct:
        n_sems = Scatter.sems(n_dp, n_z)
        plan = ((rows_down, d, BF), (rows, hidden, BF), (rows, 3 * d, BF), (rows, d, BF), (rows, LANES, F32))
        outs = [(rows, 3 * d), (rows, d), (rows, hidden), (rows_down, d), gains.shape, biases.shape, up_rows.shape]
        scratch = list(base)
        for height, width, kind in plan[2:]:
            scratch.append(pltpu.VMEM((slots, 2, height, width), kind))
        scratch += [pltpu.VMEM((LANES, LANES), F32), pltpu.VMEM((rows, LANES), F32)]
        for height, width, kind in plan:
            scratch += Scatter.scratch(n_dp, n_z, height, width, kind)
        scratch += [pltpu.SemaphoreType.DMA((len(plan), n_sems))] * 2
        token_grad, gqkv, gout, gup, gdown, ggains, gbiases, gupb = pl.pallas_call(
            functools.partial(backward_kernel, (n_dp, n_z), True),
            grid=(seqs,),
            in_specs=acts_in + [anywhere, anywhere],
            out_specs=[seq_block] + [whole(o) for o in outs],
            out_shape=[shape(tokens.shape, BF)] + [shape(o, F32) for o in outs],
            scratch_shapes=scratch,
            compiler_params=pltpu.CompilerParams(
                vmem_limit_bytes=VMEM_LIMIT, collective_id=1, has_side_effects=True
            ),
            name="attention_backward",
        )(dr1, xt, a1, ct, qkv, probs, early, small, dwu, dwd)
        return out, token_grad, gqkv, gout, gup, gdown, ggains, gbiases, gupb.reshape(-1)

    token_grad, gqkv, gout, gsmall = pl.pallas_call(
        functools.partial(backward_kernel, (n_dp, n_z), False),
        grid=(seqs,),
        in_specs=acts_in,
        out_specs=[seq_block, whole((d, 3 * d)), whole((d, d)), whole((d, LANES))],
        out_shape=[shape(tokens.shape, BF), shape((d, 3 * d), F32), shape((d, d), F32), shape((d, LANES), F32)],
        scratch_shapes=base,
        compiler_params=pltpu.CompilerParams(vmem_limit_bytes=VMEM_LIMIT),
        name="attention_backward",
    )(dr1, xt, a1, ct, qkv, probs, early, small)

    def scatter(term):
        return lax.psum_scatter(term.astype(F32), axes, scatter_dimension=0, tiled=True)

    up_sums = gsmall[:, 8 : 8 + quarter].reshape(cut, d // cut, quarter).swapaxes(1, 2)
    gsmall = scatter(gsmall[:, :8]).T
    return (
        out,
        token_grad,
        scatter(gqkv),
        scatter(gout),
        scatter(dwu.reshape(d, hidden)),
        scatter(dwd.reshape(hidden, d)),
        gsmall[:2],
        gsmall[2:8],
        scatter(up_sums.reshape(hidden)),
    )


def solution(mesh):
    axes = ("dp", "fsdp")
    rows, cols, flat = P(axes, None), P(None, axes), P(axes)
    data = P(axes, None, None)
    return jax.shard_map(
        functools.partial(per_device, mesh.shape["dp"], mesh.shape["fsdp"]),
        mesh=mesh,
        in_specs=(data, flat, data, rows, rows, rows, rows, cols, cols, flat),
        out_specs=(data, data, rows, rows, rows, rows, cols, cols, flat),
        check_vma=False,
    )
```

```python
import functools

import jax
import jax.numpy as jnp
from jax import lax
from jax.experimental import pallas as pl
from jax.experimental.pallas import tpu as pltpu
from jax.sharding import PartitionSpec as P

F32, BF = jnp.float32, jnp.bfloat16
MESH = pl.DeviceIdType.MESH
HEADS = 8
EPS = 1e-5
C0 = 0.7978845608028654
C1 = C0 * 0.044715
LANES = 128
NN = (((1,), (0,)), ((), ()))
NT = (((1,), (1,)), ((), ()))
TN = (((0,), (0,)), ((), ()))
VMEM_LIMIT = 60 * 2**20


def dot(a, b, dims=NN):
    return lax.dot_general(a, b, dims, preferred_element_type=F32)


def lane_sums(v):
    total = v[:, :LANES]
    for at in range(LANES, v.shape[1], LANES):
        total = total + v[:, at : at + LANES]
    return total


def normalize(v):
    center = v - jnp.mean(v, 0, keepdims=True)
    inverse = lax.rsqrt(jnp.mean(center * center, 0, keepdims=True) + EPS)
    return center * inverse, inverse


def normalize_back(grad, normed, inverse, gain):
    scaled = grad * gain
    return inverse * (
        scaled
        - jnp.mean(scaled, 0, keepdims=True)
        - normed * jnp.mean(scaled * normed, 0, keepdims=True)
    )


class Place:
    def __init__(self, n_dp, n_z):
        self.n_dp, self.n_z = n_dp, n_z
        self.dp = lax.axis_index("dp")
        fsdp = lax.axis_index("fsdp")
        self.fsdp, self.z, self.core = fsdp, fsdp // 2, fsdp % 2
        self.slot = self.dp * n_z + self.z
        self.mate = (self.dp, self.z * 2 + 1 - self.core)

    def z_of(self, k):
        return lax.rem(self.z + k, self.n_z)

    def dp_of(self, k):
        return lax.rem(self.dp + k, self.n_dp)

    def z_peer(self, k):
        return (self.dp, self.z_of(k) * 2 + self.core)

    def dp_peer(self, k):
        return (self.dp_of(k), self.fsdp)

    def greet(self):
        barrier = pltpu.get_barrier_semaphore()
        peers = [self.mate]
        peers += [self.z_peer(k) for k in range(1, self.n_z)]
        peers += [self.dp_peer(k) for k in range(1, self.n_dp)]
        for peer in peers:
            pl.semaphore_signal(barrier, inc=1, device_id=peer, device_id_type=MESH)
        pl.semaphore_wait(barrier, len(peers))


class Gather:
    def __init__(self, place, own, whole, send, recv):
        self.p, self.own, self.whole, self.send, self.recv = place, own, whole, send, recv

    def put(self, src, slot, core, peer, at):
        pltpu.make_async_remote_copy(
            src_ref=src,
            dst_ref=self.whole.at[slot, core],
            send_sem=self.send.at[at],
            recv_sem=self.recv.at[slot, core],
            device_id=peer,
            device_id_type=MESH,
        ).start()

    def landed(self, slot, core):
        there = self.whole.at[slot, core]
        pltpu.make_async_copy(there, there, self.recv.at[slot, core]).wait()

    def start(self):
        p, at = self.p, 0
        peers = [p.z_peer(k) for k in range(1, p.n_z)]
        peers += [p.dp_peer(k) for k in range(1, p.n_dp)]
        for peer in peers + [p.mate]:
            self.put(self.own, p.slot, p.core, peer, at)
            at += 1

    def along_z(self):
        p = self.p
        at = p.n_z + p.n_dp - 1
        for k in range(1, p.n_z):
            slot = p.dp * p.n_z + p.z_of(k)
            self.landed(slot, p.core)
            for peer in [p.dp_peer(m) for m in range(1, p.n_dp)] + [p.mate]:
                self.put(self.whole.at[slot, p.core], slot, p.core, peer, at)
                at += 1

    def over_dp(self):
        p = self.p
        at = p.n_z + p.n_dp - 1 + (p.n_z - 1) * p.n_dp
        for k in range(0, p.n_z):
            for m in range(1, p.n_dp):
                slot = p.dp_of(m) * p.n_z + p.z_of(k)
                self.landed(slot, p.core)
                self.put(self.whole.at[slot, p.core], slot, p.core, p.mate, at)
                at += 1

    def finish(self):
        p = self.p
        for k in range(0, p.n_z):
            for m in range(0, p.n_dp):
                self.landed(p.dp_of(m) * p.n_z + p.z_of(k), 1 - p.core)
        for at in range(self.sends(p.n_dp, p.n_z)):
            pltpu.make_async_copy(self.own, self.own, self.send.at[at]).wait()

    @staticmethod
    def sends(n_dp, n_z):
        return 2 * n_dp * n_z - 1


def attention_kernel(mesh_sizes, gathers, groups, lengths, x_ref, *refs):
    n_dp, n_z = mesh_sizes
    if gathers:
        (qkv_s, wo_s, wu_s, wd_s, gains_s, biases_s, upb_s,
         qkv_ref, probs_ref, ct_ref, r1_ref, a1_ref, early_ref, wo_ref, wu_ref, wd_ref,
         wqkv_t, wo_t, xt_s, normed_s, early, wo, early_own, wo_own, wu_own, wd_own, small, sems, rems, local) = refs
    else:
        (early_in, wo_in,
         qkv_ref, probs_ref, ct_ref, r1_ref, a1_ref,
         wqkv_t, wo_t, xt_s, normed_s, early, wo) = refs
    step = pl.program_id(0)
    group = lax.rem(step, groups)
    many, seq, d = x_ref.shape
    half = d // 2
    head = d // HEADS
    scale = head**-0.5

    if gathers:
        place = Place(n_dp, n_z)
        first = Gather(place, early_own, early, sems.at[0], rems.at[0])
        out = Gather(place, wo_own, wo, sems.at[1], rems.at[1])
        up = Gather(place, wu_own, wu_ref, sems.at[2], rems.at[2])
        down = Gather(place, wd_own, wd_ref, sems.at[3], rems.at[3])
        here = (place.slot, place.core)
        copies = [
            pltpu.make_async_copy(wu_own, wu_ref.at[here], local.at[0]),
            pltpu.make_async_copy(wd_own, wd_ref.at[here], local.at[1]),
            pltpu.make_async_copy(early, early_ref, local.at[2]),
            pltpu.make_async_copy(wo, wo_ref, local.at[3]),
        ]

        @pl.when(step == 0)
        def _():
            rows = qkv_s.shape[0]
            small[...] = jnp.zeros_like(small)
            small[0:2, :rows] = gains_s[...]
            small[2:8, :rows] = biases_s[...]
            for r in range(upb_s.shape[1] // rows):
                small[8 + r : 9 + r, :rows] = upb_s[:, r * rows : (r + 1) * rows]
            early_own[:, : 3 * d] = qkv_s[...].astype(BF)
            early_own[:, 3 * d :] = small[...].T[:rows].astype(BF)
            place.greet()
            first.start()
            wo_own[...] = wo_s[...].astype(BF)
            out.start()
            early[here] = early_own[...]
            wo[here] = wo_own[...]
            wu_own[...] = wu_s[...].astype(BF)
            wd_own[...] = wd_s[...].astype(BF)
            for copy in copies[:2]:
                copy.start()

        plan = {
            1: [first.along_z, out.along_z],
            2: [first.over_dp, out.over_dp],
            3: [up.start, down.start],
            4: [first.finish, out.finish, copies[2].start, copies[3].start],
            5: [up.along_z, down.along_z],
            6: [up.over_dp, down.over_dp],
        }
        for at, actions in plan.items():

            @pl.when(step == at)
            def _(actions=actions):
                for action in actions:
                    action()

    else:

        @pl.when(step == 0)
        def _():
            early[...] = early_in[...].reshape(early.shape)
            wo[...] = wo_in[...].reshape(wo.shape)

    @pl.when(step == groups)
    def _():
        whole = early[...].reshape(d, 3 * d + LANES)
        for hb in range(2):
            for part in range(3):
                to = (hb * 3 + part) * half
                at = part * d + hb * half
                wqkv_t[to : to + half] = whole[:, at : at + half].T
        wo_t[...] = wo[...].reshape(d, d).T

    @pl.when(step < groups)
    def _():
        for s in range(many):
            xt = x_ref[s].T
            xt_s[group, :, seq * s : seq * (s + 1)] = xt
            normed, _ = normalize(xt.astype(F32))
            normed_s[group, :, seq * s : seq * (s + 1)] = normed

    @pl.when(step >= groups)
    def _():
        column = early[..., 3 * d :].reshape(d, LANES).astype(F32)
        a1 = (normed_s[group] * column[:, 0:1] + column[:, 2:3]).astype(BF)
        a1_ref[...] = a1
        for hb in range(2):
            at, rows = hb * 3 * half, slice(hb * half, (hb + 1) * half)
            query = (dot(wqkv_t[at : at + half], a1) + column[rows, 3:4]).astype(BF)
            qkv_ref[at : at + half] = (query.astype(F32) * scale).astype(BF)
            at += half
            qkv_ref[at : at + half] = dot(wqkv_t[at : at + half], a1).astype(BF)
            at += half
            qkv_ref[at : at + half] = (dot(wqkv_t[at : at + half], a1) + column[rows, 4:5]).astype(BF)
        row = lax.broadcasted_iota(jnp.int32, (seq, seq), 0)
        valid = [row < lengths[group * many + s] for s in range(many)]
        items = [(s, h) for s in range(many) for h in range(HEADS)]

        def place_of(s, h, part):
            at = (h // (HEADS // 2) * 3 + part) * half + h % (HEADS // 2) * head
            return slice(at, at + head), slice(seq * s, seq * (s + 1))

        def score(s, h):
            return dot(qkv_ref[place_of(s, h, 1)], qkv_ref[place_of(s, h, 0)], TN)

        def soften(s, scores):
            scores = jnp.where(valid[s], scores, -1e30)
            exponent = jnp.exp(scores - jnp.max(scores, 0, keepdims=True))
            return (exponent * (1.0 / jnp.sum(exponent, 0, keepdims=True))).astype(BF)

        def mix(s, h, probs):
            probs_ref[s, h] = probs
            ct_ref[h * head : (h + 1) * head, seq * s : seq * (s + 1)] = dot(
                qkv_ref[place_of(s, h, 2)], probs
            ).astype(BF)

        def attended(s):
            at = slice(seq * s, seq * (s + 1))
            r1_ref[:, at] = (
                xt_s[group, :, at].astype(F32) + dot(wo_t[...], ct_ref[:, at]) + column[:, 5:6]
            )

        scores, probs = score(*items[0]), None
        for at, (s, h) in enumerate(items):
            ahead = score(*items[at + 1]) if at + 1 < len(items) else None
            if at:
                mix(*items[at - 1], probs)
            if s and h == 2:
                attended(s - 1)
            probs, scores = soften(s, scores), ahead
        mix(*items[-1], probs)

        attended(many - 1)

    if gathers:

        @pl.when(step == 2 * groups - 1)
        def _():
            up.finish()
            down.finish()
            for copy in copies:
                copy.wait()


def forward_kernel(
    r1_first, g_first, r1_next, g_next, column_ref, wu_ref, wd_ref,
    out_ref, dr1_ref, dwu_ref, dwd_ref, small_ref,
    wu_t, wd_t, gt, gt_next, a2, a2_next, normed, inverse, total_out, total_a2, total_wu, total_wd,
    u_s, dh_s, h_s, du_s, sums, sums_up, up_bias, *, block,
):
    step = pl.program_id(0)
    d, tokens = dr1_ref.shape
    hidden = wd_ref.shape[0]
    n_dev = dwd_ref.shape[0] * 2
    rows = d // n_dev
    seqs, seq = g_next.shape[:2]
    column = column_ref[...].astype(F32)
    blocks = hidden // block

    def prepare(r1_ref, g_ref, gt_to, a2_to):
        for s in range(seqs):
            gt_to[:, seq * s : seq * (s + 1)] = g_ref[s].T
        r1 = r1_ref[...]
        n, inv = normalize(r1)
        a2_to[...] = (n * column[:, 1:2] + column[:, 6:7]).astype(BF)
        normed[...] = n
        inverse[...] = jnp.broadcast_to(inv, inverse.shape)
        total_out[...] = r1 + column[:, 7:8]

    @pl.when(step == 0)
    def _():
        wu_t[...] = wu_ref[...].T
        wd_t[...] = wd_ref[...].T
        total_wu[...] = jnp.zeros_like(total_wu)
        total_wd[...] = jnp.zeros_like(total_wd)
        sums[...] = jnp.zeros_like(sums)
        sums_up[...] = jnp.zeros_like(sums_up)
        for r in range(hidden // d):
            up_bias[:, r * rows : (r + 1) * rows, :] = jnp.broadcast_to(
                column[:, 8 + r : 9 + r].reshape(n_dev, rows, 1), (n_dev, rows, LANES)
            )
        prepare(r1_first, g_first, gt, a2)

    per = block // (hidden // n_dev)

    def span(j):
        return slice(j * block, (j + 1) * block)

    def enter(j):
        bias = up_bias[j * per : (j + 1) * per].reshape(block, LANES)[:, 0:1]
        u_s[j % 2] = dot(wu_t[span(j)], a2[...]) + bias
        dh_s[j % 2] = dot(wd_ref[span(j)], gt[...])

    def bend(j):
        u = u_s[j % 2]
        square = u * u
        part = 0.5 + 0.5 * jnp.tanh(u * (C0 + C1 * square))
        h = u * part
        h_s[j] = h.astype(BF)
        slope = part + h * (1.0 - part) * (2 * C0 + 6 * C1 * square)
        du = (dh_s[j % 2] * slope).astype(BF)
        du_s[j] = du
        sums_up[span(j)] += lane_sums(du.astype(F32))

    def leave(j):
        total_out[...] += dot(wd_t[:, span(j)], h_s[j])
        term = dot(wu_ref[:, span(j)], du_s[j])
        total_a2[...] = term if j == 0 else total_a2[...] + term

    def weights(j):
        total_wd[span(j)] += dot(h_s[j], gt[...], NT)
        total_wu[:, span(j)] += dot(a2[...], du_s[j], NT)

    def close():
        for s in range(seqs):
            out_ref[s] = total_out[:, seq * s : seq * (s + 1)].astype(BF).T
        da2, n, g = total_a2[...], normed[...], gt[...].astype(F32)
        dr1_ref[...] = g + normalize_back(da2, n, inverse[0:1], column[:, 1:2])
        sums[0] += lane_sums(da2 * n)
        sums[1] += lane_sums(da2)
        sums[2] += lane_sums(g)

    enter(0)
    for j in range(blocks):
        if j + 1 < blocks:
            enter(j + 1)
        if j:
            leave(j - 1)
        bend(j)
        if 0 < j < blocks - 1:
            weights(j - 1)
    leave(blocks - 1)
    weights(blocks - 2)
    close()
    weights(blocks - 1)
    prepare(r1_next, g_next, gt_next, a2_next)
    gt[...] = gt_next[...]
    a2[...] = a2_next[...]

    @pl.when(step == pl.num_programs(0) - 1)
    def _():
        dwu_ref[...] = total_wu[...].astype(BF).reshape(dwu_ref.shape)
        dwd_ref[...] = total_wd[...].astype(BF).reshape(dwd_ref.shape)
        lane = lax.broadcasted_iota(jnp.int32, (d, LANES), 1)
        small = jnp.zeros((d, LANES), F32)
        for s, at in ((0, 1), (1, 6), (2, 7)):
            small = jnp.where(lane == at, jnp.sum(sums[s], 1, keepdims=True), small)
        up = jnp.sum(sums_up[...], 1, keepdims=True).reshape(n_dev, hidden // n_dev, 1)
        for r in range(hidden // d):
            part = up[:, r * rows : (r + 1) * rows].reshape(d, 1)
            small = jnp.where(lane == 8 + r, part, small)
        small_ref[...] = small


class Scatter:
    def __init__(self, place, part, result, bufs, send, recv):
        self.p, self.part, self.result = place, part, result
        self.mine, self.got1, self.sum1, self.got2, self.sum2, self.got3 = bufs
        self.send, self.recv = send, recv

    @staticmethod
    def scratch(n_dp, n_z, rows, width, kind):
        return [
            pltpu.VMEM((n_dp * n_z, rows, width), kind),
            pltpu.VMEM((n_dp * n_z, rows, width), kind),
            pltpu.VMEM((n_dp * n_z, rows, width), kind),
            pltpu.VMEM((n_dp - 1, n_z, rows, width), kind),
            pltpu.VMEM((n_z, rows, width), kind),
            pltpu.VMEM((n_z - 1, rows, width), kind),
        ]

    @staticmethod
    def sems(n_dp, n_z):
        return n_dp + n_z

    def copy(self, src, dst, at, peer):
        return pltpu.make_async_remote_copy(
            src_ref=src,
            dst_ref=dst,
            send_sem=self.send.at[at],
            recv_sem=self.recv.at[at],
            device_id=peer,
            device_id_type=MESH,
        )

    def to_mate(self):
        p = self.p
        return self.copy(self.part.at[:, 1 - p.core], self.got1, 0, p.mate)

    def own(self):
        p = self.p
        return pltpu.make_async_copy(
            self.part.at[:, p.core], self.mine, self.send.at[p.n_dp + p.n_z - 1]
        )

    def over_dp(self):
        p = self.p
        return [
            self.copy(
                self.sum1.at[pl.ds(p.dp_of(k) * p.n_z, p.n_z)], self.got2.at[k - 1], k, p.dp_peer(k)
            )
            for k in range(1, p.n_dp)
        ]

    def along_z(self):
        p = self.p
        return [
            self.copy(
                self.sum2.at[p.z_of(k)], self.got3.at[k - 1], p.n_dp - 1 + k, p.z_peer(k)
            )
            for k in range(1, p.n_z)
        ]

    def step1(self):
        self.to_mate().start()
        self.own().start()

    def step2(self):
        self.own().wait()
        self.to_mate().wait()

        def add(s, _):
            self.sum1[s] = (self.mine[s].astype(F32) + self.got1[s].astype(F32)).astype(
                self.sum1.dtype
            )
            return 0

        lax.fori_loop(0, self.p.n_dp * self.p.n_z, add, 0)
        for copy in self.over_dp():
            copy.start()

    def step3(self):
        for copy in self.over_dp():
            copy.wait()

        def add(s, _):
            total = self.sum1[self.p.dp * self.p.n_z + s].astype(F32)
            for k in range(self.p.n_dp - 1):
                total = total + self.got2[k, s].astype(F32)
            self.sum2[s] = total.astype(self.sum2.dtype)
            return 0

        lax.fori_loop(0, self.p.n_z, add, 0)
        for copy in self.along_z():
            copy.start()

    def step4(self):
        for copy in self.along_z():
            copy.wait()
        total = self.sum2[self.p.z].astype(F32)
        for k in range(self.p.n_z - 1):
            total = total + self.got3[k].astype(F32)
        self.result[...] = total


def backward_kernel(mesh_sizes, scatters, groups, *refs):
    n_dp, n_z = mesh_sizes
    (dr1_ref, ct_ref, qkv_ref, probs_ref, a1_ref, x_ref, early_ref, wo_ref, part_ref) = refs[:9]
    refs = refs[9:]
    if scatters:
        (dwu_ref, dwd_ref, tg_ref, gqkv_ref, gout_ref, gup_ref, gdown_ref, gsmall_ref,
         dp_s, wqkv, total_qkv, total_out, dc_s, sums, part_qkv, part_out, part_small, gqkv_half) = refs[:18]
        buffers, (send, recv) = refs[18:-2], refs[-2:]
    else:
        (tg_ref, gqkv_ref, gout_ref, gsmall_ref, dp_s, wqkv, total_qkv, total_out, dc_s, sums) = refs
    step = pl.program_id(0)
    last = pl.num_programs(0) - 1
    stage, group = step // groups, lax.rem(step, groups)
    d = dr1_ref.shape[0]
    many, seq = x_ref.shape[:2]
    half, head = d // 2, d // HEADS
    scale = head**-0.5
    column = early_ref[:, 3 * d :].astype(F32)

    @pl.when(step == 0)
    def _():
        sums[...] = jnp.zeros_like(sums)
        for hb in range(2):
            for part in range(3):
                at = part * d + hb * half
                wqkv[hb, :, part * half : (part + 1) * half] = early_ref[:, at : at + half]

    if scatters:
        place = Place(n_dp, n_z)
        down, up, qkv0, qkv1, out, small_piece = [
            Scatter(place, part, result, buffers[6 * i : 6 * i + 6], send.at[i], recv.at[i])
            for i, (part, result) in enumerate(
                (
                    (dwd_ref, gdown_ref),
                    (dwu_ref, gup_ref),
                    (part_qkv.at[0], gqkv_half.at[0]),
                    (part_qkv.at[1], gqkv_half.at[1]),
                    (part_out, gout_ref),
                    (part_small, gsmall_ref),
                )
            )
        ]

        def pack(hb):
            part_qkv[hb] = total_qkv[hb].astype(BF).reshape(part_qkv.shape[1:])

        def pack_out():
            part_out[...] = total_out[...].astype(BF).reshape(part_out.shape)

        plan = {
            0: [place.greet, down.step1, up.step1],
            1: [down.step2],
            2: [up.step2],
            4: [lambda: pack(0), qkv0.step1],
            5: [qkv0.step2, down.step3],
            7: [up.step3],
            8: [lambda: pack(1), qkv1.step1, pack_out, out.step1, down.step4],
            9: [qkv1.step2, out.step2, qkv0.step3],
            10: [up.step4],
            11: [qkv0.step4, qkv1.step3, out.step3],
        }
        for at, actions in plan.items():

            @pl.when(step == at)
            def _(actions=actions):
                for action in actions:
                    action()

    @pl.when(stage < 2)
    def _():
        do = dr1_ref[...].astype(BF)
        mine = pl.ds(pl.multiple_of(stage * half, half), half)
        dc_s[...] = dot(wo_ref[mine, :], do).astype(BF)
        to = dp_s.at[stage, group]
        items = [(s, h) for s in range(many) for h in range(HEADS // 2)]

        def place_of(s, h, part):
            at = part * half + h * head
            return slice(at, at + head), slice(seq * s, seq * (s + 1))

        def grad_probs(s, h):
            return dot(qkv_ref[place_of(s, h, 2)], dc_s[place_of(s, h, 0)], TN)

        def grad_scores(s, h, term):
            at = place_of(s, h, 0)
            delta = jnp.sum(dc_s[at].astype(F32) * ct_ref[at].astype(F32), 0, keepdims=True)
            return (probs_ref[s, h].astype(F32) * (term - delta)).astype(BF)

        def finish(s, h, ds):
            q, k, v = (place_of(s, h, part) for part in range(3))
            to[v] = dot(dc_s[q], probs_ref[s, h], NT).astype(BF)
            to[k] = dot(qkv_ref[q], ds, NT).astype(BF)
            to[q] = (dot(qkv_ref[k], ds) * scale).astype(BF)

        term, ds = grad_probs(*items[0]), None
        for at, item in enumerate(items):
            ahead = grad_probs(*items[at + 1]) if at + 1 < len(items) else None
            if at:
                finish(*items[at - 1], ds)
            ds, term = grad_scores(*item, term), ahead
        opening = group == 0
        term = dot(ct_ref[...], do, NT)
        total_out[mine, :] = jnp.where(opening, term, total_out[mine, :] + term)
        finish(*items[-1], ds)
        term = dot(a1_ref[...], to[...], NT)
        total_qkv[stage] = jnp.where(opening, term, total_qkv[stage] + term)
        sums[2, mine, :] += lane_sums(to[0:half].astype(F32))
        sums[3, mine, :] += lane_sums(to[2 * half :].astype(F32))
        sums[4, mine, :] += lane_sums(dr1_ref[mine, :].astype(BF).astype(F32))

    @pl.when(stage == 2)
    def _():
        def product(s):
            at = slice(seq * s, seq * (s + 1))
            return dot(wqkv[0], dp_s[0, group, :, at]) + dot(wqkv[1], dp_s[1, group, :, at])

        def finish(s, da1):
            normed, inverse = normalize(x_ref[s].T.astype(F32))
            dv = normalize_back(da1, normed, inverse, column[:, 0:1])
            tg_ref[s] = (dr1_ref[:, seq * s : seq * (s + 1)] + dv).astype(BF).T
            sums[0] += lane_sums(da1 * normed)
            sums[1] += lane_sums(da1)

        da1 = product(0)
        for s in range(many):
            ahead = product(s + 1) if s + 1 < many else None
            finish(s, da1)
            da1 = ahead

    @pl.when(step == last)
    def _():
        lane = lax.broadcasted_iota(jnp.int32, (d, LANES), 1)
        small = part_ref[...]
        for s, at in enumerate((0, 2, 3, 4, 5)):
            small = jnp.where(lane == at, jnp.sum(sums[s], 1, keepdims=True), small)
        if not scatters:
            for hb in range(2):
                for part in range(3):
                    at = part * d + hb * half
                    gqkv_ref[:, at : at + half] = total_qkv[hb, :, part * half : (part + 1) * half]
            gout_ref[...] = total_out[...]
            gsmall_ref[...] = small
            return
        part_small[...] = small.reshape(part_small.shape)
        small_piece.step1()
        qkv1.step4()
        small_piece.step2()
        out.step4()
        small_piece.step3()
        for hb in range(2):
            for part in range(3):
                at = part * d + hb * half
                gqkv_ref[:, at : at + half] = gqkv_half[hb, :, part * half : (part + 1) * half]
        small_piece.step4()


def finish_kernel(tg, qkv, out, up, down, small, tg_to, qkv_to, out_to, up_to, down_to, gains, biases, upb, turn, sems):
    copies = [
        pltpu.make_async_copy(tg.at[s], tg_to.at[s], sems.at[s]) for s in range(tg.shape[0])
    ]
    pairs = ((qkv, qkv_to), (out, out_to), (up, up_to), (down, down_to))
    copies += [
        pltpu.make_async_copy(a, b, sems.at[tg.shape[0] + i]) for i, (a, b) in enumerate(pairs)
    ]
    for copy in copies:
        copy.start()
    rows = small.shape[0]
    turn[...] = jnp.zeros_like(turn)
    turn[:rows] = small[...]
    turned = turn[...].T
    gains[...] = turned[0:2, :rows]
    biases[...] = turned[2:8, :rows]
    for r in range(upb.shape[1] // rows):
        upb[:, r * rows : (r + 1) * rows] = turned[8 + r : 9 + r, :rows]
    for copy in copies:
        copy.wait()


def per_device(n_dp, n_fsdp, tokens, lengths, cotangent, qkv_w, out_w, up_w, down_w, gains, biases, up_bias):
    seqs, seq, d = tokens.shape
    n_z, n_dev = n_fsdp // 2, n_dp * n_fsdp
    rows, rows_down = qkv_w.shape[0], down_w.shape[0]
    hidden = up_w.shape[1]
    half = d // 2
    slots = n_dp * n_z
    count = seqs * seq
    wide = 3 * d + LANES
    axes = ("dp", "fsdp")
    direct = rows % 16 == 0
    cut = n_dev if direct else 32
    quarter = hidden // d
    many = next(m for m in (3, 2, 1) if seqs % m == 0)
    groups, width = seqs // many, many * seq

    def whole(shape):
        return pl.BlockSpec(shape, lambda i: (0,) * len(shape), pipeline_mode=pl.Buffered(1))

    def shape(dims, kind):
        return jax.ShapeDtypeStruct(dims, kind)

    anywhere = pl.BlockSpec(memory_space=pl.ANY)
    smem = pl.BlockSpec(memory_space=pltpu.SMEM)

    def norms(i):
        return jnp.minimum(i, groups - 1)

    def heads(i):
        return jnp.maximum(i - groups, 0)

    def lanes(height):
        return pl.BlockSpec((height, width), lambda i: (0, heads(i)))

    acts_specs = [
        lanes(3 * d),
        pl.BlockSpec((many, HEADS, seq, seq), lambda i: (heads(i), 0, 0, 0)),
        lanes(d),
        lanes(d),
        lanes(d),
    ]
    acts_shapes = [
        shape((3 * d, count), BF),
        shape((seqs, HEADS, seq, seq), BF),
        shape((d, count), BF),
        shape((d, count), F32),
        shape((d, count), BF),
    ]
    in_specs = [smem, pl.BlockSpec((many, seq, d), lambda i: (norms(i), 0, 0))]
    grid_shape = (slots, 2, rows) if direct else (d,)
    scratch = [
        pltpu.VMEM((3 * d, d), BF),
        pltpu.VMEM((d, d), BF),
        pltpu.VMEM((groups, d, width), BF),
        pltpu.VMEM((groups, d, width), F32),
        pltpu.VMEM((*grid_shape, wide), BF),
        pltpu.VMEM((*grid_shape, d), BF),
    ]
    if direct:
        n_sends = Gather.sends(n_dp, n_z)
        shards = (qkv_w, out_w, up_w, down_w, gains, biases, up_bias.reshape(1, -1))
        qkv, probs, ct, r1, a1, early, wo, wu, wd = pl.pallas_call(
            functools.partial(attention_kernel, (n_dp, n_z), True, groups),
            grid=(2 * groups,),
            in_specs=in_specs + [whole(s.shape) for s in shards],
            out_specs=acts_specs + [anywhere] * 4,
            out_shape=acts_shapes
            + [
                shape((slots, 2, rows, wide), BF),
                shape((slots, 2, rows, d), BF),
                shape((slots, 2, rows, hidden), BF),
                shape((slots, 2, rows_down, d), BF),
            ],
            scratch_shapes=scratch
            + [
                pltpu.VMEM((rows, wide), BF),
                pltpu.VMEM((rows, d), BF),
                pltpu.VMEM((rows, hidden), BF),
                pltpu.VMEM((rows_down, d), BF),
                pltpu.VMEM((LANES, LANES), F32),
                pltpu.SemaphoreType.DMA((4, n_sends)),
                pltpu.SemaphoreType.DMA((4, slots, 2)),
                pltpu.SemaphoreType.DMA((4,)),
            ],
            compiler_params=pltpu.CompilerParams(
                vmem_limit_bytes=VMEM_LIMIT, collective_id=0, has_side_effects=True
            ),
            name="attention_forward",
        )(lengths, tokens, *shards)
        early, wo = early.reshape(d, wide), wo.reshape(d, d)
        wu, wd = wu.reshape(d, hidden), wd.reshape(hidden, d)
    else:
        early = jnp.concatenate([qkv_w, gains.T, biases.T], 1).astype(BF)
        early = lax.all_gather(early, axes, axis=0, tiled=True)
        up_all = lax.all_gather(up_bias.astype(BF), axes, axis=0, tiled=True)
        up_all = up_all.reshape(cut, quarter, d // cut).swapaxes(1, 2).reshape(d, quarter)
        early = jnp.concatenate([early, up_all], 1)
        early = jnp.pad(early, ((0, 0), (0, wide - early.shape[1])))
        wo = lax.all_gather(out_w.astype(BF), axes, axis=0, tiled=True)
        wu = lax.all_gather(up_w.astype(BF), axes, axis=0, tiled=True)
        wd = lax.all_gather(down_w.astype(BF), axes, axis=0, tiled=True)
        qkv, probs, ct, r1, a1 = pl.pallas_call(
            functools.partial(attention_kernel, (n_dp, n_z), False, groups),
            grid=(2 * groups,),
            in_specs=in_specs + [whole(early.shape), whole(wo.shape)],
            out_specs=acts_specs,
            out_shape=acts_shapes,
            scratch_shapes=scratch,
            compiler_params=pltpu.CompilerParams(vmem_limit_bytes=VMEM_LIMIT),
            name="attention_forward",
        )(lengths, tokens, early, wo)

    pair = 2 if seqs % 2 == 0 else 1
    chunk = pair * seq
    chunks = seqs // pair
    block = d
    tail = 3 * d // LANES

    def following(i):
        return jnp.minimum(i + 1, chunks - 1)

    out, dr1, dwu, dwd, small = pl.pallas_call(
        functools.partial(forward_kernel, block=block),
        grid=(chunks,),
        in_specs=[
            whole((d, chunk)),
            whole((pair, seq, d)),
            pl.BlockSpec((d, chunk), lambda i: (0, following(i))),
            pl.BlockSpec((pair, seq, d), lambda i: (following(i), 0, 0)),
            pl.BlockSpec((d, LANES), lambda i: (0, tail), pipeline_mode=pl.Buffered(1)),
            whole((d, hidden)),
            whole((hidden, d)),
        ],
        out_specs=[
            pl.BlockSpec((pair, seq, d), lambda i: (i, 0, 0)),
            pl.BlockSpec((d, chunk), lambda i: (0, i)),
            whole((cut // 2, 2, d // cut, hidden)),
            whole((cut // 2, 2, hidden // cut, d)),
            whole((d, LANES)),
        ],
        out_shape=[
            shape(tokens.shape, BF),
            shape((d, count), F32),
            shape((cut // 2, 2, d // cut, hidden), BF),
            shape((cut // 2, 2, hidden // cut, d), BF),
            shape((d, LANES), F32),
        ],
        scratch_shapes=[pltpu.VMEM((hidden, d), BF), pltpu.VMEM((d, hidden), BF)]
        + [pltpu.VMEM((d, chunk), BF)] * 4
        + [pltpu.VMEM((d, chunk), F32), pltpu.VMEM((8, chunk), F32)]
        + [pltpu.VMEM((d, chunk), F32)] * 2
        + [pltpu.VMEM((d, hidden), F32), pltpu.VMEM((hidden, d), F32)]
        + [pltpu.VMEM((2, block, chunk), F32)] * 2
        + [pltpu.VMEM((hidden // block, block, chunk), BF)] * 2
        + [
            pltpu.VMEM((3, d, LANES), F32),
            pltpu.VMEM((hidden, LANES), F32),
            pltpu.VMEM((cut, hidden // cut, LANES), F32),
        ],
        compiler_params=pltpu.CompilerParams(vmem_limit_bytes=VMEM_LIMIT),
        name="feed_forward",
    )(r1, cotangent, r1, cotangent, early, wu, wd)

    def turn(i):
        return lax.rem(i, groups)

    def hold(i):
        return jnp.where(i < 2 * groups, turn(i), groups - 1)

    def side(i):
        return jnp.minimum(i // groups, 1)

    def late(i):
        return jnp.where(i < 2 * groups, 0, turn(i))

    seq_block = pl.BlockSpec((many, seq, d), lambda i: (late(i), 0, 0))
    acts_in = [
        pl.BlockSpec((d, width), lambda i: (0, turn(i))),
        pl.BlockSpec((half, width), lambda i: (side(i), hold(i))),
        pl.BlockSpec((3 * half, width), lambda i: (side(i), hold(i))),
        pl.BlockSpec((many, HEADS // 2, seq, seq), lambda i: (hold(i), side(i), 0, 0)),
        pl.BlockSpec((d, width), lambda i: (0, hold(i))),
        seq_block,
        whole((d, wide)),
        whole((d, d)),
        whole((d, LANES)),
    ]
    base = [
        pltpu.VMEM((2, groups, 3 * half, width), BF),
        pltpu.VMEM((2, d, 3 * half), BF),
        pltpu.VMEM((2, d, 3 * half), F32),
        pltpu.VMEM((d, d), F32),
        pltpu.VMEM((half, width), BF),
        pltpu.VMEM((5, d, LANES), F32),
    ]
    acts = (dr1, ct, qkv, probs, a1, tokens, early, wo, small)
    if direct:
        n_sems = Scatter.sems(n_dp, n_z)
        plan = ((rows_down, d, BF), (rows, hidden, BF), (rows, 3 * half, BF), (rows, 3 * half, BF), (rows, d, BF), (rows, LANES, F32))
        outs = [(rows, 3 * d), (rows, d), (rows, hidden), (rows_down, d), (rows, LANES)]
        scratch = base + [
            pltpu.VMEM((2, slots, 2, rows, 3 * half), BF),
            pltpu.VMEM((slots, 2, rows, d), BF),
            pltpu.VMEM((slots, 2, rows, LANES), F32),
            pltpu.VMEM((2, rows, 3 * half), F32),
        ]
        for height, across, kind in plan:
            scratch += Scatter.scratch(n_dp, n_z, height, across, kind)
        scratch += [pltpu.SemaphoreType.DMA((len(plan), n_sems))] * 2
        grads = pl.pallas_call(
            functools.partial(backward_kernel, (n_dp, n_z), True, groups),
            grid=(3 * groups,),
            in_specs=acts_in + [anywhere, anywhere],
            out_specs=[seq_block] + [whole(o) for o in outs],
            out_shape=[shape(tokens.shape, BF)] + [shape(o, F32) for o in outs],
            scratch_shapes=scratch,
            compiler_params=pltpu.CompilerParams(
                vmem_limit_bytes=VMEM_LIMIT, collective_id=1, has_side_effects=True
            ),
            name="attention_backward",
        )(*acts, dwu, dwd)
        ends = [shape(tokens.shape, BF)] + [shape(o, F32) for o in outs[:4]]
        vectors = [shape(v, F32) for v in (gains.shape, biases.shape, (1, quarter * rows))]
        vmem = pl.BlockSpec(memory_space=pltpu.VMEM)
        token_grad, gqkv, gout, gup, gdown, ggains, gbiases, gupb = pl.pallas_call(
            finish_kernel,
            in_specs=[anywhere] * 5 + [vmem],
            out_specs=[anywhere] * 5 + [vmem] * 3,
            out_shape=ends + vectors,
            scratch_shapes=[
                pltpu.VMEM((LANES, LANES), F32),
                pltpu.SemaphoreType.DMA((seqs + 4,)),
            ],
            name="hand_over",
        )(*grads)
        return out, token_grad, gqkv, gout, gup, gdown, ggains, gbiases, gupb.reshape(-1)

    token_grad, gqkv, gout, gsmall = pl.pallas_call(
        functools.partial(backward_kernel, (n_dp, n_z), False, groups),
        grid=(3 * groups,),
        in_specs=acts_in,
        out_specs=[seq_block, whole((d, 3 * d)), whole((d, d)), whole((d, LANES))],
        out_shape=[shape(tokens.shape, BF), shape((d, 3 * d), F32), shape((d, d), F32), shape((d, LANES), F32)],
        scratch_shapes=base,
        compiler_params=pltpu.CompilerParams(vmem_limit_bytes=VMEM_LIMIT),
        name="attention_backward",
    )(*acts)

    def scatter(term):
        return lax.psum_scatter(term.astype(F32), axes, scatter_dimension=0, tiled=True)

    up_sums = gsmall[:, 8 : 8 + quarter].reshape(cut, d // cut, quarter).swapaxes(1, 2)
    gsmall = scatter(gsmall[:, :8]).T
    return (
        out,
        token_grad,
        scatter(gqkv),
        scatter(gout),
        scatter(dwu.reshape(d, hidden)),
        scatter(dwd.reshape(hidden, d)),
        gsmall[:2],
        gsmall[2:8],
        scatter(up_sums.reshape(hidden)),
    )


def solution(mesh):
    axes = ("dp", "fsdp")
    rows, cols, flat = P(axes, None), P(None, axes), P(axes)
    data = P(axes, None, None)
    return jax.shard_map(
        functools.partial(per_device, mesh.shape["dp"], mesh.shape["fsdp"]),
        mesh=mesh,
        in_specs=(data, flat, data, rows, rows, rows, rows, cols, cols, flat),
        out_specs=(data, data, rows, rows, rows, rows, cols, cols, flat),
        check_vma=False,
    )
```

```python
import functools

import jax
import jax.numpy as jnp
from jax import lax
from jax.experimental import pallas as pl
from jax.experimental.pallas import tpu as pltpu
from jax.sharding import PartitionSpec as P

F32, BF = jnp.float32, jnp.bfloat16
MESH = pl.DeviceIdType.MESH
HEADS = 8
EPS = 1e-5
C0 = 0.7978845608028654
C1 = C0 * 0.044715
LANES = 128
NN = (((1,), (0,)), ((), ()))
NT = (((1,), (1,)), ((), ()))
TN = (((0,), (0,)), ((), ()))
VMEM_LIMIT = 60 * 2**20


def dot(a, b, dims=NN):
    return lax.dot_general(a, b, dims, preferred_element_type=F32)


def lane_sums(v):
    total = v[:, :LANES]
    for at in range(LANES, v.shape[1], LANES):
        total = total + v[:, at : at + LANES]
    return total


def normalize(v):
    center = v - jnp.mean(v, 0, keepdims=True)
    inverse = lax.rsqrt(jnp.mean(center * center, 0, keepdims=True) + EPS)
    return center * inverse, inverse


def normalize_back(grad, normed, inverse, gain):
    scaled = grad * gain
    return inverse * (
        scaled
        - jnp.mean(scaled, 0, keepdims=True)
        - normed * jnp.mean(scaled * normed, 0, keepdims=True)
    )


class Place:
    def __init__(self, n_dp, n_z):
        self.n_dp, self.n_z = n_dp, n_z
        self.dp = lax.axis_index("dp")
        fsdp = lax.axis_index("fsdp")
        self.fsdp, self.z, self.core = fsdp, fsdp // 2, fsdp % 2
        self.slot = self.dp * n_z + self.z
        self.mate = (self.dp, self.z * 2 + 1 - self.core)

    def z_of(self, k):
        return lax.rem(self.z + k, self.n_z)

    def dp_of(self, k):
        return lax.rem(self.dp + k, self.n_dp)

    def z_peer(self, k):
        return (self.dp, self.z_of(k) * 2 + self.core)

    def dp_peer(self, k):
        return (self.dp_of(k), self.fsdp)

    def others(self):
        n_fsdp = 2 * self.n_z
        return [
            (self.dp_of(m), lax.rem(self.fsdp + k, n_fsdp))
            for m in range(self.n_dp)
            for k in range(n_fsdp)
            if m or k
        ]

    def greet(self, everyone=False):
        barrier = pltpu.get_barrier_semaphore()
        peers = [self.mate]
        peers += [self.z_peer(k) for k in range(1, self.n_z)]
        peers += [self.dp_peer(k) for k in range(1, self.n_dp)]
        if everyone:
            peers = self.others()
        for peer in peers:
            pl.semaphore_signal(barrier, inc=1, device_id=peer, device_id_type=MESH)
        pl.semaphore_wait(barrier, len(peers))


class Gather:
    def __init__(self, place, own, whole, send, recv, flip=False):
        self.p, self.own, self.whole, self.send, self.recv = place, own, whole, send, recv
        p = place
        by_z = (p.n_z, p.z_peer, lambda near, far: p.dp_of(far) * p.n_z + p.z_of(near))
        by_dp = (p.n_dp, p.dp_peer, lambda near, far: p.dp_of(near) * p.n_z + p.z_of(far))
        (self.near, self.near_peer, self.slot), (self.far, self.far_peer, _) = (
            (by_dp, by_z) if flip else (by_z, by_dp)
        )

    def put(self, src, slot, peer, at):
        pltpu.make_async_remote_copy(
            src_ref=src,
            dst_ref=self.whole.at[slot, self.p.core],
            send_sem=self.send.at[at],
            recv_sem=self.recv.at[slot, self.p.core],
            device_id=peer,
            device_id_type=MESH,
        ).start()

    def landed(self, slot, core):
        there = self.whole.at[slot, core]
        pltpu.make_async_copy(there, there, self.recv.at[slot, core]).wait()

    def far_peers(self):
        return [self.far_peer(m) for m in range(1, self.far)] + [self.p.mate]

    def start(self):
        peers = [self.near_peer(k) for k in range(1, self.near)] + self.far_peers()
        for at, peer in enumerate(peers):
            self.put(self.own, self.p.slot, peer, at)

    def relay(self):
        at = self.near + self.far - 1
        for k in range(1, self.near):
            slot = self.slot(k, 0)
            self.landed(slot, self.p.core)
            for peer in self.far_peers():
                self.put(self.whole.at[slot, self.p.core], slot, peer, at)
                at += 1

    def share(self):
        at = self.near + self.far - 1 + (self.near - 1) * self.far
        for k in range(self.near):
            for m in range(1, self.far):
                slot = self.slot(k, m)
                self.landed(slot, self.p.core)
                self.put(self.whole.at[slot, self.p.core], slot, self.p.mate, at)
                at += 1

    def finish(self):
        for k in range(self.near):
            for m in range(self.far):
                self.landed(self.slot(k, m), 1 - self.p.core)
        for at in range(self.sends(self.p.n_dp, self.p.n_z)):
            pltpu.make_async_copy(self.own, self.own, self.send.at[at]).wait()

    @staticmethod
    def sends(n_dp, n_z):
        return 2 * n_dp * n_z - 1


def attention_kernel(mesh_sizes, gathers, groups, lengths, x_ref, *refs):
    n_dp, n_z = mesh_sizes
    if gathers:
        (qkv_s, wo_s, wu_s, wd_s, gains_s, biases_s, upb_s,
         qkv_ref, probs_ref, ct_ref, r1_ref, a1_ref, early_ref, late_ref, wo_ref, wu_ref, wd_ref,
         wqkv_t, wo_t, xt_s, normed_s, a1_s, ct_s, early, late, wo,
         early_own, late_own, wo_own, wu_own, wd_own, small, sems, rems, local) = refs
    else:
        (early_in, late_in, wo_in,
         qkv_ref, probs_ref, ct_ref, r1_ref, a1_ref,
         wqkv_t, wo_t, xt_s, normed_s, a1_s, ct_s, early, late, wo) = refs
    step = pl.program_id(0)
    stage, group = step // groups, lax.rem(step, groups)
    many, seq, d = x_ref.shape
    half = d // 2
    head = d // HEADS
    scale = head**-0.5

    if gathers:
        place = Place(n_dp, n_z)
        first = Gather(place, early_own, early, sems.at[0], rems.at[0])
        second = Gather(place, late_own, late, sems.at[1], rems.at[1])
        out = Gather(place, wo_own, wo, sems.at[2], rems.at[2])
        up = Gather(place, wu_own, wu_ref, sems.at[3], rems.at[3])
        cut = wd_own.shape[0] // 2
        down = Gather(place, wd_own.at[:cut], wd_ref.at[:, :, :cut], sems.at[4], rems.at[4])
        down2 = Gather(place, wd_own.at[cut:], wd_ref.at[:, :, cut:], sems.at[5], rems.at[5], flip=True)
        here = (place.slot, place.core)
        copies = [
            pltpu.make_async_copy(wu_own, wu_ref.at[here], local.at[0]),
            pltpu.make_async_copy(wd_own, wd_ref.at[here], local.at[1]),
            pltpu.make_async_copy(early, early_ref, local.at[2]),
            pltpu.make_async_copy(late, late_ref, local.at[3]),
            pltpu.make_async_copy(wo, wo_ref, local.at[4]),
        ]

        def enter():
            rows = qkv_s.shape[0]
            small[...] = jnp.zeros_like(small)
            small[0:2, :rows] = gains_s[...]
            small[2:8, :rows] = biases_s[...]
            for r in range(upb_s.shape[1] // rows):
                small[8 + r : 9 + r, :rows] = upb_s[:, r * rows : (r + 1) * rows]
            for part in range(3):
                at = part * d
                early_own[:, part * half : (part + 1) * half] = qkv_s[:, at : at + half].astype(BF)
                late_own[:, part * half : (part + 1) * half] = qkv_s[:, at + half : at + d].astype(BF)
            early_own[:, 3 * half :] = small[...].T[:rows].astype(BF)
            place.greet()
            first.start()
            wo_own[...] = wo_s[...].astype(BF)
            wu_own[...] = wu_s[...].astype(BF)
            wd_own[...] = wd_s[...].astype(BF)
            early[here] = early_own[...]
            late[here] = late_own[...]
            wo[here] = wo_own[...]
            for copy in copies[:2]:
                copy.start()

        plan = plan_forward(groups, enter, first, second, out, up, down, down2, copies)
        for at, actions in plan.items():

            @pl.when(step == at)
            def _(actions=actions):
                for action in actions:
                    action()

    else:

        @pl.when(step == 0)
        def _():
            early[...] = early_in[...].reshape(early.shape)
            late[...] = late_in[...].reshape(late.shape)
            wo[...] = wo_in[...].reshape(wo.shape)

    def columns():
        return early[..., 3 * half :].reshape(d, LANES).astype(F32)

    @pl.when(stage == 0)
    def _():
        for s in range(many):
            xt = x_ref[s].T
            xt_s[group, :, seq * s : seq * (s + 1)] = xt
            normed, _ = normalize(xt.astype(F32))
            normed_s[group, :, seq * s : seq * (s + 1)] = normed

    @pl.when(step == groups)
    def _():
        wqkv_t[...] = early[..., : 3 * half].reshape(d, 3 * half).T

    @pl.when(step == 2 * groups)
    def _():
        wqkv_t[...] = late[...].reshape(d, 3 * half).T
        wo_t[...] = wo[...].reshape(d, d).T

    @pl.when(stage == 1)
    def _():
        column = columns()
        a1 = (normed_s[group] * column[:, 0:1] + column[:, 2:3]).astype(BF)
        a1_s[group] = a1
        a1_ref[...] = a1

    def heads(hb):
        column = columns()
        rows = slice(hb * half, (hb + 1) * half)
        query = (dot(wqkv_t[:half], a1_s[group]) + column[rows, 3:4]).astype(BF)
        qkv_ref[:half] = (query.astype(F32) * scale).astype(BF)
        qkv_ref[half : 2 * half] = dot(wqkv_t[half : 2 * half], a1_s[group]).astype(BF)
        qkv_ref[2 * half :] = (dot(wqkv_t[2 * half :], a1_s[group]) + column[rows, 4:5]).astype(BF)
        row = lax.broadcasted_iota(jnp.int32, (seq, seq), 0)
        valid = [row < lengths[group * many + s] for s in range(many)]
        items = [(s, h) for s in range(many) for h in range(HEADS // 2)]

        def place_of(s, h, part):
            at = part * half + h * head
            return slice(at, at + head), slice(seq * s, seq * (s + 1))

        def score(s, h):
            return dot(qkv_ref[place_of(s, h, 1)], qkv_ref[place_of(s, h, 0)], TN)

        def soften(s, scores):
            scores = jnp.where(valid[s], scores, -1e30)
            exponent = jnp.exp(scores - jnp.max(scores, 0, keepdims=True))
            return (exponent * (1.0 / jnp.sum(exponent, 0, keepdims=True))).astype(BF)

        def mix(s, h, probs):
            probs_ref[s, h] = probs
            ct_ref[place_of(s, h, 0)] = dot(qkv_ref[place_of(s, h, 2)], probs).astype(BF)

        def attended(s):
            at = slice(seq * s, seq * (s + 1))
            term = dot(wo_t[:, :half], ct_s[group, :, at]) + dot(wo_t[:, half:], ct_ref[:, at])
            r1_ref[:, at] = xt_s[group, :, at].astype(F32) + term + column[:, 5:6]

        scores, probs = score(*items[0]), None
        for at, (s, h) in enumerate(items):
            ahead = score(*items[at + 1]) if at + 1 < len(items) else None
            if at:
                mix(*items[at - 1], probs)
            if hb and s and h == 1:
                attended(s - 1)
            probs, scores = soften(s, scores), ahead
        mix(*items[-1], probs)
        if hb:
            attended(many - 1)
        else:
            ct_s[group] = ct_ref[...]

    pl.when(stage == 1)(lambda: heads(0))
    pl.when(stage == 2)(lambda: heads(1))

    if gathers:

        @pl.when(step == 3 * groups - 1)
        def _():
            for each in (up, down, down2):
                each.finish()
            for copy in copies:
                copy.wait()


def plan_forward(groups, enter, first, second, out, up, down, down2, copies):
    return {
        0: [enter],
        1: [second.start, out.start],
        2: [first.relay],
        3: [first.share, up.start, down.start, down2.start],
        4: [first.finish, copies[2].start, second.relay, out.relay],
        5: [up.relay, second.share, out.share],
        6: [down2.relay, down.relay],
        8: [second.finish, out.finish, copies[3].start, copies[4].start, up.share],
        9: [down2.share, down.share],
    }


def forward_kernel(
    r1_first, g_first, r1_next, g_next, column_ref, wu_ref, wd_ref,
    out_ref, dr1_ref, dwu_ref, dwd_ref, small_ref,
    wu_t, wd_t, gt, gt_next, a2, a2_next, normed, inverse, total_out, total_a2, total_wu, total_wd,
    u_s, dh_s, h_s, du_s, sums, sums_up, up_bias, *, block,
):
    step = pl.program_id(0)
    d, tokens = dr1_ref.shape
    hidden = wd_ref.shape[0]
    n_dev = dwd_ref.shape[0] * 2
    rows = d // n_dev
    seqs, seq = g_next.shape[:2]
    column = column_ref[...].astype(F32)
    blocks = hidden // block

    def prepare(r1_ref, g_ref, gt_to, a2_to):
        for s in range(seqs):
            gt_to[:, seq * s : seq * (s + 1)] = g_ref[s].T
        r1 = r1_ref[...]
        n, inv = normalize(r1)
        a2_to[...] = (n * column[:, 1:2] + column[:, 6:7]).astype(BF)
        normed[...] = n
        inverse[...] = jnp.broadcast_to(inv, inverse.shape)
        total_out[...] = r1 + column[:, 7:8]

    @pl.when(step == 0)
    def _():
        wu_t[...] = wu_ref[...].T
        wd_t[...] = wd_ref[...].T
        sums[...] = jnp.zeros_like(sums)
        sums_up[...] = jnp.zeros_like(sums_up)
        for r in range(hidden // d):
            up_bias[:, r * rows : (r + 1) * rows, :] = jnp.broadcast_to(
                column[:, 8 + r : 9 + r].reshape(n_dev, rows, 1), (n_dev, rows, LANES)
            )
        prepare(r1_first, g_first, gt, a2)

    per = block // (hidden // n_dev)

    def span(j):
        return slice(j * block, (j + 1) * block)

    def enter(j):
        bias = up_bias[j * per : (j + 1) * per].reshape(block, LANES)[:, 0:1]
        u_s[j % 2] = dot(wu_t[span(j)], a2[...]) + bias
        dh_s[j % 2] = dot(wd_ref[span(j)], gt[...])

    def bend(j):
        u = u_s[j % 2]
        square = u * u
        part = 0.5 + 0.5 * jnp.tanh(u * (C0 + C1 * square))
        h = u * part
        h_s[j] = h.astype(BF)
        slope = part + h * (1.0 - part) * (2 * C0 + 6 * C1 * square)
        du = (dh_s[j % 2] * slope).astype(BF)
        du_s[j] = du
        sums_up[span(j)] += lane_sums(du.astype(F32))

    def leave(j):
        total_out[...] += dot(wd_t[:, span(j)], h_s[j])
        term = dot(wu_ref[:, span(j)], du_s[j])
        total_a2[...] = term if j == 0 else total_a2[...] + term

    def weights(j):
        term = dot(h_s[j], gt[...], NT)
        total_wd[span(j)] = jnp.where(step == 0, term, total_wd[span(j)] + term)
        term = dot(a2[...], du_s[j], NT)
        total_wu[:, span(j)] = jnp.where(step == 0, term, total_wu[:, span(j)] + term)

    def close():
        for s in range(seqs):
            out_ref[s] = total_out[:, seq * s : seq * (s + 1)].astype(BF).T
        da2, n, g = total_a2[...], normed[...], gt[...].astype(F32)
        dr1_ref[...] = g + normalize_back(da2, n, inverse[0:1], column[:, 1:2])
        sums[0] += lane_sums(da2 * n)
        sums[1] += lane_sums(da2)
        sums[2] += lane_sums(g)

    enter(0)
    for j in range(blocks):
        if j + 1 < blocks:
            enter(j + 1)
        if j:
            leave(j - 1)
        bend(j)
        if 0 < j < blocks - 1:
            weights(j - 1)
    leave(blocks - 1)
    weights(blocks - 2)
    close()
    weights(blocks - 1)
    prepare(r1_next, g_next, gt_next, a2_next)
    gt[...] = gt_next[...]
    a2[...] = a2_next[...]

    @pl.when(step == pl.num_programs(0) - 1)
    def _():
        dwu_ref[...] = total_wu[...].astype(BF).reshape(dwu_ref.shape)
        dwd_ref[...] = total_wd[...].astype(BF).reshape(dwd_ref.shape)
        lane = lax.broadcasted_iota(jnp.int32, (d, LANES), 1)
        small = jnp.zeros((d, LANES), F32)
        for s, at in ((0, 1), (1, 6), (2, 7)):
            small = jnp.where(lane == at, jnp.sum(sums[s], 1, keepdims=True), small)
        up = jnp.sum(sums_up[...], 1, keepdims=True).reshape(n_dev, hidden // n_dev, 1)
        for r in range(hidden // d):
            part = up[:, r * rows : (r + 1) * rows].reshape(d, 1)
            small = jnp.where(lane == 8 + r, part, small)
        small_ref[...] = small


class Scatter:
    def __init__(self, place, part, result, bufs, send, recv, flip=False):
        self.p, self.part, self.result = place, part, result
        self.mine, self.got1, self.sum1, self.got2, self.sum2, self.got3 = bufs
        self.send, self.recv = send, recv
        p = place
        by_z = (p.n_z, p.z_peer, lambda far, near: p.dp_of(near) * p.n_z + p.z_of(far))
        by_dp = (p.n_dp, p.dp_peer, lambda far, near: p.dp_of(far) * p.n_z + p.z_of(near))
        (self.far, self.far_peer, self.slot), (self.near, self.near_peer, _) = (
            (by_z, by_dp) if flip else (by_dp, by_z)
        )

    @staticmethod
    def scratch(n_dp, n_z, rows, width, kind, flip=False):
        far, near = (n_z, n_dp) if flip else (n_dp, n_z)
        return [
            pltpu.VMEM((n_dp * n_z, rows, width), kind),
            pltpu.VMEM((n_dp * n_z, rows, width), kind),
            pltpu.VMEM((n_dp * n_z, rows, width), kind),
            pltpu.VMEM((far - 1, near, rows, width), kind),
            pltpu.VMEM((near, rows, width), kind),
            pltpu.VMEM((near - 1, rows, width), kind),
        ]

    @staticmethod
    def sems(n_dp, n_z):
        return 2 + (max(n_dp, n_z) - 1) * max(n_dp, n_z) + max(n_dp, n_z) - 1

    def copy(self, src, dst, at, peer):
        return pltpu.make_async_remote_copy(
            src_ref=src,
            dst_ref=dst,
            send_sem=self.send.at[at],
            recv_sem=self.recv.at[at],
            device_id=peer,
            device_id_type=MESH,
        )

    def to_mate(self):
        p = self.p
        return self.copy(self.part.at[:, 1 - p.core], self.got1, 0, p.mate)

    def own(self):
        return pltpu.make_async_copy(self.part.at[:, self.p.core], self.mine, self.send.at[1])

    def afar(self):
        return [
            self.copy(
                self.sum1.at[self.slot(k, m)],
                self.got2.at[k - 1, m],
                2 + (k - 1) * self.near + m,
                self.far_peer(k),
            )
            for k in range(1, self.far)
            for m in range(self.near)
        ]

    def nearby(self):
        return [
            self.copy(
                self.sum2.at[m],
                self.got3.at[m - 1],
                2 + (self.far - 1) * self.near + m - 1,
                self.near_peer(m),
            )
            for m in range(1, self.near)
        ]

    def step1(self):
        self.to_mate().start()
        self.own().start()

    def step2(self):
        self.own().wait()
        self.to_mate().wait()

        def add(s, _):
            self.sum1[s] = (self.mine[s].astype(F32) + self.got1[s].astype(F32)).astype(
                self.sum1.dtype
            )
            return 0

        lax.fori_loop(0, self.p.n_dp * self.p.n_z, add, 0)
        for copy in self.afar():
            copy.start()

    def step3(self):
        for copy in self.afar():
            copy.wait()
        for m in range(self.near):
            total = self.sum1[self.slot(0, m)].astype(F32)
            for k in range(self.far - 1):
                total = total + self.got2[k, m].astype(F32)
            self.sum2[m] = total.astype(self.sum2.dtype)
        for copy in self.nearby():
            copy.start()

    def step4(self):
        for copy in self.nearby():
            copy.wait()
        total = self.sum2[0].astype(F32)
        for m in range(self.near - 1):
            total = total + self.got3[m].astype(F32)
        self.result[...] = total


def backward_kernel(mesh_sizes, scatters, groups, *refs):
    n_dp, n_z = mesh_sizes
    (dr1_ref, ct_ref, qkv_ref, probs_ref, a1_ref, x_ref, early_ref, late_ref, wo_ref, part_ref) = refs[:10]
    refs = refs[10:]
    if scatters:
        (dwu_ref, dwd_ref, tg_ref, gqkv_ref, gout_ref, gup_ref, gdown_ref, gsmall_ref,
         dp_s, total_qkv, total_out, dc_s, sums, part_qkv, part_out, part_small, got_small, gqkv_half) = refs[:18]
        buffers, (send, recv, small_send, small_recv) = refs[18:-4], refs[-4:]
    else:
        tg_ref, gqkv_ref, gout_ref, gsmall_ref, dp_s, total_qkv, total_out, dc_s, sums = refs
    step = pl.program_id(0)
    last = pl.num_programs(0) - 1
    stage, group = step // groups, lax.rem(step, groups)
    d = dr1_ref.shape[0]
    many, seq = x_ref.shape[:2]
    half, head = d // 2, d // HEADS
    scale = head**-0.5
    column = early_ref[:, 3 * half :].astype(F32)

    @pl.when(step == 0)
    def _():
        sums[...] = jnp.zeros_like(sums)

    if scatters:
        place = Place(n_dp, n_z)
        cut = dwd_ref.shape[2] // 2
        parts = (
            (dwu_ref, gup_ref, False),
            (dwd_ref.at[:, :, :cut], gdown_ref.at[:cut], False),
            (dwd_ref.at[:, :, cut:], gdown_ref.at[cut:], True),
            (part_qkv.at[0], gqkv_half.at[0], False),
            (part_qkv.at[1], gqkv_half.at[1], False),
            (part_out, gout_ref, False),
        )
        up, down, down2, qkv0, qkv1, out = [
            Scatter(place, part, result, buffers[6 * i : 6 * i + 6], send.at[i], recv.at[i], flip)
            for i, (part, result, flip) in enumerate(parts)
        ]

        def pack(hb):
            part_qkv[hb] = total_qkv[hb].astype(BF).reshape(part_qkv.shape[1:])

        def pack_out():
            part_out[...] = total_out[...].astype(BF).reshape(part_out.shape)

        plan = plan_backward(
            lambda: place.greet(True), up, down, down2, qkv0, qkv1, out,
            lambda: pack(0), lambda: pack(1), pack_out,
        )
        for at, actions in plan.items():

            @pl.when(step == at)
            def _(actions=actions):
                for action in actions:
                    action()

    @pl.when(stage < 2)
    def _():
        do = dr1_ref[...].astype(BF)
        mine = pl.ds(pl.multiple_of(stage * half, half), half)
        dc_s[...] = dot(wo_ref[mine, :], do).astype(BF)
        to = dp_s.at[stage, group]
        items = [(s, h) for s in range(many) for h in range(HEADS // 2)]

        def place_of(s, h, part):
            at = part * half + h * head
            return slice(at, at + head), slice(seq * s, seq * (s + 1))

        def grad_probs(s, h):
            return dot(qkv_ref[place_of(s, h, 2)], dc_s[place_of(s, h, 0)], TN)

        def grad_scores(s, h, term):
            rows, at = place_of(s, h, 0)
            there = pl.ds(pl.multiple_of(stage * half + h * head, head), head)
            delta = dc_s[rows, at].astype(F32) * ct_ref[there, at].astype(F32)
            delta = jnp.sum(delta, 0, keepdims=True)
            return (probs_ref[s, h].astype(F32) * (term - delta)).astype(BF)

        def finish(s, h, ds):
            q, k, v = (place_of(s, h, part) for part in range(3))
            to[v] = dot(dc_s[q], probs_ref[s, h], NT).astype(BF)
            to[k] = dot(qkv_ref[q], ds, NT).astype(BF)
            to[q] = (dot(qkv_ref[k], ds) * scale).astype(BF)

        term, ds = grad_probs(*items[0]), None
        for at, item in enumerate(items):
            ahead = grad_probs(*items[at + 1]) if at + 1 < len(items) else None
            if at:
                finish(*items[at - 1], ds)
            ds, term = grad_scores(*item, term), ahead
        opening = group == 0

        @pl.when(stage == 0)
        def _():
            term = dot(ct_ref[...], dr1_ref[...].astype(BF), NT)
            total_out[...] = jnp.where(opening, term, total_out[...] + term)

        finish(*items[-1], ds)
        term = dot(a1_ref[...], to[...], NT)
        total_qkv[stage] = jnp.where(opening, term, total_qkv[stage] + term)
        sums[2, mine, :] += lane_sums(to[0:half].astype(F32))
        sums[3, mine, :] += lane_sums(to[2 * half :].astype(F32))
        sums[4, mine, :] += lane_sums(dr1_ref[mine, :].astype(BF).astype(F32))

    @pl.when(stage == 2)
    def _():
        def product(s):
            at = slice(seq * s, seq * (s + 1))
            return dot(early_ref[:, : 3 * half], dp_s[0, group, :, at]) + dot(
                late_ref[...], dp_s[1, group, :, at]
            )

        def finish(s, da1):
            normed, inverse = normalize(x_ref[s].T.astype(F32))
            dv = normalize_back(da1, normed, inverse, column[:, 0:1])
            tg_ref[s] = (dr1_ref[:, seq * s : seq * (s + 1)] + dv).astype(BF).T
            sums[0] += lane_sums(da1 * normed)
            sums[1] += lane_sums(da1)

        da1 = product(0)
        for s in range(many):
            ahead = product(s + 1) if s + 1 < many else None
            finish(s, da1)
            da1 = ahead

    @pl.when(step == last)
    def _():
        lane = lax.broadcasted_iota(jnp.int32, (d, LANES), 1)
        small = part_ref[...]
        for s, at in enumerate((0, 2, 3, 4, 5)):
            small = jnp.where(lane == at, jnp.sum(sums[s], 1, keepdims=True), small)
        if not scatters:
            for hb in range(2):
                for part in range(3):
                    at = part * d + hb * half
                    gqkv_ref[:, at : at + half] = total_qkv[hb, :, part * half : (part + 1) * half]
            gout_ref[...] = total_out[...]
            gsmall_ref[...] = small
            return
        part_small[...] = small.reshape(part_small.shape)

        def exchange(at, peer):
            dp, fsdp = peer
            return pltpu.make_async_remote_copy(
                src_ref=part_small.at[dp * n_z + fsdp // 2, fsdp % 2],
                dst_ref=got_small.at[at],
                send_sem=small_send.at[at],
                recv_sem=small_recv.at[at],
                device_id=peer,
                device_id_type=MESH,
            )

        swaps = [exchange(at, peer) for at, peer in enumerate(place.others())]
        for swap in swaps:
            swap.start()
        qkv1.step4()
        for hb in range(2):
            for part in range(3):
                at = part * d + hb * half
                gqkv_ref[:, at : at + half] = gqkv_half[hb, :, part * half : (part + 1) * half]
        total = part_small[place.slot, place.core]
        for at, swap in enumerate(swaps):
            swap.wait()
            total = total + got_small[at]
        gsmall_ref[...] = total


def plan_backward(greet, up, down, down2, qkv0, qkv1, out, pack0, pack1, pack_out):
    return {
        0: [greet, up.step1, down2.step1, down.step1],
        1: [up.step2, down2.step2, down.step2],
        4: [pack0, qkv0.step1, pack_out, out.step1],
        5: [up.step3, down2.step3, qkv0.step2, out.step2],
        7: [down.step3],
        8: [pack1, qkv1.step1, up.step4, down2.step4],
        9: [qkv1.step2, qkv0.step3, out.step3],
        10: [down.step4],
        11: [qkv1.step3, qkv0.step4, out.step4],
    }


def finish_kernel(tg, qkv, out, up, down, small, tg_to, qkv_to, out_to, up_to, down_to, gains, biases, upb, turn):
    tg_to[...] = tg[...]

    @pl.when(pl.program_id(0) == 0)
    def _():
        for source, to in ((qkv, qkv_to), (out, out_to), (up, up_to), (down, down_to)):
            to[...] = source[...]
        rows = small.shape[0]
        turn[...] = jnp.zeros_like(turn)
        turn[:rows] = small[...]
        turned = turn[...].T
        gains[...] = turned[0:2, :rows]
        biases[...] = turned[2:8, :rows]
        for r in range(upb.shape[1] // rows):
            upb[:, r * rows : (r + 1) * rows] = turned[8 + r : 9 + r, :rows]


def per_device(n_dp, n_fsdp, tokens, lengths, cotangent, qkv_w, out_w, up_w, down_w, gains, biases, up_bias):
    seqs, seq, d = tokens.shape
    n_z, n_dev = n_fsdp // 2, n_dp * n_fsdp
    rows, rows_down = qkv_w.shape[0], down_w.shape[0]
    hidden = up_w.shape[1]
    half = d // 2
    slots = n_dp * n_z
    count = seqs * seq
    wide = 3 * half + LANES
    axes = ("dp", "fsdp")
    direct = rows % 16 == 0
    cut = n_dev if direct else 32
    quarter = hidden // d
    many = next(m for m in (3, 2, 1) if seqs % m == 0)
    groups, width = seqs // many, many * seq

    def whole(shape):
        return pl.BlockSpec(shape, lambda i: (0,) * len(shape), pipeline_mode=pl.Buffered(1))

    def shape(dims, kind):
        return jax.ShapeDtypeStruct(dims, kind)

    anywhere = pl.BlockSpec(memory_space=pl.ANY)
    smem = pl.BlockSpec(memory_space=pltpu.SMEM)

    def turn(i):
        return lax.rem(i, groups)

    def norms(i):
        return jnp.minimum(i, groups - 1)

    def heads(i):
        return jnp.where(i < groups, 0, turn(i))

    def side(i):
        return jnp.maximum(i // groups - 1, 0)

    def once(i, stage):
        return jnp.clip(i - stage * groups, 0, groups - 1)

    acts_specs = [
        pl.BlockSpec((3 * half, width), lambda i: (side(i), heads(i))),
        pl.BlockSpec((many, HEADS // 2, seq, seq), lambda i: (heads(i), side(i), 0, 0)),
        pl.BlockSpec((half, width), lambda i: (side(i), heads(i))),
        pl.BlockSpec((d, width), lambda i: (0, once(i, 2))),
        pl.BlockSpec((d, width), lambda i: (0, once(i, 1))),
    ]
    acts_shapes = [
        shape((3 * d, count), BF),
        shape((seqs, HEADS, seq, seq), BF),
        shape((d, count), BF),
        shape((d, count), F32),
        shape((d, count), BF),
    ]
    in_specs = [smem, pl.BlockSpec((many, seq, d), lambda i: (norms(i), 0, 0))]
    grid_shape = (slots, 2, rows) if direct else (d,)
    scratch = [
        pltpu.VMEM((3 * half, d), BF),
        pltpu.VMEM((d, d), BF),
        pltpu.VMEM((groups, d, width), BF),
        pltpu.VMEM((groups, d, width), F32),
        pltpu.VMEM((groups, d, width), BF),
        pltpu.VMEM((groups, half, width), BF),
        pltpu.VMEM((*grid_shape, wide), BF),
        pltpu.VMEM((*grid_shape, 3 * half), BF),
        pltpu.VMEM((*grid_shape, d), BF),
    ]
    if direct:
        n_sends = Gather.sends(n_dp, n_z)
        shards = (qkv_w, out_w, up_w, down_w, gains, biases, up_bias.reshape(1, -1))
        qkv, probs, ct, r1, a1, early, late, wo, wu, wd = pl.pallas_call(
            functools.partial(attention_kernel, (n_dp, n_z), True, groups),
            grid=(3 * groups,),
            in_specs=in_specs + [whole(s.shape) for s in shards],
            out_specs=acts_specs + [anywhere] * 5,
            out_shape=acts_shapes
            + [
                shape((slots, 2, rows, wide), BF),
                shape((slots, 2, rows, 3 * half), BF),
                shape((slots, 2, rows, d), BF),
                shape((slots, 2, rows, hidden), BF),
                shape((slots, 2, rows_down, d), BF),
            ],
            scratch_shapes=scratch
            + [
                pltpu.VMEM((rows, wide), BF),
                pltpu.VMEM((rows, 3 * half), BF),
                pltpu.VMEM((rows, d), BF),
                pltpu.VMEM((rows, hidden), BF),
                pltpu.VMEM((rows_down, d), BF),
                pltpu.VMEM((LANES, LANES), F32),
                pltpu.SemaphoreType.DMA((6, n_sends)),
                pltpu.SemaphoreType.DMA((6, slots, 2)),
                pltpu.SemaphoreType.DMA((5,)),
            ],
            compiler_params=pltpu.CompilerParams(
                vmem_limit_bytes=VMEM_LIMIT, collective_id=0, has_side_effects=True
            ),
            name="attention_forward",
        )(lengths, tokens, *shards)
        early, late = early.reshape(d, wide), late.reshape(d, 3 * half)
        wo = wo.reshape(d, d)
        wu, wd = wu.reshape(d, hidden), wd.reshape(hidden, d)
    else:
        sides = [
            jnp.concatenate([qkv_w[:, p * d + hb * half :][:, :half] for p in range(3)], 1)
            for hb in range(2)
        ]
        early = jnp.concatenate([sides[0], gains.T, biases.T], 1).astype(BF)
        early = lax.all_gather(early, axes, axis=0, tiled=True)
        late = lax.all_gather(sides[1].astype(BF), axes, axis=0, tiled=True)
        up_all = lax.all_gather(up_bias.astype(BF), axes, axis=0, tiled=True)
        up_all = up_all.reshape(cut, quarter, d // cut).swapaxes(1, 2).reshape(d, quarter)
        early = jnp.concatenate([early, up_all], 1)
        early = jnp.pad(early, ((0, 0), (0, wide - early.shape[1])))
        wo = lax.all_gather(out_w.astype(BF), axes, axis=0, tiled=True)
        wu = lax.all_gather(up_w.astype(BF), axes, axis=0, tiled=True)
        wd = lax.all_gather(down_w.astype(BF), axes, axis=0, tiled=True)
        qkv, probs, ct, r1, a1 = pl.pallas_call(
            functools.partial(attention_kernel, (n_dp, n_z), False, groups),
            grid=(3 * groups,),
            in_specs=in_specs + [whole(early.shape), whole(late.shape), whole(wo.shape)],
            out_specs=acts_specs,
            out_shape=acts_shapes,
            scratch_shapes=scratch,
            compiler_params=pltpu.CompilerParams(vmem_limit_bytes=VMEM_LIMIT),
            name="attention_forward",
        )(lengths, tokens, early, late, wo)

    pair = 2 if seqs % 2 == 0 else 1
    chunk = pair * seq
    chunks = seqs // pair
    block = d
    tail = 3 * half // LANES

    def following(i):
        return jnp.minimum(i + 1, chunks - 1)

    out, dr1, dwu, dwd, small = pl.pallas_call(
        functools.partial(forward_kernel, block=block),
        grid=(chunks,),
        in_specs=[
            whole((d, chunk)),
            whole((pair, seq, d)),
            pl.BlockSpec((d, chunk), lambda i: (0, following(i))),
            pl.BlockSpec((pair, seq, d), lambda i: (following(i), 0, 0)),
            pl.BlockSpec((d, LANES), lambda i: (0, tail), pipeline_mode=pl.Buffered(1)),
            whole((d, hidden)),
            whole((hidden, d)),
        ],
        out_specs=[
            pl.BlockSpec((pair, seq, d), lambda i: (i, 0, 0)),
            pl.BlockSpec((d, chunk), lambda i: (0, i)),
            whole((cut // 2, 2, d // cut, hidden)),
            whole((cut // 2, 2, hidden // cut, d)),
            whole((d, LANES)),
        ],
        out_shape=[
            shape(tokens.shape, BF),
            shape((d, count), F32),
            shape((cut // 2, 2, d // cut, hidden), BF),
            shape((cut // 2, 2, hidden // cut, d), BF),
            shape((d, LANES), F32),
        ],
        scratch_shapes=[pltpu.VMEM((hidden, d), BF), pltpu.VMEM((d, hidden), BF)]
        + [pltpu.VMEM((d, chunk), BF)] * 4
        + [pltpu.VMEM((d, chunk), F32), pltpu.VMEM((8, chunk), F32)]
        + [pltpu.VMEM((d, chunk), F32)] * 2
        + [pltpu.VMEM((d, hidden), F32), pltpu.VMEM((hidden, d), F32)]
        + [pltpu.VMEM((2, block, chunk), F32)] * 2
        + [pltpu.VMEM((hidden // block, block, chunk), BF)] * 2
        + [
            pltpu.VMEM((3, d, LANES), F32),
            pltpu.VMEM((hidden, LANES), F32),
            pltpu.VMEM((cut, hidden // cut, LANES), F32),
        ],
        compiler_params=pltpu.CompilerParams(vmem_limit_bytes=VMEM_LIMIT),
        name="feed_forward",
    )(r1, cotangent, r1, cotangent, early, wu, wd)

    def hold(i):
        return jnp.where(i < 2 * groups, turn(i), groups - 1)

    def back_side(i):
        return jnp.minimum(i // groups, 1)

    def closing(i):
        return jnp.where(i < 2 * groups, 0, turn(i))

    seq_block = pl.BlockSpec((many, seq, d), lambda i: (closing(i), 0, 0))
    acts_in = [
        pl.BlockSpec((d, width), lambda i: (0, turn(i))),
        pl.BlockSpec((d, width), lambda i: (0, hold(i))),
        pl.BlockSpec((3 * half, width), lambda i: (back_side(i), hold(i))),
        pl.BlockSpec((many, HEADS // 2, seq, seq), lambda i: (hold(i), back_side(i), 0, 0)),
        pl.BlockSpec((d, width), lambda i: (0, hold(i))),
        seq_block,
        whole((d, wide)),
        whole((d, 3 * half)),
        whole((d, d)),
        whole((d, LANES)),
    ]
    base = [
        pltpu.VMEM((2, groups, 3 * half, width), BF),
        pltpu.VMEM((2, d, 3 * half), F32),
        pltpu.VMEM((d, d), F32),
        pltpu.VMEM((half, width), BF),
        pltpu.VMEM((5, d, LANES), F32),
    ]
    acts = (dr1, ct, qkv, probs, a1, tokens, early, late, wo, small)
    if direct:
        n_sems = Scatter.sems(n_dp, n_z)
        plan = ((rows, hidden, False), (rows_down // 2, d, False), (rows_down // 2, d, True), (rows, 3 * half, False), (rows, 3 * half, False), (rows, d, False))
        outs = [(rows, 3 * d), (rows, d), (rows, hidden), (rows_down, d), (rows, LANES)]
        scratch = base + [
            pltpu.VMEM((2, slots, 2, rows, 3 * half), BF),
            pltpu.VMEM((slots, 2, rows, d), BF),
            pltpu.VMEM((slots, 2, rows, LANES), F32),
            pltpu.VMEM((n_dev - 1, rows, LANES), F32),
            pltpu.VMEM((2, rows, 3 * half), F32),
        ]
        for height, across, flip in plan:
            scratch += Scatter.scratch(n_dp, n_z, height, across, BF, flip)
        scratch += [pltpu.SemaphoreType.DMA((len(plan), n_sems))] * 2
        scratch += [pltpu.SemaphoreType.DMA((n_dev - 1,))] * 2
        grads = pl.pallas_call(
            functools.partial(backward_kernel, (n_dp, n_z), True, groups),
            grid=(3 * groups,),
            in_specs=acts_in + [anywhere, anywhere],
            out_specs=[seq_block] + [whole(o) for o in outs],
            out_shape=[shape(tokens.shape, BF)] + [shape(o, F32) for o in outs],
            scratch_shapes=scratch,
            compiler_params=pltpu.CompilerParams(
                vmem_limit_bytes=VMEM_LIMIT, collective_id=1, has_side_effects=True
            ),
            name="attention_backward",
        )(*acts, dwu, dwd)
        ends = [shape(tokens.shape, BF)] + [shape(o, F32) for o in outs[:4]]
        vectors = [shape(v, F32) for v in (gains.shape, biases.shape, (1, quarter * rows))]
        seq_block = pl.BlockSpec((many, seq, d), lambda i: (i, 0, 0))
        token_grad, gqkv, gout, gup, gdown, ggains, gbiases, gupb = pl.pallas_call(
            finish_kernel,
            grid=(groups,),
            in_specs=[seq_block] + [whole(o) for o in outs],
            out_specs=[seq_block] + [whole(o.shape) for o in ends[1:] + vectors],
            out_shape=ends + vectors,
            scratch_shapes=[pltpu.VMEM((LANES, LANES), F32)],
            compiler_params=pltpu.CompilerParams(vmem_limit_bytes=VMEM_LIMIT),
            name="hand_over",
        )(*grads)
        return out, token_grad, gqkv, gout, gup, gdown, ggains, gbiases, gupb.reshape(-1)

    token_grad, gqkv, gout, gsmall = pl.pallas_call(
        functools.partial(backward_kernel, (n_dp, n_z), False, groups),
        grid=(3 * groups,),
        in_specs=acts_in,
        out_specs=[seq_block, whole((d, 3 * d)), whole((d, d)), whole((d, LANES))],
        out_shape=[shape(tokens.shape, BF), shape((d, 3 * d), F32), shape((d, d), F32), shape((d, LANES), F32)],
        scratch_shapes=base,
        compiler_params=pltpu.CompilerParams(vmem_limit_bytes=VMEM_LIMIT),
        name="attention_backward",
    )(*acts)

    def scatter(term):
        return lax.psum_scatter(term.astype(F32), axes, scatter_dimension=0, tiled=True)

    up_sums = gsmall[:, 8 : 8 + quarter].reshape(cut, d // cut, quarter).swapaxes(1, 2)
    gsmall = scatter(gsmall[:, :8]).T
    return (
        out,
        token_grad,
        scatter(gqkv),
        scatter(gout),
        scatter(dwu.reshape(d, hidden)),
        scatter(dwd.reshape(hidden, d)),
        gsmall[:2],
        gsmall[2:8],
        scatter(up_sums.reshape(hidden)),
    )


def solution(mesh):
    axes = ("dp", "fsdp")
    rows, cols, flat = P(axes, None), P(None, axes), P(axes)
    data = P(axes, None, None)
    return jax.shard_map(
        functools.partial(per_device, mesh.shape["dp"], mesh.shape["fsdp"]),
        mesh=mesh,
        in_specs=(data, flat, data, rows, rows, rows, rows, cols, cols, flat),
        out_specs=(data, data, rows, rows, rows, rows, cols, cols, flat),
        check_vma=False,
    )
```

```python
import functools

import jax
import jax.numpy as jnp
from jax import lax
from jax.experimental import pallas as pl
from jax.experimental.pallas import tpu as pltpu
from jax.sharding import PartitionSpec as P

F32, BF = jnp.float32, jnp.bfloat16
MESH = pl.DeviceIdType.MESH
HEADS = 8
EPS = 1e-5
C0 = 0.7978845608028654
C1 = C0 * 0.044715
LANES = 128
NN = (((1,), (0,)), ((), ()))
NT = (((1,), (1,)), ((), ()))
TN = (((0,), (0,)), ((), ()))
VMEM_FORWARD, VMEM_MIDDLE, VMEM_BACKWARD = 32, 30.5, 37
R1 = BF


def dot(a, b, dims=NN):
    return lax.dot_general(a, b, dims, preferred_element_type=F32)


def lane_sums(v):
    total = v[:, :LANES]
    for at in range(LANES, v.shape[1], LANES):
        total = total + v[:, at : at + LANES]
    return total


def normalize(v):
    center = v - jnp.mean(v, 0, keepdims=True)
    inverse = lax.rsqrt(jnp.mean(center * center, 0, keepdims=True) + EPS)
    return center * inverse, inverse


def normalize_back(grad, normed, inverse, gain):
    scaled = grad * gain
    return inverse * (
        scaled
        - jnp.mean(scaled, 0, keepdims=True)
        - normed * jnp.mean(scaled * normed, 0, keepdims=True)
    )


class Place:
    def __init__(self, n_dp, n_z):
        self.n_dp, self.n_z = n_dp, n_z
        self.dp = lax.axis_index("dp")
        fsdp = lax.axis_index("fsdp")
        self.fsdp, self.z, self.core = fsdp, fsdp // 2, fsdp % 2
        self.slot = self.dp * n_z + self.z
        self.mate = (self.dp, self.z * 2 + 1 - self.core)

    def z_of(self, k):
        return lax.rem(self.z + k, self.n_z)

    def dp_of(self, k):
        return lax.rem(self.dp + k, self.n_dp)

    def corner(self, i):
        if i == 0:
            return self.dp
        low, high = lax.rem(self.dp, 2), self.dp // 2
        if i != 2:
            low = 1 - low
        if i != 1:
            high = 1 - high
        return high * 2 + low

    def z_peer(self, k):
        return (self.dp, self.z_of(k) * 2 + self.core)

    def dp_peer(self, k):
        return (self.dp_of(k), self.fsdp)

    def others(self):
        n_fsdp = 2 * self.n_z
        return [
            (self.dp_of(m), lax.rem(self.fsdp + k, n_fsdp))
            for m in range(self.n_dp)
            for k in range(n_fsdp)
            if m or k
        ]

    def greet(self, everyone=False):
        barrier = pltpu.get_barrier_semaphore()
        peers = [self.mate]
        peers += [self.z_peer(k) for k in range(1, self.n_z)]
        peers += [self.dp_peer(k) for k in range(1, self.n_dp)]
        if everyone:
            peers = self.others()
        for peer in peers:
            pl.semaphore_signal(barrier, inc=1, device_id=peer, device_id_type=MESH)
        pl.semaphore_wait(barrier, len(peers))


class Gather:
    def __init__(self, place, own, whole, send, recv):
        self.p, self.own, self.whole, self.send, self.recv = place, own, whole, send, recv

    def put(self, src, slot, peer, at):
        pltpu.make_async_remote_copy(
            src_ref=src,
            dst_ref=self.whole.at[slot, self.p.core],
            send_sem=self.send.at[at],
            recv_sem=self.recv.at[slot, self.p.core],
            device_id=peer,
            device_id_type=MESH,
        ).start()

    def pass_on(self, slot, peers, at):
        for i, peer in enumerate(peers):
            self.put(self.whole.at[slot, self.p.core], slot, peer, at + i)

    def landed(self, slot, core):
        there = self.whole.at[slot, core]
        pltpu.make_async_copy(there, there, self.recv.at[slot, core]).wait()

    def slot(self, corner, k):
        return self.p.corner(corner) * self.p.n_z + self.p.z_of(k)

    def side_peers(self):
        return [(self.p.corner(1), self.p.fsdp), (self.p.corner(2), self.p.fsdp), self.p.mate]

    def start(self):
        for k in range(1, self.p.n_z):
            self.put(self.own, self.p.slot, self.p.z_peer(k), k - 1)

    def spread(self):
        for i, peer in enumerate(self.side_peers()):
            self.put(self.own, self.p.slot, peer, self.p.n_z - 1 + i)

    def relay(self):
        for k in range(1, self.p.n_z):
            slot = self.slot(0, k)
            self.landed(slot, self.p.core)
            self.pass_on(slot, self.side_peers(), self.p.n_z - 1 + 3 * k)

    def cross(self):
        n_z = self.p.n_z
        first, second, mate = self.side_peers()
        at = 4 * n_z - 1
        for k in range(n_z):
            for corner, other in ((1, second), (2, first)):
                slot = self.slot(corner, k)
                self.landed(slot, self.p.core)
                early = k < n_z // 2
                peers = [mate, other] if early == (corner == 1) else [mate]
                self.pass_on(slot, peers, at)
                at += len(peers)

    def share(self):
        n_z = self.p.n_z
        for k in range(n_z):
            slot = self.slot(3, k)
            self.landed(slot, self.p.core)
            self.pass_on(slot, [self.p.mate], 7 * n_z - 1 + k)

    def finish(self):
        for k in range(self.p.n_z):
            for corner in range(4):
                self.landed(self.slot(corner, k), 1 - self.p.core)
        for at in range(self.sends(self.p.n_z)):
            pltpu.make_async_copy(self.own, self.own, self.send.at[at]).wait()

    @staticmethod
    def sends(n_z):
        return 8 * n_z - 1


def pipelined(items, ahead, behind, first, second, third):
    begun, done = {}, {}
    for at in range(-ahead, len(items) + behind):
        if 0 <= at + ahead < len(items):
            begun[at + ahead] = first(*items[at + ahead])
        if 0 <= at - behind < len(items):
            third(*items[at - behind], done.pop(at - behind))
        if 0 <= at < len(items):
            done[at] = second(*items[at], begun.pop(at))


def attention_kernel(mesh_sizes, gathers, sides, groups, lengths, x_ref, *refs):
    n_dp, n_z = mesh_sizes
    if gathers:
        (qkv_s, wo_s, wu_s, wd_s, gains_s, biases_s, upb_s,
         qkv_ref, probs_ref, inv_ref, ct_ref, r1_ref, n1_ref, inv1_ref,
         early_ref, late_ref, wo_ref, wu_ref, wd_ref,
         wqkv_t, wo_t, xt_s, normed_s, a1_s, early, late, wo, wu, wd,
         early_own, late_own, wo_own, wu_own, wd_own, small, sems, rems) = refs
    else:
        (early, late, wo,
         qkv_ref, probs_ref, inv_ref, ct_ref, r1_ref, n1_ref, inv1_ref,
         wqkv_t, wo_t, xt_s, normed_s, a1_s) = refs
    step = pl.program_id(0)
    stage, group = step // groups, lax.rem(step, groups)
    many, seq, d = x_ref.shape
    head = d // HEADS
    side_rows, side_heads = d // sides, HEADS // sides
    cols = 3 * side_rows
    scale = head**-0.5

    if gathers:
        place = Place(n_dp, n_z)
        pairs = [(early_own, early)] + [(late_own.at[i], late.at[i]) for i in range(sides - 1)]
        pairs += [(wo_own, wo), (wu_own, wu), (wd_own, wd)]
        first, *rest, out, up, down = [
            Gather(place, own, whole, sems.at[i], rems.at[i])
            for i, (own, whole) in enumerate(pairs)
        ]
        here = (place.slot, place.core)

        def enter():
            rows = qkv_s.shape[0]
            small[...] = jnp.zeros_like(small)
            small[0:2, :rows] = gains_s[...]
            small[2:8, :rows] = biases_s[...]
            for r in range(upb_s.shape[1] // rows):
                small[8 + r : 9 + r, :rows] = upb_s[:, r * rows : (r + 1) * rows]
            for side in range(sides):
                own = late_own.at[side - 1] if side else early_own
                for part in range(3):
                    at = part * d + side * side_rows
                    own[:, part * side_rows : (part + 1) * side_rows] = qkv_s[:, at : at + side_rows].astype(BF)
            early_own[:, cols:] = small[...].T[:rows].astype(BF)
            place.greet()
            first.start()
            first.spread()
            wo_own[...] = wo_s[...].astype(BF)
            wu_own[...] = wu_s[...].astype(BF)
            wd_own[...] = wd_s[...].astype(BF)
            early[here] = early_own[...]
            for i in range(sides - 1):
                late[(i, *here)] = late_own[i]
            wo[here] = wo_own[...]
            wu[here] = wu_own[...]
            wd[here] = wd_own[...]

        plan, after = plan_forward(enter, first, rest[0], out, up, down)
        for at, actions in plan.items():

            @pl.when(step == at)
            def _(actions=actions):
                for action in actions:
                    action()

    def columns():
        return early[..., cols:].reshape(d, LANES).astype(F32)

    @pl.when(stage == 0)
    def _():
        tail = lax.broadcasted_iota(jnp.int32, (16, many * seq), 0)
        n1_ref[group, d:] = jnp.where(tail == 0, 1.0, 0.0).astype(BF)
        for s in range(many):
            at = slice(seq * s, seq * (s + 1))
            xt = x_ref[s].T
            xt_s[group, :, at] = xt
            normed, inverse = normalize(xt.astype(F32))
            normed_s[group, :, at] = normed
            n1_ref[group, :d, at] = normed.astype(BF)
            inv1_ref[group, :, at] = jnp.broadcast_to(inverse, (8, seq))

    for side in range(sides):

        @pl.when(step == (side + 1) * groups)
        def _(side=side):
            if side:
                wqkv_t[...] = late[side - 1].reshape(d, cols).T
            else:
                wqkv_t[...] = early[..., :cols].reshape(d, cols).T
            if side == sides - 1:
                wo_t[...] = wo[...].reshape(d, d).T

    @pl.when(stage == 1)
    def _():
        column = columns()
        a1_s[group] = (normed_s[group] * column[:, 0:1] + column[:, 2:3]).astype(BF)

    def heads(side, last):
        mine = pl.ds(pl.multiple_of(side * side_rows, side_rows), side_rows)
        qkv = qkv_ref.at[0]
        small = early[..., cols:].reshape(d, LANES)
        if sides > 1:
            sides_small = early[pl.ds(side * (early.shape[0] // sides), early.shape[0] // sides), :, :, cols:] if len(early.shape) == 4 else early[mine, cols:]
            bias = sides_small.reshape(side_rows, LANES).astype(F32)
        else:
            bias = small.astype(F32)
        query = (dot(wqkv_t[:side_rows], a1_s[group]) + bias[:, 3:4]).astype(BF)
        qkv[:side_rows] = (query.astype(F32) * scale).astype(BF)
        qkv[side_rows : 2 * side_rows] = dot(wqkv_t[side_rows : 2 * side_rows], a1_s[group]).astype(BF)
        qkv[2 * side_rows :] = (dot(wqkv_t[2 * side_rows :], a1_s[group]) + bias[:, 4:5]).astype(BF)
        row = lax.broadcasted_iota(jnp.int32, (16, seq), 0)
        key = lax.broadcasted_iota(jnp.int32, (16, seq), 1)
        one = jnp.where(row == 0, 1.0, 0.0).astype(BF)
        masks = [
            jnp.where((row == 0) & (key >= lengths[group * many + s]), -1e30, 0.0).astype(BF)
            for s in range(many)
        ]
        items = [(s, h) for s in range(many) for h in range(side_heads)]

        def place_of(s, h, part):
            at = part * side_rows + h * head
            return slice(at, at + head), slice(seq * s, seq * (s + 1))

        def score(s, h):
            keys = jnp.concatenate([qkv[place_of(s, h, 1)], masks[s]], 0)
            queries = jnp.concatenate([qkv[place_of(s, h, 0)], one], 0)
            return dot(keys, queries, TN)

        def soften(s, h, scores):
            return jnp.exp(scores - jnp.max(scores, 0, keepdims=True)).astype(BF)

        def mix(s, h, exponent):
            probs_ref[0, s, h] = exponent
            values = jnp.concatenate([qkv[place_of(s, h, 2)], one], 0)
            mixed = dot(values, exponent)
            inverse = 1.0 / mixed[head : head + 1]
            inv_ref[side, group, pl.ds(s * side_heads + h, 1), :] = inverse
            to = pl.ds(pl.multiple_of(side * side_rows + h * head, head), head)
            ct_ref[group, to, seq * s : seq * (s + 1)] = (mixed[:head] * inverse).astype(BF)
            if last and h == side_heads - 1:
                at = slice(seq * s, seq * (s + 1))
                term = dot(wo_t[...], ct_ref[group, :, at]) + small[:, 5:6].astype(F32)
                r1_ref[group, :, at] = (xt_s[group, :, at].astype(F32) + term).astype(r1_ref.dtype)

        pipelined(items, 3, 2, score, soften, mix)

    pl.when((stage > 0) & (stage < sides))(lambda: heads(stage - 1, False))
    pl.when(stage == sides)(lambda: heads(sides - 1, True))


    if gathers:

        @pl.when(step == pl.num_programs(0) - 1)
        def _():
            for whole, to in ((early, early_ref), (late, late_ref), (wo, wo_ref)):
                to[...] = whole[...]
            for action in after:
                action()
            for whole, to in ((wu, wu_ref), (wd, wd_ref)):
                to[...] = whole[...]


def plan_forward(enter, first, late, out, up, down):
    plan = {
        0: [enter],
        2: [first.relay, late.start, out.start, up.start],
        3: [late.spread, out.spread],
        4: [first.cross, late.relay, first.share, out.relay, up.spread, down.start, first.finish],
        5: [late.cross, out.cross, up.relay, down.spread],
        6: [late.share, out.share],
        7: [down.relay, up.cross],
        8: [late.finish, out.finish],
        9: [down.cross, up.share],
        11: [down.share],
    }
    return plan, [up.finish, down.finish]


def forward_kernel(
    r1_ref, g_first, g_next, early_ref, wu_ref, wd_ref,
    out_ref, do_ref, dwu_ref, dwd_ref, small_ref,
    wu_t, wd_t, total_wu, total_wd, gt, gt_next, a2, a2_next, normed, inverse, total_out, total_a2,
    u_s, dh_s, h_s, du_s, sums, sums_up, up_bias, *, block,
):
    step = pl.program_id(0)
    groups, d, width = r1_ref.shape
    hidden = wu_t.shape[0]
    n_dev = dwd_ref.shape[0] * 2
    rows = d // n_dev
    seqs, seq = g_next.shape[:2]
    many = width // seq
    cols = early_ref.shape[-1] - LANES
    column = early_ref[..., cols:].reshape(d, LANES).astype(F32)
    blocks = hidden // block
    slots = h_s.shape[0]

    def at_of(chunk, s):
        which = chunk * seqs + s
        lane = pl.multiple_of(lax.rem(which, many) * seq, seq)
        return which // many, slice(None), pl.ds(lane, seq)

    def prepare(chunk, g_ref, gt_to, a2_to):
        for s in range(seqs):
            at = slice(seq * s, seq * (s + 1))
            gt_to[:, at] = g_ref[s].T
            r1 = r1_ref[at_of(chunk, s)].astype(F32)
            n, inv = normalize(r1)
            a2_to[:, at] = (n * column[:, 1:2] + column[:, 6:7]).astype(BF)
            normed[:, at] = n
            inverse[:, at] = jnp.broadcast_to(inv, (8, seq))
            total_out[:, at] = r1 + column[:, 7:8]

    @pl.when(step == 0)
    def _():
        wu_t[...] = wu_ref[...].reshape(d, hidden).T
        wd_t[...] = wd_ref[...].reshape(hidden, d).T
        sums[...] = jnp.zeros_like(sums)
        sums_up[...] = jnp.zeros_like(sums_up)
        for r in range(hidden // d):
            up_bias[:, r * rows : (r + 1) * rows, :] = jnp.broadcast_to(
                column[:, 8 + r : 9 + r].reshape(n_dev, rows, 1), (n_dev, rows, LANES)
            )
        prepare(0, g_first, gt, a2)

    per = block // (hidden // n_dev)

    def span(j):
        return slice(j * block, (j + 1) * block)

    def down_rows(j):
        if len(wd_ref.shape) == 2:
            return wd_ref[span(j)]
        unit = block // (2 * wd_ref.shape[2])
        return wd_ref[j * unit : (j + 1) * unit].reshape(block, d)

    def enter(j):
        bias = up_bias[j * per : (j + 1) * per].reshape(block, LANES)[:, 0:1]
        u_s[j % 2] = dot(wu_t[span(j)], a2[...]) + bias
        dh_s[j % 2] = dot(down_rows(j), gt[...])

    def bend(j):
        u = u_s[j % 2]
        square = u * u
        part = 0.5 + 0.5 * jnp.tanh(u * (C0 + C1 * square))
        h = u * part
        h_s[j % slots] = h.astype(BF)
        slope = part + h * (1.0 - part) * (2 * C0 + 6 * C1 * square)
        du = (dh_s[j % 2] * slope).astype(BF)
        du_s[j % slots] = du
        sums_up[span(j)] += lane_sums(du.astype(F32))

    def leave(j):
        total_out[...] += dot(wd_t[:, span(j)], h_s[j % slots])
        term = dot(wu_ref[..., span(j)].reshape(d, block), du_s[j % slots])
        total_a2[...] = term if j == 0 else total_a2[...] + term

    def weights(j):
        unit = block // (2 * dwd_ref.shape[2])
        at = slice(j * unit, (j + 1) * unit)
        term = dot(h_s[j % slots], gt[...], NT)
        term = jnp.where(step == 0, term, total_wd[span(j)] + term)
        total_wd[span(j)] = term
        dwd_ref[at] = term.astype(BF).reshape(unit, *dwd_ref.shape[1:])
        term = dot(a2[...], du_s[j % slots], NT)
        term = jnp.where(step == 0, term, total_wu[:, span(j)] + term)
        total_wu[:, span(j)] = term
        dwu_ref[..., span(j)] = term.astype(BF).reshape(*dwu_ref.shape[:3], block)

    def close():
        da2, n, g = total_a2[...], normed[...], gt[...].astype(F32)
        dr1 = (g + normalize_back(da2, n, inverse[0:1], column[:, 1:2])).astype(BF)
        for s in range(seqs):
            at = slice(seq * s, seq * (s + 1))
            out_ref[s] = total_out[:, at].astype(BF).T
            do_ref[at_of(step, s)] = dr1[:, at]
        sums[0] += lane_sums(da2 * n)
        sums[1] += lane_sums(da2)
        sums[2] += lane_sums(g)

    enter(0)
    for j in range(blocks):
        if j + 1 < blocks:
            enter(j + 1)
        if j:
            leave(j - 1)
        bend(j)
        if 0 < j < blocks - 1:
            weights(j - 1)
    leave(blocks - 1)
    weights(blocks - 2)
    close()
    weights(blocks - 1)
    prepare(jnp.minimum(step + 1, pl.num_programs(0) - 1), g_next, gt_next, a2_next)
    gt[...] = gt_next[...]
    a2[...] = a2_next[...]

    @pl.when(step == pl.num_programs(0) - 1)
    def _():
        lane = lax.broadcasted_iota(jnp.int32, (d, LANES), 1)
        small = jnp.zeros((d, LANES), F32)
        for s, at in ((0, 1), (1, 6), (2, 7)):
            small = jnp.where(lane == at, jnp.sum(sums[s], 1, keepdims=True), small)
        up = jnp.sum(sums_up[...], 1, keepdims=True).reshape(n_dev, hidden // n_dev, 1)
        for r in range(hidden // d):
            part = up[:, r * rows : (r + 1) * rows].reshape(d, 1)
            small = jnp.where(lane == 8 + r, part, small)
        small_ref[...] = small


class Scatter:
    def __init__(self, place, part, result, bufs, send, recv, flip=False):
        self.p, self.part, self.result = place, part, result
        self.sum1, self.got1, self.got2, self.sum2, self.got3 = bufs
        self.send, self.recv = send, recv
        p = place
        by_z = (p.n_z, p.z_peer, lambda far, near: p.dp_of(near) * p.n_z + p.z_of(far))
        by_dp = (p.n_dp, p.dp_peer, lambda far, near: p.dp_of(far) * p.n_z + p.z_of(near))
        (self.far, self.far_peer, self.slot), (self.near, self.near_peer, _) = (
            (by_z, by_dp) if flip else (by_dp, by_z)
        )

    @staticmethod
    def scratch(n_dp, n_z, rows, width, kind, flip=False):
        far, near = (n_z, n_dp) if flip else (n_dp, n_z)
        return [
            pltpu.VMEM((n_dp * n_z, rows, width), kind),
            pltpu.VMEM((n_dp * n_z, rows, width), kind),
            pltpu.VMEM((far - 1, near, rows, width), kind),
            pltpu.VMEM((near, rows, width), kind),
            pltpu.VMEM((near - 1, rows, width), kind),
        ]

    @staticmethod
    def sems(n_dp, n_z):
        return 1 + (max(n_dp, n_z) - 1) * max(n_dp, n_z) + max(n_dp, n_z) - 1

    def copy(self, src, dst, at, peer):
        return pltpu.make_async_remote_copy(
            src_ref=src,
            dst_ref=dst,
            send_sem=self.send.at[at],
            recv_sem=self.recv.at[at],
            device_id=peer,
            device_id_type=MESH,
        )

    def to_mate(self):
        return self.copy(self.sum1, self.got1, 0, self.p.mate)

    def afar(self):
        return [
            self.copy(
                self.sum1.at[self.slot(k, m)],
                self.got2.at[k - 1, m],
                1 + (k - 1) * self.near + m,
                self.far_peer(k),
            )
            for k in range(1, self.far)
            for m in range(self.near)
        ]

    def nearby(self):
        return [
            self.copy(
                self.sum2.at[m],
                self.got3.at[m - 1],
                1 + (self.far - 1) * self.near + m - 1,
                self.near_peer(m),
            )
            for m in range(1, self.near)
        ]

    def step1(self):
        def cast(s, _):
            self.sum1[s] = self.part[s, 1 - self.p.core].astype(self.sum1.dtype)
            return 0

        lax.fori_loop(0, self.p.n_dp * self.p.n_z, cast, 0)
        self.to_mate().start()

    def step2(self):
        self.to_mate().wait()

        def add(s, _):
            total = self.part[s, self.p.core].astype(F32) + self.got1[s].astype(F32)
            self.sum1[s] = total.astype(self.sum1.dtype)
            return 0

        lax.fori_loop(0, self.p.n_dp * self.p.n_z, add, 0)
        for copy in self.afar():
            copy.start()

    def step3(self):
        for copy in self.afar():
            copy.wait()
        for m in range(self.near):
            total = self.sum1[self.slot(0, m)].astype(F32)
            for k in range(self.far - 1):
                total = total + self.got2[k, m].astype(F32)
            self.sum2[m] = total.astype(self.sum2.dtype)
        for copy in self.nearby():
            copy.start()

    def step4(self):
        for copy in self.nearby():
            copy.wait()
        total = self.sum2[0].astype(F32)
        for m in range(self.near - 1):
            total = total + self.got3[m].astype(F32)
        self.result[...] = total


def backward_kernel(mesh_sizes, scatters, sides, groups, *refs):
    n_dp, n_z = mesh_sizes
    (do_ref, ct_ref, qkv_ref, probs_ref, inv_ref, n1_ref, inv1_ref,
     early_ref, late_ref, wo_ref, part_ref) = refs[:11]
    refs = refs[11:]
    if scatters:
        (dwu_ref, dwd_ref, tg_ref, gqkv_ref, gout_ref, gup_ref, gdown_ref, gsmall_ref,
         dp_s, total_qkv, total_out, sum_dp, dc_s, sums, part_small, gqkv_side) = refs[:16]
        buffers, (send, recv) = refs[16:-2], refs[-2:]
    else:
        (tg_ref, gqkv_ref, gout_ref, gsmall_ref, dp_s, total_qkv, total_out, sum_dp, dc_s, sums) = refs
    step = pl.program_id(0)
    last = pl.num_programs(0) - 1
    stage, group = step // groups, lax.rem(step, groups)
    d, width = do_ref.shape[1:]
    many, seq = tg_ref.shape[:2]
    head = d // HEADS
    side_rows, side_heads = d // sides, HEADS // sides
    cols = 3 * side_rows
    scale = head**-0.5
    opening = group == 0

    def columns():
        return early_ref[..., cols:].reshape(d, LANES).astype(F32)

    def side_weights(side):
        w = late_ref[side - 1] if side else early_ref[..., :cols]
        return w.reshape(d, cols)

    @pl.when(step == 0)
    def _():
        sums[...] = jnp.zeros_like(sums)

    def pack(side):
        n_slots, _, rows, _ = total_qkv.shape[1:]
        column, w = columns(), side_weights(side)
        row = sum_dp[side, 0:1]
        for slot in range(n_slots):
            at = slice(slot * 2 * rows, (slot + 1) * 2 * rows)
            product = total_qkv[side, slot].reshape(2 * rows, cols)
            piece = w[at].astype(F32)
            sums[0, at] += lane_sums(piece * product)
            sums[1, at] += lane_sums(piece * row)
            whole = column[at, 0:1] * product + column[at, 2:3] * row
            total_qkv[side, slot] = whole.reshape(2, rows, cols)

    def vectors():
        lane = lax.broadcasted_iota(jnp.int32, (d, LANES), 1)
        small = part_ref[...]
        for s, at in enumerate((0, 2, 3, 4, 5)):
            small = jnp.where(lane == at, jnp.sum(sums[s], 1, keepdims=True), small)
        return small

    if scatters:
        place = Place(n_dp, n_z)
        cut = dwd_ref.shape[2] // 2
        parts = [
            (dwu_ref, gup_ref, False),
            (dwd_ref.at[:, :, :cut], gdown_ref.at[:cut], False),
            (dwd_ref.at[:, :, cut:], gdown_ref.at[cut:], True),
            (total_out, gout_ref, False),
            (part_small, gsmall_ref, False),
        ]
        parts += [(total_qkv.at[i], gqkv_side.at[i], False) for i in range(sides)]
        up, down, down2, out, small, *qkvs = [
            Scatter(place, part, result, buffers[5 * i : 5 * i + 5], send.at[i], recv.at[i], flip)
            for i, (part, result, flip) in enumerate(parts)
        ]

        def pack_small():
            part_small[...] = vectors().reshape(part_small.shape)

        packs = [functools.partial(pack, i) for i in range(sides)]
        plan, after = plan_backward(place.greet, up, down, down2, out, small, qkvs, packs, pack_small)
        for at, actions in plan.items():

            @pl.when(step == at)
            def _(actions=actions):
                for action in actions:
                    action()

    @pl.when(stage == 0)
    def _():
        n_slots = total_out.shape[0]
        for part in range(2):
            at = slice(part * n_slots // 2, (part + 1) * n_slots // 2)
            term = dot(ct_ref[group, part * d // 2 : (part + 1) * d // 2], do_ref[group], NT)
            term = term.reshape(n_slots // 2, *total_out.shape[1:])
            total_out[at] = jnp.where(opening, term, total_out[at] + term)
        sums[4] += lane_sums(do_ref[group].astype(F32))

    def heads(side):
        mine = pl.ds(pl.multiple_of(side * side_rows, side_rows), side_rows)
        qkv, to = qkv_ref.at[0], dp_s.at[side, group]
        if len(wo_ref.shape) == 4:
            part = wo_ref.shape[0] // sides
            wo = wo_ref[pl.ds(side * part, part)].reshape(side_rows, d)
        else:
            wo = wo_ref[mine, :]
        dc_s[...] = dot(wo, do_ref[group])
        items = [(s, h) for s in range(many) for h in range(side_heads)]

        def place_of(s, h, part):
            at = part * side_rows + h * head
            return slice(at, at + head), slice(seq * s, seq * (s + 1))

        def grad_probs(s, h):
            inverse = inv_ref[side, group, pl.ds(s * side_heads + h, 1), :]
            dc = (dc_s[place_of(s, h, 0)] * inverse).astype(BF)
            return dc, dot(qkv[place_of(s, h, 2)], dc, TN)

        def grad_scores(s, h, begun):
            dc, term = begun
            there = pl.ds(pl.multiple_of(side * side_rows + h * head, head), head)
            delta = dc.astype(F32) * ct_ref[group, there, seq * s : seq * (s + 1)].astype(F32)
            delta = jnp.sum(delta, 0, keepdims=True)
            return dc, (probs_ref[0, s, h].astype(F32) * (term - delta)).astype(BF)

        def finish(s, h, done):
            dc, ds = done
            q, k, v = (place_of(s, h, part) for part in range(3))
            to[v] = dot(dc, probs_ref[0, s, h], NT).astype(BF)
            to[k] = dot(qkv[q], ds, NT).astype(BF)
            to[q] = (dot(qkv[k], ds) * scale).astype(BF)

        pipelined(items, 2, 1, grad_probs, grad_scores, finish)
        n_slots = total_qkv.shape[1]
        for part in range(2):
            at = slice(part * n_slots // 2, (part + 1) * n_slots // 2)
            term = dot(n1_ref[group, part * d // 2 : (d // 2, d + 16)[part]], to[...], NT)
            product = term[: d // 2].reshape(n_slots // 2, *total_qkv.shape[2:])
            total_qkv[side, at] = jnp.where(opening, product, total_qkv[side, at] + product)
        row = term[d // 2 : d // 2 + 8]
        sum_dp[side] = jnp.where(opening, row, sum_dp[side] + row)
        sums[2, mine, :] += lane_sums(to[:side_rows].astype(F32))
        sums[3, mine, :] += lane_sums(to[2 * side_rows :].astype(F32))

    pl.when(stage < sides)(lambda: heads(stage))

    @pl.when(stage == sides)
    def _():
        gain = columns()[:, 0:1]

        def product(s):
            at = slice(seq * s, seq * (s + 1))
            total = dot(side_weights(0), dp_s[0, group, :, at])
            for side in range(1, sides):
                total = total + dot(side_weights(side), dp_s[side, group, :, at])
            return total

        def finish(s, _, da1):
            at = slice(seq * s, seq * (s + 1))
            normed = n1_ref[group, :d, at].astype(F32)
            dv = normalize_back(da1, normed, inv1_ref[group, 0:1, at], gain)
            tg_ref[s] = (do_ref[group, :, at].astype(F32) + dv).astype(BF).T

        ahead = product(0)
        for s in range(many):
            da1, ahead = ahead, product(s + 1) if s + 1 < many else None
            finish(s, None, da1)

    @pl.when(step == last)
    def _():
        if scatters:
            for action in after:
                action()
            shards = gqkv_side
        else:
            for side in range(sides):
                pack(side)
            gout_ref[...] = total_out[...].reshape(d, d)
            gsmall_ref[...] = vectors()
            shards = total_qkv
        for side in range(sides):
            whole = shards[side].reshape(gqkv_ref.shape[0], cols)
            for part in range(3):
                at = part * d + side * side_rows
                gqkv_ref[:, at : at + side_rows] = whole[:, part * side_rows : (part + 1) * side_rows]


def plan_backward(greet, up, down, down2, out, small, qkvs, packs, pack_small):
    qkv0, qkv1 = qkvs
    plan = {
        0: [greet, up.step1, down2.step1, down.step1],
        1: [up.step2, down2.step2, down.step2],
        4: [packs[0], qkv0.step1, out.step1],
        5: [up.step3, down2.step3, qkv0.step2, out.step2],
        7: [down.step3],
        8: [packs[1], qkv1.step1, pack_small, small.step1, up.step4, down2.step4],
        9: [qkv1.step2, small.step2, qkv0.step3, out.step3],
        10: [down.step4],
        11: [qkv0.step4, out.step4],
    }
    return plan, [qkv1.step3, small.step3, qkv1.step4, small.step4]


def finish_kernel(tg, qkv, out, up, down, small, tg_to, qkv_to, out_to, up_to, down_to, gains, biases, upb, turn):
    tg_to[...] = tg[...]

    @pl.when(pl.program_id(0) == 0)
    def _():
        for source, to in ((qkv, qkv_to), (out, out_to), (up, up_to), (down, down_to)):
            to[...] = source[...]
        rows = small.shape[0]
        turn[...] = jnp.zeros_like(turn)
        turn[:rows] = small[...]
        turned = turn[...].T
        gains[...] = turned[0:2, :rows]
        biases[...] = turned[2:8, :rows]
        for r in range(upb.shape[1] // rows):
            upb[:, r * rows : (r + 1) * rows] = turned[8 + r : 9 + r, :rows]


def in_hbm(*arrays):
    return tuple(pltpu.with_memory_space_constraint(array, pltpu.HBM) for array in arrays)


def per_device(n_dp, n_fsdp, tokens, lengths, cotangent, qkv_w, out_w, up_w, down_w, gains, biases, up_bias):
    tokens, lengths, cotangent = in_hbm(tokens, lengths, cotangent)
    seqs, seq, d = tokens.shape
    n_z, n_dev = n_fsdp // 2, n_dp * n_fsdp
    rows, rows_down = qkv_w.shape[0], down_w.shape[0]
    hidden = up_w.shape[1]
    slots = n_dp * n_z
    axes = ("dp", "fsdp")
    direct = rows % 16 == 0 and n_dp == 4
    cut = n_dev if direct else 32
    quarter = hidden // d
    many = next(m for m in (3, 2, 1) if seqs % m == 0)
    groups, width = seqs // many, many * seq
    sides = 2
    side_rows, side_heads = d // sides, HEADS // sides
    cols = 3 * side_rows
    wide = cols + LANES

    def whole(shape):
        return pl.BlockSpec(shape, lambda i: (0,) * len(shape), pipeline_mode=pl.Buffered(1))

    def shape(dims, kind):
        return jax.ShapeDtypeStruct(dims, kind)

    anywhere = pl.BlockSpec(memory_space=pl.ANY)
    smem = pl.BlockSpec(memory_space=pltpu.SMEM)
    vmem = pl.BlockSpec(memory_space=pltpu.VMEM)
    probs_block = (1, many, side_heads, seq, seq)

    def params(mib, **more):
        return pltpu.CompilerParams(vmem_limit_bytes=int(mib * 2**20), **more)

    held = [
        pltpu.HBM((sides * groups, cols, width), BF),
        pltpu.HBM((sides * groups, *probs_block[1:]), BF),
        pltpu.VMEM((sides, groups, many * side_heads, seq), F32),
        pltpu.VMEM((groups, d, width), BF),
        pltpu.VMEM((groups, d, width), R1),
        pltpu.VMEM((groups, d + 16, width), BF),
        pltpu.VMEM((groups, 8, width), F32),
    ]
    held_specs = [vmem] * len(held)
    held_specs[0] = pl.BlockSpec((1, cols, width), lambda i: (jnp.maximum(i - groups, 0), 0, 0))
    held_specs[1] = pl.BlockSpec(
        probs_block, lambda i: (jnp.maximum(i - groups, 0), 0, 0, 0, 0)
    )
    in_specs = [
        smem,
        pl.BlockSpec((many, seq, d), lambda i: (jnp.minimum(i, groups - 1), 0, 0)),
    ]
    scratch = [
        pltpu.VMEM((cols, d), BF),
        pltpu.VMEM((d, d), BF),
        pltpu.VMEM((groups, d, width), BF),
        pltpu.VMEM((groups, d, width), F32),
        pltpu.VMEM((groups, d, width), BF),
    ]
    steps = (1 + sides) * groups
    if direct:
        n_sends = Gather.sends(n_z)
        shards = in_hbm(qkv_w, out_w, up_w, down_w, gains, biases, up_bias.reshape(1, -1))
        qkv, probs, inv, ct, r1, n1, inv1, early, late, wo, wu, wd = pl.pallas_call(
            functools.partial(attention_kernel, (n_dp, n_z), True, sides, groups),
            grid=(steps,),
            in_specs=in_specs + [whole(s.shape) for s in shards],
            out_specs=held_specs + [vmem] * 5,
            out_shape=held
            + [
                pltpu.VMEM((slots, 2, rows, wide), BF),
                pltpu.VMEM((sides - 1, slots, 2, rows, cols), BF),
                pltpu.VMEM((slots, 2, rows, d), BF),
                pltpu.VMEM((slots, 2, rows, hidden), BF),
                pltpu.VMEM((slots, 2, rows_down, d), BF),
            ],
            scratch_shapes=scratch
            + [
                pltpu.VMEM((slots, 2, rows, wide), BF),
                pltpu.VMEM((sides - 1, slots, 2, rows, cols), BF),
                pltpu.VMEM((slots, 2, rows, d), BF),
                pltpu.VMEM((slots, 2, rows, hidden), BF),
                pltpu.VMEM((slots, 2, rows_down, d), BF),
                pltpu.VMEM((rows, wide), BF),
                pltpu.VMEM((sides - 1, rows, cols), BF),
                pltpu.VMEM((rows, d), BF),
                pltpu.VMEM((rows, hidden), BF),
                pltpu.VMEM((rows_down, d), BF),
                pltpu.VMEM((LANES, LANES), F32),
                pltpu.SemaphoreType.DMA((sides + 3, n_sends)),
                pltpu.SemaphoreType.DMA((sides + 3, slots, 2)),
            ],
            compiler_params=params(VMEM_FORWARD, collective_id=0, has_side_effects=True),
            name="attention_forward",
        )(lengths, tokens, *shards)
    else:
        split = [
            jnp.concatenate([qkv_w[:, p * d + i * side_rows :][:, :side_rows] for p in range(3)], 1)
            for i in range(sides)
        ]
        early = jnp.concatenate([split[0], gains.T, biases.T], 1).astype(BF)
        early = lax.all_gather(early, axes, axis=0, tiled=True)
        up_all = lax.all_gather(up_bias.astype(BF), axes, axis=0, tiled=True)
        up_all = up_all.reshape(cut, quarter, d // cut).swapaxes(1, 2).reshape(d, quarter)
        early = jnp.concatenate([early, up_all], 1)
        early = jnp.pad(early, ((0, 0), (0, wide - early.shape[1])))
        late = lax.all_gather(jnp.stack(split[1:]).astype(BF), axes, axis=1, tiled=True)
        wo = lax.all_gather(out_w.astype(BF), axes, axis=0, tiled=True)
        wu = lax.all_gather(up_w.astype(BF), axes, axis=0, tiled=True)
        wd = lax.all_gather(down_w.astype(BF), axes, axis=0, tiled=True)
        qkv, probs, inv, ct, r1, n1, inv1 = pl.pallas_call(
            functools.partial(attention_kernel, (n_dp, n_z), False, sides, groups),
            grid=(steps,),
            in_specs=in_specs + [whole(early.shape), whole(late.shape), whole(wo.shape)],
            out_specs=held_specs,
            out_shape=held,
            scratch_shapes=scratch,
            compiler_params=params(VMEM_FORWARD),
            name="attention_forward",
        )(lengths, tokens, early, late, wo)

    def weight(array):
        return vmem if direct else whole(array.shape)

    pair = 2 if seqs % 2 == 0 else 1
    chunk = pair * seq
    chunks = seqs // pair
    block = d // 2
    lag = 4
    parts = [
        pltpu.VMEM((cut // 2, 2, d // cut, hidden), BF),
        pltpu.VMEM((cut // 2, 2, hidden // cut, d), BF),
    ]
    part_specs = [vmem] * 2
    if not direct:
        parts = [shape(part.shape, BF) for part in parts]
        part_specs = [whole(part.shape) for part in parts]
    out, do, dwu, dwd, small = pl.pallas_call(
        functools.partial(forward_kernel, block=block),
        grid=(chunks,),
        in_specs=[
            vmem,
            whole((pair, seq, d)),
            pl.BlockSpec((pair, seq, d), lambda i: (jnp.minimum(i + 1, chunks - 1), 0, 0)),
            weight(early),
            weight(wu),
            weight(wd),
        ],
        out_specs=[pl.BlockSpec((pair, seq, d), lambda i: (i, 0, 0)), vmem]
        + part_specs
        + [whole((d, LANES))],
        out_shape=[pltpu.HBM(tokens.shape, BF), pltpu.VMEM((groups, d, width), BF)]
        + parts
        + [shape((d, LANES), F32)],
        scratch_shapes=[pltpu.VMEM((hidden, d), BF), pltpu.VMEM((d, hidden), BF)]
        + [pltpu.VMEM((d, hidden), F32), pltpu.VMEM((hidden, d), F32)]
        + [pltpu.VMEM((d, chunk), BF)] * 4
        + [pltpu.VMEM((d, chunk), F32), pltpu.VMEM((8, chunk), F32)]
        + [pltpu.VMEM((d, chunk), F32)] * 2
        + [pltpu.VMEM((2, block, chunk), F32)] * 2
        + [pltpu.VMEM((lag, block, chunk), BF)] * 2
        + [
            pltpu.VMEM((3, d, LANES), F32),
            pltpu.VMEM((hidden, LANES), F32),
            pltpu.VMEM((cut, hidden // cut, LANES), F32),
        ],
        compiler_params=params(VMEM_MIDDLE if direct else VMEM_MIDDLE + 16),
        name="feed_forward",
    )(r1, cotangent, cotangent, early, wu, wd)

    seq_block = pl.BlockSpec((many, seq, d), lambda i: (jnp.maximum(i - sides * groups, 0), 0, 0))
    acts = (do, ct, qkv, probs, inv, n1, inv1, early, late, wo, small)
    acts_in = [vmem] * 7 + [weight(early), weight(late), weight(wo), whole((d, LANES))]
    acts_in[2] = pl.BlockSpec(
        (1, cols, width), lambda i: (jnp.minimum(i, sides * groups - 1), 0, 0)
    )
    acts_in[3] = pl.BlockSpec(
        probs_block, lambda i: (jnp.minimum(i, sides * groups - 1), 0, 0, 0, 0)
    )
    base = [
        pltpu.VMEM((sides, groups, cols, width), BF),
        pltpu.VMEM((sides, cut // 2, 2, d // cut, cols), F32),
        pltpu.VMEM((cut // 2, 2, d // cut, d), F32),
        pltpu.VMEM((sides, 8, cols), F32),
        pltpu.VMEM((side_rows, width), F32),
        pltpu.VMEM((5, d, LANES), F32),
    ]
    if direct:
        n_sems = Scatter.sems(n_dp, n_z)
        plan = [(rows, hidden, False), (rows_down // 2, d, False), (rows_down // 2, d, True), (rows, d, False), (rows, LANES, False)]
        plan += [(rows, cols, False)] * sides
        outs = [(rows, 3 * d), (rows, d), (rows, hidden), (rows_down, d), (rows, LANES)]
        scratch = base + [
            pltpu.VMEM((slots, 2, rows, LANES), F32),
            pltpu.VMEM((sides, rows, cols), F32),
        ]
        for height, across, flip in plan:
            scratch += Scatter.scratch(n_dp, n_z, height, across, BF, flip)
        scratch += [pltpu.SemaphoreType.DMA((len(plan), n_sems))] * 2
        grads = pl.pallas_call(
            functools.partial(backward_kernel, (n_dp, n_z), True, sides, groups),
            grid=(steps,),
            in_specs=acts_in + [vmem, vmem],
            out_specs=[seq_block] + [whole(o) for o in outs],
            out_shape=[pltpu.HBM(o, BF if i == 0 else F32) for i, o in enumerate([tokens.shape] + outs)],
            scratch_shapes=scratch,
            compiler_params=params(VMEM_BACKWARD, collective_id=1, has_side_effects=True),
            name="attention_backward",
        )(*acts, dwu, dwd)
        ends = [shape(tokens.shape, BF)] + [shape(o, F32) for o in outs[:4]]
        vectors = [shape(v, F32) for v in (gains.shape, biases.shape, (1, quarter * rows))]
        seq_block = pl.BlockSpec((many, seq, d), lambda i: (i, 0, 0))
        token_grad, gqkv, gout, gup, gdown, ggains, gbiases, gupb = pl.pallas_call(
            finish_kernel,
            grid=(groups,),
            in_specs=[seq_block] + [whole(o) for o in outs],
            out_specs=[seq_block] + [whole(o.shape) for o in ends[1:] + vectors],
            out_shape=ends + vectors,
            scratch_shapes=[pltpu.VMEM((LANES, LANES), F32)],
            compiler_params=params(60),
            name="hand_over",
        )(*grads)
        return out, token_grad, gqkv, gout, gup, gdown, ggains, gbiases, gupb.reshape(-1)

    token_grad, gqkv, gout, gsmall = pl.pallas_call(
        functools.partial(backward_kernel, (n_dp, n_z), False, sides, groups),
        grid=(steps,),
        in_specs=acts_in,
        out_specs=[seq_block, whole((d, 3 * d)), whole((d, d)), whole((d, LANES))],
        out_shape=[shape(tokens.shape, BF), shape((d, 3 * d), F32), shape((d, d), F32), shape((d, LANES), F32)],
        scratch_shapes=base,
        compiler_params=params(VMEM_BACKWARD),
        name="attention_backward",
    )(*acts)

    def scatter(term):
        return lax.psum_scatter(term.astype(F32), axes, scatter_dimension=0, tiled=True)

    up_sums = gsmall[:, 8 : 8 + quarter].reshape(cut, d // cut, quarter).swapaxes(1, 2)
    gsmall = scatter(gsmall[:, :8]).T
    return (
        out,
        token_grad,
        scatter(gqkv),
        scatter(gout),
        scatter(dwu.reshape(d, hidden)),
        scatter(dwd.reshape(hidden, d)),
        gsmall[:2],
        gsmall[2:8],
        scatter(up_sums.reshape(hidden)),
    )


def solution(mesh):
    axes = ("dp", "fsdp")
    rows, cols, flat = P(axes, None), P(None, axes), P(axes)
    data = P(axes, None, None)
    return jax.shard_map(
        functools.partial(per_device, mesh.shape["dp"], mesh.shape["fsdp"]),
        mesh=mesh,
        in_specs=(data, flat, data, rows, rows, rows, rows, cols, cols, flat),
        out_specs=(data, data, rows, rows, rows, rows, cols, cols, flat),
        check_vma=False,
    )
```

```python
import functools

import jax
import jax.numpy as jnp
from jax import lax
from jax.experimental import pallas as pl
from jax.experimental.pallas import tpu as pltpu
from jax.sharding import PartitionSpec as P

F32, BF = jnp.float32, jnp.bfloat16
MESH = pl.DeviceIdType.MESH
HEADS = 8
EPS = 1e-5
C0 = 0.7978845608028654
C1 = C0 * 0.044715
LANES = 128
NN = (((1,), (0,)), ((), ()))
NT = (((1,), (1,)), ((), ()))
TN = (((0,), (0,)), ((), ()))
VMEM_FORWARD, VMEM_MIDDLE, VMEM_BACKWARD = 40, 36, 36


def dot(a, b, dims=NN):
    return lax.dot_general(a, b, dims, preferred_element_type=F32)


def lane_sums(v):
    total = v[:, :LANES]
    for at in range(LANES, v.shape[1], LANES):
        total = total + v[:, at : at + LANES]
    return total


def center_of(v):
    mean = jnp.mean(v, 0, keepdims=True)
    center = v - mean
    inverse = lax.rsqrt(jnp.mean(center * center, 0, keepdims=True) + EPS)
    return center, inverse, mean


def normalize(v):
    center, inverse, _ = center_of(v)
    return center * inverse, inverse


def normalize_back(grad, normed, inverse, gain):
    scaled = grad * gain
    return inverse * (
        scaled
        - jnp.mean(scaled, 0, keepdims=True)
        - normed * jnp.mean(scaled * normed, 0, keepdims=True)
    )


class Place:
    def __init__(self, n_dp, n_z):
        self.n_dp, self.n_z = n_dp, n_z
        self.dp = lax.axis_index("dp")
        fsdp = lax.axis_index("fsdp")
        self.fsdp, self.z, self.core = fsdp, fsdp // 2, fsdp % 2
        self.slot = self.dp * n_z + self.z
        self.mate = (self.dp, self.z * 2 + 1 - self.core)

    def z_of(self, k):
        return lax.rem(self.z + k, self.n_z)

    def dp_of(self, k):
        return lax.rem(self.dp + k, self.n_dp)

    def corner(self, i):
        if i == 0:
            return self.dp
        low, high = lax.rem(self.dp, 2), self.dp // 2
        if i != 2:
            low = 1 - low
        if i != 1:
            high = 1 - high
        return high * 2 + low

    def z_peer(self, k):
        return (self.dp, self.z_of(k) * 2 + self.core)

    def dp_peer(self, k):
        return (self.dp_of(k), self.fsdp)

    def others(self):
        n_fsdp = 2 * self.n_z
        return [
            (self.dp_of(m), lax.rem(self.fsdp + k, n_fsdp))
            for m in range(self.n_dp)
            for k in range(n_fsdp)
            if m or k
        ]

    def greet(self, everyone=False):
        barrier = pltpu.get_barrier_semaphore()
        peers = [self.mate]
        peers += [self.z_peer(k) for k in range(1, self.n_z)]
        peers += [self.dp_peer(k) for k in range(1, self.n_dp)]
        if everyone:
            peers = self.others()
        for peer in peers:
            pl.semaphore_signal(barrier, inc=1, device_id=peer, device_id_type=MESH)
        pl.semaphore_wait(barrier, len(peers))


class Gather:
    def __init__(self, place, own, whole, send, recv):
        self.p, self.own, self.whole, self.send, self.recv = place, own, whole, send, recv

    def put(self, src, slot, peer, at):
        pltpu.make_async_remote_copy(
            src_ref=src,
            dst_ref=self.whole.at[slot, self.p.core],
            send_sem=self.send.at[at],
            recv_sem=self.recv.at[slot, self.p.core],
            device_id=peer,
            device_id_type=MESH,
        ).start()

    def pass_on(self, slot, peers, at):
        for i, peer in enumerate(peers):
            self.put(self.whole.at[slot, self.p.core], slot, peer, at + i)

    def landed(self, slot, core):
        there = self.whole.at[slot, core]
        pltpu.make_async_copy(there, there, self.recv.at[slot, core]).wait()

    def slot(self, corner, k):
        return self.p.corner(corner) * self.p.n_z + self.p.z_of(k)

    def side_peers(self):
        return [(self.p.corner(1), self.p.fsdp), (self.p.corner(2), self.p.fsdp), self.p.mate]

    def start(self):
        for k in range(1, self.p.n_z):
            self.put(self.own, self.p.slot, self.p.z_peer(k), k - 1)

    def spread(self):
        for i, peer in enumerate(self.side_peers()):
            self.put(self.own, self.p.slot, peer, self.p.n_z - 1 + i)

    def relay(self):
        for k in range(1, self.p.n_z):
            slot = self.slot(0, k)
            self.landed(slot, self.p.core)
            self.pass_on(slot, self.side_peers(), self.p.n_z - 1 + 3 * k)

    def cross(self):
        n_z = self.p.n_z
        first, second, mate = self.side_peers()
        at = 4 * n_z - 1
        for k in range(n_z):
            for corner, other in ((1, second), (2, first)):
                slot = self.slot(corner, k)
                self.landed(slot, self.p.core)
                early = k < n_z // 2
                peers = [mate, other] if early == (corner == 1) else [mate]
                self.pass_on(slot, peers, at)
                at += len(peers)

    def share(self):
        n_z = self.p.n_z
        for k in range(n_z):
            slot = self.slot(3, k)
            self.landed(slot, self.p.core)
            self.pass_on(slot, [self.p.mate], 7 * n_z - 1 + k)

    def finish(self):
        for k in range(self.p.n_z):
            for corner in range(4):
                self.landed(self.slot(corner, k), 1 - self.p.core)
        for at in range(self.sends(self.p.n_z)):
            pltpu.make_async_copy(self.own, self.own, self.send.at[at]).wait()

    @staticmethod
    def sends(n_z):
        return 8 * n_z - 1


class ShortGather(Gather):
    def side_peers(self):
        p = self.p
        return [(p.corner(i), p.fsdp) for i in (1, 2, 3)] + [p.mate]

    def relay(self):
        for k in range(1, self.p.n_z):
            slot = self.slot(0, k)
            self.landed(slot, self.p.core)
            self.pass_on(slot, self.side_peers(), self.p.n_z - 1 + 4 * k)

    def cross(self):
        n_z = self.p.n_z
        at = 5 * n_z - 1
        for k in range(n_z):
            for corner in (1, 2, 3):
                slot = self.slot(corner, k)
                self.landed(slot, self.p.core)
                self.pass_on(slot, [self.p.mate], at)
                at += 1

    def share(self):
        pass


def pipelined(items, ahead, behind, first, second, third):
    begun, done = {}, {}
    for at in range(-ahead, len(items) + behind):
        if 0 <= at + ahead < len(items):
            begun[at + ahead] = first(*items[at + ahead])
        if 0 <= at - behind < len(items):
            third(*items[at - behind], done.pop(at - behind))
        if 0 <= at < len(items):
            done[at] = second(*items[at], begun.pop(at))


def attention_kernel(mesh_sizes, gathers, sides, groups, lengths, x_ref, g_ref, *refs):
    n_dp, n_z = mesh_sizes
    if gathers:
        (qkv_s, wo_s, wu_s, wd_s, gains_s, biases_s, upb_s,
         qkv_ref, probs_ref, inv_ref, ct_ref, n1_ref, inv1_ref, r1_ref, a2_ref, gt_ref, norm2_ref, gsum_ref,
         early_ref, late_ref, wo_ref, wu_ref, wd_ref,
         wqkv_t, wo_t, xt_s, normed_s, a1_s, early, late, wo, wu, wd,
         early_own, late_own, wo_own, wu_own, wd_own, small, sems, rems) = refs
    else:
        (early, late, wo,
         qkv_ref, probs_ref, inv_ref, ct_ref, n1_ref, inv1_ref, r1_ref, a2_ref, gt_ref, norm2_ref, gsum_ref,
         wqkv_t, wo_t, xt_s, normed_s, a1_s) = refs
    step = pl.program_id(0)
    stage, group = step // groups, lax.rem(step, groups)
    many, seq, d = x_ref.shape
    head = d // HEADS
    side_rows, side_heads = d // sides, HEADS // sides
    cols = 3 * side_rows
    scale = head**-0.5

    if gathers:
        place = Place(n_dp, n_z)
        pairs = [(early_own, early)] + [(late_own.at[i], late.at[i]) for i in range(sides - 1)]
        pairs += [(wo_own, wo), (wu_own, wu), (wd_own, wd)]
        first, *rest, out, up, down = [
            (Gather if i else ShortGather)(place, own, whole, sems.at[i], rems.at[i])
            for i, (own, whole) in enumerate(pairs)
        ]
        here = (place.slot, place.core)

        def enter():
            rows = qkv_s.shape[0]
            small[...] = jnp.zeros_like(small)
            small[0:2, :rows] = gains_s[...]
            small[2:8, :rows] = biases_s[...]
            for r in range(upb_s.shape[1] // rows):
                small[8 + r : 9 + r, :rows] = upb_s[:, r * rows : (r + 1) * rows]
            for side in range(sides):
                own = late_own.at[side - 1] if side else early_own
                for part in range(3):
                    at = part * d + side * side_rows
                    own[:, part * side_rows : (part + 1) * side_rows] = qkv_s[:, at : at + side_rows].astype(BF)
            early_own[:, cols:] = small[...].T[:rows].astype(BF)
            place.greet()
            first.start()
            first.spread()
            wo_own[...] = wo_s[...].astype(BF)
            wu_own[...] = wu_s[...].astype(BF)
            wd_own[...] = wd_s[...].astype(BF)
            early[here] = early_own[...]
            for i in range(sides - 1):
                late[(i, *here)] = late_own[i]
            wo[here] = wo_own[...]
            wu[here] = wu_own[...]
            wd[here] = wd_own[...]

        plan, after = plan_forward(enter, first, rest[0], out, up, down)
        for at, actions in plan.items():

            @pl.when(step == at)
            def _(actions=actions):
                for action in actions:
                    action()

    def columns():
        return early[..., cols:].reshape(d, LANES).astype(F32)

    @pl.when(stage == 0)
    def _():
        tail = lax.broadcasted_iota(jnp.int32, (16, many * seq), 0)
        n1_ref[0, d:] = jnp.where(tail == 0, 1.0, 0.0).astype(BF)
        for s in range(many):
            at = slice(seq * s, seq * (s + 1))
            xt = x_ref[s].T
            xt_s[group, :, at] = xt
            normed, inverse = normalize(xt.astype(F32))
            normed_s[group, :, at] = normed
            n1_ref[0, :d, at] = normed.astype(BF)
            inv1_ref[group, :, at] = jnp.broadcast_to(inverse, (8, seq))
            gt = g_ref[s].T
            gt_ref[0, :, at] = gt
            term = lane_sums(gt.astype(F32))
            gsum_ref[...] = jnp.where((step == 0) & (s == 0), term, gsum_ref[...] + term)

    for side in range(sides):

        @pl.when(step == (side + 1) * groups)
        def _(side=side):
            if side:
                wqkv_t[...] = late[side - 1].reshape(d, cols).T
            else:
                wqkv_t[...] = early[..., :cols].reshape(d, cols).T
            if side == sides - 1:
                wo_t[...] = wo[...].reshape(d, d).T

    @pl.when(stage == 1)
    def _():
        column = columns()
        a1_s[group] = (normed_s[group] * column[:, 0:1] + column[:, 2:3]).astype(BF)

    def attended(group, s):
        at = slice(seq * s, seq * (s + 1))
        small = columns()
        term = dot(wo_t[...], ct_ref[group, :, at]) + small[:, 5:6]
        r1 = (xt_s[group, :, at].astype(F32) + term).astype(BF)
        r1_ref[0, :, at] = r1
        center, inverse, mean = center_of(r1.astype(F32))
        a2_ref[0, :, at] = (center * inverse * small[:, 1:2] + small[:, 6:7]).astype(BF)
        norm2_ref[group, :8, at] = jnp.broadcast_to(mean, (8, seq))
        norm2_ref[group, 8:, at] = jnp.broadcast_to(inverse, (8, seq))

    def heads(side, last):
        mine = pl.ds(pl.multiple_of(side * side_rows, side_rows), side_rows)
        qkv = qkv_ref.at[0]
        if early.ndim == 4:
            part = early.shape[0] // sides
            bias = early[pl.ds(side * part, part), :, :, cols:].reshape(side_rows, LANES)
        else:
            bias = early[mine, cols:]
        bias = bias.astype(F32)
        query = (dot(wqkv_t[:side_rows], a1_s[group]) + bias[:, 3:4]).astype(BF)
        qkv[:side_rows] = (query.astype(F32) * scale).astype(BF)
        qkv[side_rows : 2 * side_rows] = dot(wqkv_t[side_rows : 2 * side_rows], a1_s[group]).astype(BF)
        qkv[2 * side_rows :] = (dot(wqkv_t[2 * side_rows :], a1_s[group]) + bias[:, 4:5]).astype(BF)
        row = lax.broadcasted_iota(jnp.int32, (16, seq), 0)
        key = lax.broadcasted_iota(jnp.int32, (16, seq), 1)
        one = jnp.where(row == 0, 1.0, 0.0).astype(BF)
        masks = [
            jnp.where((row == 0) & (key >= lengths[group * many + s]), -1e30, 0.0).astype(BF)
            for s in range(many)
        ]
        items = [(s, h) for s in range(many) for h in range(side_heads)]

        def place_of(s, h, part):
            at = part * side_rows + h * head
            return slice(at, at + head), slice(seq * s, seq * (s + 1))

        def score(s, h):
            keys = jnp.concatenate([qkv[place_of(s, h, 1)], masks[s]], 0)
            queries = jnp.concatenate([qkv[place_of(s, h, 0)], one], 0)
            return dot(keys, queries, TN)

        def soften(s, h, scores):
            return jnp.exp(scores - jnp.max(scores, 0, keepdims=True)).astype(BF)

        def mix(s, h, exponent):
            probs_ref[0, s, h] = exponent
            values = jnp.concatenate([qkv[place_of(s, h, 2)], one], 0)
            mixed = dot(values, exponent)
            inverse = 1.0 / mixed[head : head + 1]
            inv_ref[side, group, pl.ds(s * side_heads + h, 1), :] = inverse
            to = pl.ds(pl.multiple_of(side * side_rows + h * head, head), head)
            ct_ref[group, to, seq * s : seq * (s + 1)] = (mixed[:head] * inverse).astype(BF)
            if last and h == 0:
                attended(jnp.maximum(group - 1, 0), s)

        pipelined(items, 3, 2, score, soften, mix)

    pl.when((stage > 0) & (stage < sides))(lambda: heads(stage - 1, False))
    pl.when(stage == sides)(lambda: heads(sides - 1, True))

    @pl.when(stage > sides)
    def _():
        for s in range(many):
            attended(groups - 1, s)


    if gathers:

        @pl.when(step == pl.num_programs(0) - 1)
        def _():
            for whole, to in ((early, early_ref), (late, late_ref), (wo, wo_ref)):
                to[...] = whole[...]
            for action in after:
                action()
            for whole, to in ((wu, wu_ref), (wd, wd_ref)):
                to[...] = whole[...]


def plan_forward(enter, first, late, out, up, down):
    plan = {
        0: [enter],
        2: [first.relay, late.start, out.start],
        3: [late.spread, out.spread],
        4: [first.cross, late.relay, first.share, out.relay, up.start, first.finish],
        5: [late.cross, out.cross, up.spread, down.start],
        6: [late.share, out.share, down.spread, up.relay],
        8: [late.finish, out.finish, down.relay],
        9: [up.cross],
        10: [down.cross, up.share],
        11: [down.share],
    }
    return plan, [up.finish, down.finish]


def forward_kernel(
    r1_ref, a2_ref, gt_ref, norm2_ref, gsum_ref, early_ref, wu_ref, wd_ref,
    out_ref, do_ref, dwu_ref, dwd_ref, small_ref,
    wu_t, wd_t, total_wu, total_wd, total_out, total_a2, u_s, dh_s, h_s, du_s, sums, sums_up, up_bias, *, block,
):
    step = pl.program_id(0)
    d, tokens = r1_ref.shape[1:]
    hidden = wu_t.shape[0]
    n_dev = dwd_ref.shape[0] * 2
    rows = d // n_dev
    seqs, seq = out_ref.shape[:2]
    cols = early_ref.shape[-1] - LANES
    column = early_ref[..., cols:].reshape(d, LANES).astype(F32)
    blocks = hidden // block
    slots = h_s.shape[0]
    a2, gt = a2_ref.at[0], gt_ref.at[0]

    @pl.when(step == 0)
    def _():
        wu_t[...] = wu_ref[...].reshape(d, hidden).T
        wd_t[...] = wd_ref[...].reshape(hidden, d).T
        sums[...] = jnp.zeros_like(sums)
        sums_up[...] = jnp.zeros_like(sums_up)
        for r in range(hidden // d):
            up_bias[:, r * rows : (r + 1) * rows, :] = jnp.broadcast_to(
                column[:, 8 + r : 9 + r].reshape(n_dev, rows, 1), (n_dev, rows, LANES)
            )

    per = block // (hidden // n_dev)

    def span(j):
        return slice(j * block, (j + 1) * block)

    def down_rows(j):
        if len(wd_ref.shape) == 2:
            return wd_ref[span(j)]
        unit = block // (2 * wd_ref.shape[2])
        return wd_ref[j * unit : (j + 1) * unit].reshape(block, d)

    def enter(j):
        bias = up_bias[j * per : (j + 1) * per].reshape(block, LANES)[:, 0:1]
        u_s[j % 2] = dot(wu_t[span(j)], a2[...]) + bias
        dh_s[j % 2] = dot(down_rows(j), gt[...])

    def bend(j):
        u = u_s[j % 2]
        square = u * u
        part = 0.5 + 0.5 * jnp.tanh(u * (C0 + C1 * square))
        h = u * part
        h_s[j % slots] = h.astype(BF)
        slope = part + h * (1.0 - part) * (2 * C0 + 6 * C1 * square)
        du = (dh_s[j % 2] * slope).astype(BF)
        du_s[j % slots] = du
        sums_up[span(j)] += lane_sums(du.astype(F32))

    def leave(j):
        term = dot(wd_t[:, span(j)], h_s[j % slots])
        total_out[...] = term if j == 0 else total_out[...] + term
        term = dot(wu_ref[..., span(j)].reshape(d, block), du_s[j % slots])
        total_a2[...] = term if j == 0 else total_a2[...] + term

    def weights(j):
        unit = block // (2 * dwd_ref.shape[2])
        at = slice(j * unit, (j + 1) * unit)
        term = dot(h_s[j % slots], gt[...], NT)
        term = jnp.where(step == 0, term, total_wd[span(j)] + term)
        total_wd[span(j)] = term
        dwd_ref[at] = term.astype(BF).reshape(unit, *dwd_ref.shape[1:])
        term = dot(a2[...], du_s[j % slots], NT)
        term = jnp.where(step == 0, term, total_wu[:, span(j)] + term)
        total_wu[:, span(j)] = term
        dwu_ref[..., span(j)] = term.astype(BF).reshape(*dwu_ref.shape[:3], block)

    def close():
        for s in range(seqs):
            at = slice(seq * s, seq * (s + 1))
            r1, g = r1_ref[0, :, at].astype(F32), gt[:, at].astype(F32)
            out_ref[s] = (r1 + total_out[:, at] + column[:, 7:8]).astype(BF).T
            da2, inverse = total_a2[:, at], norm2_ref[step, 8:9, at]
            n = (r1 - norm2_ref[step, 0:1, at]) * inverse
            dr1 = g + normalize_back(da2, n, inverse, column[:, 1:2])
            do_ref[step, :, at] = dr1.astype(BF)
            sums[0] += lane_sums(da2 * n)
            sums[1] += lane_sums(da2)

    enter(0)
    for j in range(blocks):
        if j + 1 < blocks:
            enter(j + 1)
        if j:
            leave(j - 1)
        bend(j)
        if 0 < j < blocks - 1:
            weights(j - 1)
    leave(blocks - 1)
    weights(blocks - 2)
    close()
    weights(blocks - 1)

    @pl.when(step == pl.num_programs(0) - 1)
    def _():
        lane = lax.broadcasted_iota(jnp.int32, (d, LANES), 1)
        small = jnp.zeros((d, LANES), F32)
        for total, at in ((sums[0], 1), (sums[1], 6), (gsum_ref[...], 7)):
            small = jnp.where(lane == at, jnp.sum(total, 1, keepdims=True), small)
        up = jnp.sum(sums_up[...], 1, keepdims=True).reshape(n_dev, hidden // n_dev, 1)
        for r in range(hidden // d):
            part = up[:, r * rows : (r + 1) * rows].reshape(d, 1)
            small = jnp.where(lane == 8 + r, part, small)
        small_ref[...] = small


class Scatter:
    def __init__(self, place, part, result, bufs, send, recv, flip=False):
        self.p, self.part, self.result = place, part, result
        self.sum1, self.got1, self.got2, self.sum2, self.got3 = bufs
        self.send, self.recv = send, recv
        p = place
        by_z = (p.n_z, p.z_peer, lambda far, near: p.dp_of(near) * p.n_z + p.z_of(far))
        by_dp = (p.n_dp, p.dp_peer, lambda far, near: p.dp_of(far) * p.n_z + p.z_of(near))
        (self.far, self.far_peer, self.slot), (self.near, self.near_peer, _) = (
            (by_z, by_dp) if flip else (by_dp, by_z)
        )

    @staticmethod
    def scratch(n_dp, n_z, rows, width, kind, flip=False):
        far, near = (n_z, n_dp) if flip else (n_dp, n_z)
        return [
            pltpu.VMEM((n_dp * n_z, rows, width), kind),
            pltpu.VMEM((n_dp * n_z, rows, width), kind),
            pltpu.VMEM((far - 1, near, rows, width), kind),
            pltpu.VMEM((near, rows, width), kind),
            pltpu.VMEM((near - 1, rows, width), kind),
        ]

    @staticmethod
    def sems(n_dp, n_z):
        return 1 + (max(n_dp, n_z) - 1) * max(n_dp, n_z) + max(n_dp, n_z) - 1

    def copy(self, src, dst, at, peer):
        return pltpu.make_async_remote_copy(
            src_ref=src,
            dst_ref=dst,
            send_sem=self.send.at[at],
            recv_sem=self.recv.at[at],
            device_id=peer,
            device_id_type=MESH,
        )

    def to_mate(self):
        return self.copy(self.sum1, self.got1, 0, self.p.mate)

    def afar(self):
        return [
            self.copy(
                self.sum1.at[self.slot(k, m)],
                self.got2.at[k - 1, m],
                1 + (k - 1) * self.near + m,
                self.far_peer(k),
            )
            for k in range(1, self.far)
            for m in range(self.near)
        ]

    def nearby(self):
        return [
            self.copy(
                self.sum2.at[m],
                self.got3.at[m - 1],
                1 + (self.far - 1) * self.near + m - 1,
                self.near_peer(m),
            )
            for m in range(1, self.near)
        ]

    def step1(self):
        def cast(s, _):
            self.sum1[s] = self.part[s, 1 - self.p.core].astype(self.sum1.dtype)
            return 0

        lax.fori_loop(0, self.p.n_dp * self.p.n_z, cast, 0)
        self.to_mate().start()

    def step2(self):
        self.to_mate().wait()

        def add(s, _):
            total = self.part[s, self.p.core].astype(F32) + self.got1[s].astype(F32)
            self.sum1[s] = total.astype(self.sum1.dtype)
            return 0

        lax.fori_loop(0, self.p.n_dp * self.p.n_z, add, 0)
        for copy in self.afar():
            copy.start()

    def step3(self):
        for copy in self.afar():
            copy.wait()
        for m in range(self.near):
            total = self.sum1[self.slot(0, m)].astype(F32)
            for k in range(self.far - 1):
                total = total + self.got2[k, m].astype(F32)
            self.sum2[m] = total.astype(self.sum2.dtype)
        for copy in self.nearby():
            copy.start()

    def step4(self):
        for copy in self.nearby():
            copy.wait()
        total = self.sum2[0].astype(F32)
        for m in range(self.near - 1):
            total = total + self.got3[m].astype(F32)
        self.result[...] = total


def backward_kernel(mesh_sizes, scatters, sides, groups, *refs):
    n_dp, n_z = mesh_sizes
    (do_ref, ct_ref, qkv_ref, probs_ref, inv_ref, n1_ref, inv1_ref,
     early_ref, late_ref, wo_ref, part_ref) = refs[:11]
    refs = refs[11:]
    if scatters:
        (dwu_ref, dwd_ref, tg_ref, gqkv_ref, gout_ref, gup_ref, gdown_ref, gsmall_ref,
         dp_s, total_qkv, total_out, sum_dp, dc_s, sums, part_small, gqkv_side) = refs[:16]
        buffers, (send, recv) = refs[16:-2], refs[-2:]
    else:
        (tg_ref, gqkv_ref, gout_ref, gsmall_ref, dp_s, total_qkv, total_out, sum_dp, dc_s, sums) = refs
    step = pl.program_id(0)
    last = pl.num_programs(0) - 1
    stage, group = step // groups, lax.rem(step, groups)
    d, width = do_ref.shape[1:]
    many, seq = tg_ref.shape[:2]
    head = d // HEADS
    side_rows, side_heads = d // sides, HEADS // sides
    cols = 3 * side_rows
    scale = head**-0.5
    opening = group == 0

    def columns():
        return early_ref[..., cols:].reshape(d, LANES).astype(F32)

    def side_weights(side):
        w = late_ref[side - 1] if side else early_ref[..., :cols]
        return w.reshape(d, cols)

    @pl.when(step == 0)
    def _():
        sums[...] = jnp.zeros_like(sums)

    def pack(side):
        n_slots, _, rows, _ = total_qkv.shape[1:]
        column, w = columns(), side_weights(side)
        row = sum_dp[side, 0:1]
        for slot in range(n_slots):
            at = slice(slot * 2 * rows, (slot + 1) * 2 * rows)
            product = total_qkv[side, slot].reshape(2 * rows, cols)
            piece = w[at].astype(F32)
            sums[0, at] += lane_sums(piece * product)
            sums[1, at] += lane_sums(piece * row)
            whole = column[at, 0:1] * product + column[at, 2:3] * row
            total_qkv[side, slot] = whole.reshape(2, rows, cols)

    def vectors():
        lane = lax.broadcasted_iota(jnp.int32, (d, LANES), 1)
        small = part_ref[...]
        for s, at in enumerate((0, 2, 3, 4, 5)):
            small = jnp.where(lane == at, jnp.sum(sums[s], 1, keepdims=True), small)
        return small

    if scatters:
        place = Place(n_dp, n_z)
        cut = dwd_ref.shape[2] // 2
        parts = [
            (dwu_ref, gup_ref, False),
            (dwd_ref.at[:, :, :cut], gdown_ref.at[:cut], False),
            (dwd_ref.at[:, :, cut:], gdown_ref.at[cut:], True),
            (total_out, gout_ref, False),
            (part_small, gsmall_ref, False),
        ]
        parts += [(total_qkv.at[i], gqkv_side.at[i], False) for i in range(sides)]
        up, down, down2, out, small, *qkvs = [
            Scatter(place, part, result, buffers[5 * i : 5 * i + 5], send.at[i], recv.at[i], flip)
            for i, (part, result, flip) in enumerate(parts)
        ]

        def pack_small():
            part_small[...] = vectors().reshape(part_small.shape)

        packs = [functools.partial(pack, i) for i in range(sides)]
        plan, after = plan_backward(place.greet, up, down, down2, out, small, qkvs, packs, pack_small)
        for at, actions in plan.items():

            @pl.when(step == at)
            def _(actions=actions):
                for action in actions:
                    action()

    @pl.when(stage == 0)
    def _():
        n_slots = total_out.shape[0]
        for part in range(2):
            at = slice(part * n_slots // 2, (part + 1) * n_slots // 2)
            term = dot(ct_ref[group, part * d // 2 : (part + 1) * d // 2], do_ref[group], NT)
            term = term.reshape(n_slots // 2, *total_out.shape[1:])
            total_out[at] = jnp.where(opening, term, total_out[at] + term)
        sums[4] += lane_sums(do_ref[group].astype(F32))

    def heads(side):
        mine = pl.ds(pl.multiple_of(side * side_rows, side_rows), side_rows)
        qkv, to = qkv_ref.at[0], dp_s.at[side, group]
        if len(wo_ref.shape) == 4:
            part = wo_ref.shape[0] // sides
            wo = wo_ref[pl.ds(side * part, part)].reshape(side_rows, d)
        else:
            wo = wo_ref[mine, :]
        dc_s[...] = dot(wo, do_ref[group])
        items = [(s, h) for s in range(many) for h in range(side_heads)]

        def place_of(s, h, part):
            at = part * side_rows + h * head
            return slice(at, at + head), slice(seq * s, seq * (s + 1))

        def grad_probs(s, h):
            inverse = inv_ref[side, group, pl.ds(s * side_heads + h, 1), :]
            dc = (dc_s[place_of(s, h, 0)] * inverse).astype(BF)
            return dc, dot(qkv[place_of(s, h, 2)], dc, TN)

        def grad_scores(s, h, begun):
            dc, term = begun
            there = pl.ds(pl.multiple_of(side * side_rows + h * head, head), head)
            delta = dc.astype(F32) * ct_ref[group, there, seq * s : seq * (s + 1)].astype(F32)
            delta = jnp.sum(delta, 0, keepdims=True)
            return dc, (probs_ref[0, s, h].astype(F32) * (term - delta)).astype(BF)

        def finish(s, h, done):
            dc, ds = done
            q, k, v = (place_of(s, h, part) for part in range(3))
            to[v] = dot(dc, probs_ref[0, s, h], NT).astype(BF)
            to[k] = dot(qkv[q], ds, NT).astype(BF)
            to[q] = (dot(qkv[k], ds) * scale).astype(BF)

        pipelined(items, 2, 1, grad_probs, grad_scores, finish)
        n_slots = total_qkv.shape[1]
        for part in range(2):
            at = slice(part * n_slots // 2, (part + 1) * n_slots // 2)
            term = dot(n1_ref[0, part * d // 2 : (d // 2, d + 16)[part]], to[...], NT)
            product = term[: d // 2].reshape(n_slots // 2, *total_qkv.shape[2:])
            total_qkv[side, at] = jnp.where(opening, product, total_qkv[side, at] + product)
        row = term[d // 2 : d // 2 + 8]
        sum_dp[side] = jnp.where(opening, row, sum_dp[side] + row)
        sums[2, mine, :] += lane_sums(to[:side_rows].astype(F32))
        sums[3, mine, :] += lane_sums(to[2 * side_rows :].astype(F32))

    pl.when(stage < sides)(lambda: heads(stage))

    @pl.when(stage == sides)
    def _():
        gain = columns()[:, 0:1]

        def product(s):
            at = slice(seq * s, seq * (s + 1))
            total = dot(side_weights(0), dp_s[0, group, :, at])
            for side in range(1, sides):
                total = total + dot(side_weights(side), dp_s[side, group, :, at])
            return total

        def finish(s, _, da1):
            at = slice(seq * s, seq * (s + 1))
            normed = n1_ref[0, :d, at].astype(F32)
            dv = normalize_back(da1, normed, inv1_ref[group, 0:1, at], gain)
            tg_ref[s] = (do_ref[group, :, at].astype(F32) + dv).astype(BF).T

        ahead = product(0)
        for s in range(many):
            da1, ahead = ahead, product(s + 1) if s + 1 < many else None
            finish(s, None, da1)

    @pl.when(step == last)
    def _():
        if scatters:
            for action in after:
                action()
            shards = gqkv_side
        else:
            for side in range(sides):
                pack(side)
            gout_ref[...] = total_out[...].reshape(d, d)
            gsmall_ref[...] = vectors()
            shards = total_qkv
        for side in range(sides):
            whole = shards[side].reshape(gqkv_ref.shape[0], cols)
            for part in range(3):
                at = part * d + side * side_rows
                gqkv_ref[:, at : at + side_rows] = whole[:, part * side_rows : (part + 1) * side_rows]


def plan_backward(greet, up, down, down2, out, small, qkvs, packs, pack_small):
    qkv0, qkv1 = qkvs
    plan = {
        0: [greet, up.step1, down2.step1, down.step1],
        1: [up.step2, down2.step2, down.step2],
        4: [packs[0], qkv0.step1, out.step1],
        5: [up.step3, down2.step3, qkv0.step2, out.step2],
        7: [down.step3],
        8: [packs[1], qkv1.step1, pack_small, small.step1, up.step4, down2.step4],
        9: [qkv1.step2, small.step2, qkv0.step3, out.step3],
        10: [down.step4],
        11: [qkv0.step4, out.step4],
    }
    return plan, [qkv1.step3, small.step3, qkv1.step4, small.step4]


def finish_kernel(tg, qkv, out, up, down, small, tg_to, qkv_to, out_to, up_to, down_to, gains, biases, upb, held, turn, sems):
    pieces = range(tg.shape[0])
    inward = [pltpu.make_async_copy(tg.at[s], held.at[s], sems.at[0, s]) for s in pieces]
    outward = [pltpu.make_async_copy(held.at[s], tg_to.at[s], sems.at[1, s]) for s in pieces]
    for copy in inward:
        copy.start()
    for source, to in ((qkv, qkv_to), (out, out_to), (up, up_to), (down, down_to)):
        to[...] = source[...]
    rows = small.shape[0]
    turn[...] = jnp.zeros_like(turn)
    turn[:rows] = small[...]
    turned = turn[...].T
    gains[...] = turned[0:2, :rows]
    biases[...] = turned[2:8, :rows]
    for r in range(upb.shape[1] // rows):
        upb[:, r * rows : (r + 1) * rows] = turned[8 + r : 9 + r, :rows]
    for copy, then in zip(inward, outward):
        copy.wait()
        then.start()
    for copy in outward:
        copy.wait()


def in_hbm(*arrays):
    return tuple(pltpu.with_memory_space_constraint(array, pltpu.HBM) for array in arrays)


def per_device(n_dp, n_fsdp, tokens, lengths, cotangent, qkv_w, out_w, up_w, down_w, gains, biases, up_bias):
    tokens, lengths, cotangent = in_hbm(tokens, lengths, cotangent)
    seqs, seq, d = tokens.shape
    n_z, n_dev = n_fsdp // 2, n_dp * n_fsdp
    rows, rows_down = qkv_w.shape[0], down_w.shape[0]
    hidden = up_w.shape[1]
    slots = n_dp * n_z
    axes = ("dp", "fsdp")
    direct = rows % 16 == 0 and n_dp == 4
    cut = n_dev if direct else 32
    quarter = hidden // d
    many = next(m for m in (3, 2, 1) if seqs % m == 0)
    groups, width = seqs // many, many * seq
    sides = 2
    side_rows, side_heads = d // sides, HEADS // sides
    cols = 3 * side_rows
    wide = cols + LANES

    def whole(shape):
        return pl.BlockSpec(shape, lambda i: (0,) * len(shape), pipeline_mode=pl.Buffered(1))

    def shape(dims, kind):
        return jax.ShapeDtypeStruct(dims, kind)

    anywhere = pl.BlockSpec(memory_space=pl.ANY)
    smem = pl.BlockSpec(memory_space=pltpu.SMEM)
    vmem = pl.BlockSpec(memory_space=pltpu.VMEM)
    probs_block = (1, many, side_heads, seq, seq)

    def params(mib, **more):
        return pltpu.CompilerParams(vmem_limit_bytes=int(mib * 2**20), **more)

    held = [
        pltpu.HBM((sides * groups, cols, width), BF),
        pltpu.HBM((sides * groups, *probs_block[1:]), BF),
        pltpu.VMEM((sides, groups, many * side_heads, seq), F32),
        pltpu.VMEM((groups, d, width), BF),
        pltpu.HBM((groups, d + 16, width), BF),
        pltpu.VMEM((groups, 8, width), F32),
        pltpu.HBM((groups, d, width), BF),
        pltpu.HBM((groups, d, width), BF),
        pltpu.HBM((groups, d, width), BF),
        pltpu.VMEM((groups, 16, width), F32),
        pltpu.VMEM((d, LANES), F32),
    ]
    held_specs = [vmem] * len(held)
    def working(i):
        return jnp.clip(i - groups, 0, sides * groups - 1)

    held_specs[0] = pl.BlockSpec((1, cols, width), lambda i: (working(i), 0, 0))
    held_specs[4] = pl.BlockSpec(
        (1, d + 16, width), lambda i: (jnp.minimum(i, groups - 1), 0, 0)
    )
    closing = pl.BlockSpec(
        (1, d, width), lambda i: (jnp.maximum(i - sides * groups - 1, 0), 0, 0)
    )
    held_specs[6] = held_specs[7] = closing
    held_specs[8] = pl.BlockSpec((1, d, width), lambda i: (jnp.minimum(i, groups - 1), 0, 0))
    held_specs[1] = pl.BlockSpec(
        probs_block, lambda i: (working(i), 0, 0, 0, 0)
    )
    in_specs = [
        smem,
    ] + [pl.BlockSpec((many, seq, d), lambda i: (jnp.minimum(i, groups - 1), 0, 0))] * 2
    scratch = [
        pltpu.VMEM((cols, d), BF),
        pltpu.VMEM((d, d), BF),
        pltpu.VMEM((groups, d, width), BF),
        pltpu.VMEM((groups, d, width), F32),
        pltpu.VMEM((groups, d, width), BF),
    ]
    steps = (1 + sides) * groups
    if direct:
        n_sends = Gather.sends(n_z)
        shards = in_hbm(qkv_w, out_w, up_w, down_w, gains, biases, up_bias.reshape(1, -1))
        qkv, probs, inv, ct, n1, inv1, r1, a2, gt, norm2, gsum, early, late, wo, wu, wd = pl.pallas_call(
            functools.partial(attention_kernel, (n_dp, n_z), True, sides, groups),
            grid=(steps + 1,),
            in_specs=in_specs + [whole(s.shape) for s in shards],
            out_specs=held_specs + [vmem] * 5,
            out_shape=held
            + [
                pltpu.VMEM((slots, 2, rows, wide), BF),
                pltpu.VMEM((sides - 1, slots, 2, rows, cols), BF),
                pltpu.VMEM((slots, 2, rows, d), BF),
                pltpu.VMEM((slots, 2, rows, hidden), BF),
                pltpu.VMEM((slots, 2, rows_down, d), BF),
            ],
            scratch_shapes=scratch
            + [
                pltpu.VMEM((slots, 2, rows, wide), BF),
                pltpu.VMEM((sides - 1, slots, 2, rows, cols), BF),
                pltpu.VMEM((slots, 2, rows, d), BF),
                pltpu.VMEM((slots, 2, rows, hidden), BF),
                pltpu.VMEM((slots, 2, rows_down, d), BF),
                pltpu.VMEM((rows, wide), BF),
                pltpu.VMEM((sides - 1, rows, cols), BF),
                pltpu.VMEM((rows, d), BF),
                pltpu.VMEM((rows, hidden), BF),
                pltpu.VMEM((rows_down, d), BF),
                pltpu.VMEM((LANES, LANES), F32),
                pltpu.SemaphoreType.DMA((sides + 3, n_sends)),
                pltpu.SemaphoreType.DMA((sides + 3, slots, 2)),
            ],
            compiler_params=params(VMEM_FORWARD, collective_id=0, has_side_effects=True),
            name="attention_forward",
        )(lengths, tokens, cotangent, *shards)
    else:
        split = [
            jnp.concatenate([qkv_w[:, p * d + i * side_rows :][:, :side_rows] for p in range(3)], 1)
            for i in range(sides)
        ]
        early = jnp.concatenate([split[0], gains.T, biases.T], 1).astype(BF)
        early = lax.all_gather(early, axes, axis=0, tiled=True)
        up_all = lax.all_gather(up_bias.astype(BF), axes, axis=0, tiled=True)
        up_all = up_all.reshape(cut, quarter, d // cut).swapaxes(1, 2).reshape(d, quarter)
        early = jnp.concatenate([early, up_all], 1)
        early = jnp.pad(early, ((0, 0), (0, wide - early.shape[1])))
        late = lax.all_gather(jnp.stack(split[1:]).astype(BF), axes, axis=1, tiled=True)
        wo = lax.all_gather(out_w.astype(BF), axes, axis=0, tiled=True)
        wu = lax.all_gather(up_w.astype(BF), axes, axis=0, tiled=True)
        wd = lax.all_gather(down_w.astype(BF), axes, axis=0, tiled=True)
        qkv, probs, inv, ct, n1, inv1, r1, a2, gt, norm2, gsum = pl.pallas_call(
            functools.partial(attention_kernel, (n_dp, n_z), False, sides, groups),
            grid=(steps + 1,),
            in_specs=in_specs + [whole(early.shape), whole(late.shape), whole(wo.shape)],
            out_specs=held_specs,
            out_shape=held,
            scratch_shapes=scratch,
            compiler_params=params(VMEM_FORWARD),
            name="attention_forward",
        )(lengths, tokens, cotangent, early, late, wo)

    r1, a2, gt, n1, qkv, probs = in_hbm(r1, a2, gt, n1, qkv, probs)

    def weight(array):
        return vmem if direct else whole(array.shape)

    block = d
    lag = 2
    parts = [
        pltpu.VMEM((cut // 2, 2, d // cut, hidden), BF),
        pltpu.VMEM((cut // 2, 2, hidden // cut, d), BF),
    ]
    part_specs = [vmem] * 2
    if not direct:
        parts = [shape(part.shape, BF) for part in parts]
        part_specs = [whole(part.shape) for part in parts]
    out, do, dwu, dwd, small = pl.pallas_call(
        functools.partial(forward_kernel, block=block),
        grid=(groups,),
        in_specs=[pl.BlockSpec((1, d, width), lambda i: (i, 0, 0))] * 3
        + [vmem] * 2
        + [weight(early), weight(wu), weight(wd)],
        out_specs=[pl.BlockSpec((many, seq, d), lambda i: (i, 0, 0)), vmem]
        + part_specs
        + [whole((d, LANES))],
        out_shape=[pltpu.HBM(tokens.shape, BF), pltpu.VMEM((groups, d, width), BF)]
        + parts
        + [shape((d, LANES), F32)],
        scratch_shapes=[pltpu.VMEM((hidden, d), BF), pltpu.VMEM((d, hidden), BF)]
        + [pltpu.VMEM((d, hidden), F32), pltpu.VMEM((hidden, d), F32)]
        + [pltpu.VMEM((d, width), F32)] * 2
        + [pltpu.VMEM((2, block, width), F32)] * 2
        + [pltpu.VMEM((lag, block, width), BF)] * 2
        + [
            pltpu.VMEM((2, d, LANES), F32),
            pltpu.VMEM((hidden, LANES), F32),
            pltpu.VMEM((cut, hidden // cut, LANES), F32),
        ],
        compiler_params=params(VMEM_MIDDLE if direct else VMEM_MIDDLE + 16),
        name="feed_forward",
    )(r1, a2, gt, norm2, gsum, early, wu, wd)

    seq_block = pl.BlockSpec((many, seq, d), lambda i: (jnp.maximum(i - sides * groups, 0), 0, 0))
    acts = (do, ct, qkv, probs, inv, n1, inv1, early, late, wo, small)
    acts_in = [vmem] * 7 + [weight(early), weight(late), weight(wo), whole((d, LANES))]
    acts_in[5] = pl.BlockSpec((1, d + 16, width), lambda i: (lax.rem(i, groups), 0, 0))
    acts_in[2] = pl.BlockSpec(
        (1, cols, width), lambda i: (jnp.minimum(i, sides * groups - 1), 0, 0)
    )
    acts_in[3] = pl.BlockSpec(
        probs_block, lambda i: (jnp.minimum(i, sides * groups - 1), 0, 0, 0, 0)
    )
    base = [
        pltpu.VMEM((sides, groups, cols, width), BF),
        pltpu.VMEM((sides, cut // 2, 2, d // cut, cols), F32),
        pltpu.VMEM((cut // 2, 2, d // cut, d), F32),
        pltpu.VMEM((sides, 8, cols), F32),
        pltpu.VMEM((side_rows, width), F32),
        pltpu.VMEM((5, d, LANES), F32),
    ]
    if direct:
        n_sems = Scatter.sems(n_dp, n_z)
        plan = [(rows, hidden, False), (rows_down // 2, d, False), (rows_down // 2, d, True), (rows, d, False), (rows, LANES, False)]
        plan += [(rows, cols, False)] * sides
        outs = [(rows, 3 * d), (rows, d), (rows, hidden), (rows_down, d), (rows, LANES)]
        scratch = base + [
            pltpu.VMEM((slots, 2, rows, LANES), F32),
            pltpu.VMEM((sides, rows, cols), F32),
        ]
        for height, across, flip in plan:
            scratch += Scatter.scratch(n_dp, n_z, height, across, BF, flip)
        scratch += [pltpu.SemaphoreType.DMA((len(plan), n_sems))] * 2
        grads = pl.pallas_call(
            functools.partial(backward_kernel, (n_dp, n_z), True, sides, groups),
            grid=(steps,),
            in_specs=acts_in + [vmem, vmem],
            out_specs=[seq_block] + [whole(o) for o in outs],
            out_shape=[pltpu.HBM(o, BF if i == 0 else F32) for i, o in enumerate([tokens.shape] + outs)],
            scratch_shapes=scratch,
            compiler_params=params(VMEM_BACKWARD, collective_id=1, has_side_effects=True),
            name="attention_backward",
        )(*acts, dwu, dwd)
        ends = [shape(tokens.shape, BF)] + [shape(o, F32) for o in outs[:4]]
        vectors = [shape(v, F32) for v in (gains.shape, biases.shape, (1, quarter * rows))]
        token_grad, gqkv, gout, gup, gdown, ggains, gbiases, gupb = pl.pallas_call(
            finish_kernel,
            in_specs=[anywhere] + [vmem] * 5,
            out_specs=[anywhere] + [vmem] * 7,
            out_shape=ends + vectors,
            scratch_shapes=[
                pltpu.VMEM(tokens.shape, BF),
                pltpu.VMEM((LANES, LANES), F32),
                pltpu.SemaphoreType.DMA((2, seqs)),
            ],
            compiler_params=params(60),
            name="hand_over",
        )(*grads)
        return out, token_grad, gqkv, gout, gup, gdown, ggains, gbiases, gupb.reshape(-1)

    token_grad, gqkv, gout, gsmall = pl.pallas_call(
        functools.partial(backward_kernel, (n_dp, n_z), False, sides, groups),
        grid=(steps,),
        in_specs=acts_in,
        out_specs=[seq_block, whole((d, 3 * d)), whole((d, d)), whole((d, LANES))],
        out_shape=[shape(tokens.shape, BF), shape((d, 3 * d), F32), shape((d, d), F32), shape((d, LANES), F32)],
        scratch_shapes=base,
        compiler_params=params(VMEM_BACKWARD),
        name="attention_backward",
    )(*acts)

    def scatter(term):
        return lax.psum_scatter(term.astype(F32), axes, scatter_dimension=0, tiled=True)

    up_sums = gsmall[:, 8 : 8 + quarter].reshape(cut, d // cut, quarter).swapaxes(1, 2)
    gsmall = scatter(gsmall[:, :8]).T
    return (
        out,
        token_grad,
        scatter(gqkv),
        scatter(gout),
        scatter(dwu.reshape(d, hidden)),
        scatter(dwd.reshape(hidden, d)),
        gsmall[:2],
        gsmall[2:8],
        scatter(up_sums.reshape(hidden)),
    )


def solution(mesh):
    axes = ("dp", "fsdp")
    rows, cols, flat = P(axes, None), P(None, axes), P(axes)
    data = P(axes, None, None)
    return jax.shard_map(
        functools.partial(per_device, mesh.shape["dp"], mesh.shape["fsdp"]),
        mesh=mesh,
        in_specs=(data, flat, data, rows, rows, rows, rows, cols, cols, flat),
        out_specs=(data, data, rows, rows, rows, rows, cols, cols, flat),
        check_vma=False,
    )
```

```python
import functools

import jax
import jax.numpy as jnp
from jax import lax
from jax.experimental import pallas as pl
from jax.experimental.pallas import tpu as pltpu
from jax.sharding import PartitionSpec as P

F32, BF = jnp.float32, jnp.bfloat16
MESH = pl.DeviceIdType.MESH
HEADS = 8
EPS = 1e-5
C0 = 0.7978845608028654
C1 = C0 * 0.044715
LANES = 128
NN = (((1,), (0,)), ((), ()))
NT = (((1,), (1,)), ((), ()))
TN = (((0,), (0,)), ((), ()))
VMEM_FORWARD, VMEM_MIDDLE, VMEM_BACKWARD = 40, 36, 36


def dot(a, b, dims=NN):
    return lax.dot_general(a, b, dims, preferred_element_type=F32)


def lane_sums(v):
    total = v[:, :LANES]
    for at in range(LANES, v.shape[1], LANES):
        total = total + v[:, at : at + LANES]
    return total


def center_of(v):
    mean = jnp.mean(v, 0, keepdims=True)
    center = v - mean
    inverse = lax.rsqrt(jnp.mean(center * center, 0, keepdims=True) + EPS)
    return center, inverse, mean


def normalize(v):
    center, inverse, _ = center_of(v)
    return center * inverse, inverse


def normalize_back(grad, normed, inverse, gain):
    scaled = grad * gain
    return inverse * (
        scaled
        - jnp.mean(scaled, 0, keepdims=True)
        - normed * jnp.mean(scaled * normed, 0, keepdims=True)
    )


class Place:
    def __init__(self, n_dp, n_z):
        self.n_dp, self.n_z = n_dp, n_z
        self.dp = lax.axis_index("dp")
        fsdp = lax.axis_index("fsdp")
        self.fsdp, self.z, self.core = fsdp, fsdp // 2, fsdp % 2
        self.slot = self.dp * n_z + self.z
        self.mate = (self.dp, self.z * 2 + 1 - self.core)

    def z_of(self, k):
        return lax.rem(self.z + k, self.n_z)

    def dp_of(self, k):
        return lax.rem(self.dp + k, self.n_dp)

    def corner(self, i):
        if i == 0:
            return self.dp
        low, high = lax.rem(self.dp, 2), self.dp // 2
        if i != 2:
            low = 1 - low
        if i != 1:
            high = 1 - high
        return high * 2 + low

    def z_peer(self, k):
        return (self.dp, self.z_of(k) * 2 + self.core)

    def dp_peer(self, k):
        return (self.dp_of(k), self.fsdp)

    def others(self):
        n_fsdp = 2 * self.n_z
        return [
            (self.dp_of(m), lax.rem(self.fsdp + k, n_fsdp))
            for m in range(self.n_dp)
            for k in range(n_fsdp)
            if m or k
        ]

    def greet(self, everyone=False):
        barrier = pltpu.get_barrier_semaphore()
        peers = [self.mate]
        peers += [self.z_peer(k) for k in range(1, self.n_z)]
        peers += [self.dp_peer(k) for k in range(1, self.n_dp)]
        if everyone:
            peers = self.others()
        for peer in peers:
            pl.semaphore_signal(barrier, inc=1, device_id=peer, device_id_type=MESH)
        pl.semaphore_wait(barrier, len(peers))


class Gather:
    def __init__(self, place, own, whole, send, recv):
        self.p, self.own, self.whole, self.send, self.recv = place, own, whole, send, recv

    def put(self, src, slot, peer, at):
        pltpu.make_async_remote_copy(
            src_ref=src,
            dst_ref=self.whole.at[slot, self.p.core],
            send_sem=self.send.at[at],
            recv_sem=self.recv.at[slot, self.p.core],
            device_id=peer,
            device_id_type=MESH,
        ).start()

    def pass_on(self, slot, peers, at):
        for i, peer in enumerate(peers):
            self.put(self.whole.at[slot, self.p.core], slot, peer, at + i)

    def landed(self, slot, core):
        there = self.whole.at[slot, core]
        pltpu.make_async_copy(there, there, self.recv.at[slot, core]).wait()

    def slot(self, corner, k):
        return self.p.corner(corner) * self.p.n_z + self.p.z_of(k)

    def side_peers(self):
        return [(self.p.corner(1), self.p.fsdp), (self.p.corner(2), self.p.fsdp), self.p.mate]

    def start(self):
        for k in range(1, self.p.n_z):
            self.put(self.own, self.p.slot, self.p.z_peer(k), k - 1)

    def spread(self):
        for i, peer in enumerate(self.side_peers()):
            self.put(self.own, self.p.slot, peer, self.p.n_z - 1 + i)

    def relay(self):
        for k in range(1, self.p.n_z):
            slot = self.slot(0, k)
            self.landed(slot, self.p.core)
            self.pass_on(slot, self.side_peers(), self.p.n_z - 1 + 3 * k)

    def cross(self):
        n_z = self.p.n_z
        first, second, mate = self.side_peers()
        at = 4 * n_z - 1
        for k in range(n_z):
            for corner, other in ((1, second), (2, first)):
                slot = self.slot(corner, k)
                self.landed(slot, self.p.core)
                early = k < n_z // 2
                peers = [mate, other] if early == (corner == 1) else [mate]
                self.pass_on(slot, peers, at)
                at += len(peers)

    def share(self):
        n_z = self.p.n_z
        for k in range(n_z):
            slot = self.slot(3, k)
            self.landed(slot, self.p.core)
            self.pass_on(slot, [self.p.mate], 7 * n_z - 1 + k)

    def finish(self):
        for k in range(self.p.n_z):
            for corner in range(4):
                self.landed(self.slot(corner, k), 1 - self.p.core)
        for at in range(self.sends(self.p.n_z)):
            pltpu.make_async_copy(self.own, self.own, self.send.at[at]).wait()

    @staticmethod
    def sends(n_z):
        return 8 * n_z - 1


class ShortGather(Gather):
    def side_peers(self):
        p = self.p
        return [(p.corner(i), p.fsdp) for i in (1, 2, 3)] + [p.mate]

    def relay(self):
        for k in range(1, self.p.n_z):
            slot = self.slot(0, k)
            self.landed(slot, self.p.core)
            self.pass_on(slot, self.side_peers(), self.p.n_z - 1 + 4 * k)

    def cross(self):
        n_z = self.p.n_z
        at = 5 * n_z - 1
        for k in range(n_z):
            for corner in (1, 2, 3):
                slot = self.slot(corner, k)
                self.landed(slot, self.p.core)
                self.pass_on(slot, [self.p.mate], at)
                at += 1

    def share(self):
        pass


def pipelined(items, ahead, behind, first, second, third):
    begun, done = {}, {}
    for at in range(-ahead, len(items) + behind):
        if 0 <= at + ahead < len(items):
            begun[at + ahead] = first(*items[at + ahead])
        if 0 <= at - behind < len(items):
            third(*items[at - behind], done.pop(at - behind))
        if 0 <= at < len(items):
            done[at] = second(*items[at], begun.pop(at))


def attention_kernel(mesh_sizes, gathers, sides, groups, lengths, x_ref, g_ref, *refs):
    n_dp, n_z = mesh_sizes
    if gathers:
        (qkv_s, wo_s, wu_s, wd_s, gains_s, biases_s, upb_s,
         qkv_ref, probs_ref, inv_ref, ct_ref, n1_ref, inv1_ref, r1_ref, a2_ref, gt_ref, norm2_ref, gsum_ref,
         early_ref, late_ref, wo_ref, wu_ref, wd_ref,
         wqkv_t, wo_t, xt_s, normed_s, a1_s, early, late, wo, wu, wd,
         early_own, late_own, wo_own, wu_own, wd_own, small, sems, rems) = refs
    else:
        (early, late, wo,
         qkv_ref, probs_ref, inv_ref, ct_ref, n1_ref, inv1_ref, r1_ref, a2_ref, gt_ref, norm2_ref, gsum_ref,
         wqkv_t, wo_t, xt_s, normed_s, a1_s) = refs
    step = pl.program_id(0)
    stage, group = step // groups, lax.rem(step, groups)
    many, seq, d = x_ref.shape
    head = d // HEADS
    side_rows, side_heads = d // sides, HEADS // sides
    cols = 3 * side_rows
    scale = head**-0.5

    if gathers:
        place = Place(n_dp, n_z)
        pairs = [(early_own, early)] + [(late_own.at[i], late.at[i]) for i in range(sides - 1)]
        pairs += [(wo_own, wo), (wu_own, wu), (wd_own, wd)]
        first, *rest, out, up, down = [
            (Gather if i else ShortGather)(place, own, whole, sems.at[i], rems.at[i])
            for i, (own, whole) in enumerate(pairs)
        ]
        here = (place.slot, place.core)

        def enter():
            rows = qkv_s.shape[0]
            small[...] = jnp.zeros_like(small)
            small[0:2, :rows] = gains_s[...]
            small[2:8, :rows] = biases_s[...]
            for r in range(upb_s.shape[1] // rows):
                small[8 + r : 9 + r, :rows] = upb_s[:, r * rows : (r + 1) * rows]
            for side in range(sides):
                own = late_own.at[side - 1] if side else early_own
                for part in range(3):
                    at = part * d + side * side_rows
                    own[:, part * side_rows : (part + 1) * side_rows] = qkv_s[:, at : at + side_rows].astype(BF)
            early_own[:, cols:] = small[...].T[:rows].astype(BF)
            place.greet()
            first.start()
            first.spread()
            wo_own[...] = wo_s[...].astype(BF)
            wu_own[...] = wu_s[...].astype(BF)
            wd_own[...] = wd_s[...].astype(BF)
            early[here] = early_own[...]
            for i in range(sides - 1):
                late[(i, *here)] = late_own[i]
            wo[here] = wo_own[...]
            wu[here] = wu_own[...]
            wd[here] = wd_own[...]

        plan, after = plan_forward(enter, first, rest[0], out, up, down)
        for at, actions in plan.items():

            @pl.when(step == at)
            def _(actions=actions):
                for action in actions:
                    action()

    def columns():
        return early[..., cols:].reshape(d, LANES).astype(F32)

    @pl.when(stage == 0)
    def _():
        tail = lax.broadcasted_iota(jnp.int32, (16, many * seq), 0)
        n1_ref[0, d:] = jnp.where(tail == 0, 1.0, 0.0).astype(BF)
        for s in range(many):
            at = slice(seq * s, seq * (s + 1))
            xt = x_ref[s].T
            xt_s[group, :, at] = xt
            normed, inverse = normalize(xt.astype(F32))
            normed_s[group, :, at] = normed
            n1_ref[0, :d, at] = normed.astype(BF)
            inv1_ref[group, :, at] = jnp.broadcast_to(inverse, (8, seq))
            gt = g_ref[s].T
            gt_ref[0, :, at] = gt
            term = lane_sums(gt.astype(F32))
            gsum_ref[...] = jnp.where((step == 0) & (s == 0), term, gsum_ref[...] + term)

    for side in range(sides):

        @pl.when(step == (side + 1) * groups)
        def _(side=side):
            if side:
                wqkv_t[...] = late[side - 1].reshape(d, cols).T
            else:
                wqkv_t[...] = early[..., :cols].reshape(d, cols).T
            if side == sides - 1:
                wo_t[...] = wo[...].reshape(d, d).T

    @pl.when(stage == 1)
    def _():
        column = columns()
        a1_s[group] = (normed_s[group] * column[:, 0:1] + column[:, 2:3]).astype(BF)

    def attended(group, s):
        at = slice(seq * s, seq * (s + 1))
        small = columns()
        term = dot(wo_t[...], ct_ref[group, :, at]) + small[:, 5:6]
        r1 = (xt_s[group, :, at].astype(F32) + term).astype(BF)
        r1_ref[0, :, at] = r1
        center, inverse, mean = center_of(r1.astype(F32))
        a2_ref[0, :, at] = (center * inverse * small[:, 1:2] + small[:, 6:7]).astype(BF)
        norm2_ref[group, :8, at] = jnp.broadcast_to(mean, (8, seq))
        norm2_ref[group, 8:, at] = jnp.broadcast_to(inverse, (8, seq))

    def heads(side, last):
        mine = pl.ds(pl.multiple_of(side * side_rows, side_rows), side_rows)
        qkv = qkv_ref.at[0]
        if early.ndim == 4:
            part = early.shape[0] // sides
            bias = early[pl.ds(side * part, part), :, :, cols:].reshape(side_rows, LANES)
        else:
            bias = early[mine, cols:]
        bias = bias.astype(F32)
        query = (dot(wqkv_t[:side_rows], a1_s[group]) + bias[:, 3:4]).astype(BF)
        qkv[:side_rows] = (query.astype(F32) * scale).astype(BF)
        qkv[side_rows : 2 * side_rows] = dot(wqkv_t[side_rows : 2 * side_rows], a1_s[group]).astype(BF)
        qkv[2 * side_rows :] = (dot(wqkv_t[2 * side_rows :], a1_s[group]) + bias[:, 4:5]).astype(BF)
        row = lax.broadcasted_iota(jnp.int32, (16, seq), 0)
        key = lax.broadcasted_iota(jnp.int32, (16, seq), 1)
        one = jnp.where(row == 0, 1.0, 0.0).astype(BF)
        masks = [
            jnp.where((row == 0) & (key >= lengths[group * many + s]), -1e30, 0.0).astype(BF)
            for s in range(many)
        ]
        items = [(s, h) for s in range(many) for h in range(side_heads)]

        def place_of(s, h, part):
            at = part * side_rows + h * head
            return slice(at, at + head), slice(seq * s, seq * (s + 1))

        def score(s, h):
            keys = jnp.concatenate([qkv[place_of(s, h, 1)], masks[s]], 0)
            queries = jnp.concatenate([qkv[place_of(s, h, 0)], one], 0)
            return dot(keys, queries, TN)

        def soften(s, h, scores):
            return jnp.exp(scores - jnp.max(scores, 0, keepdims=True)).astype(BF)

        def mix(s, h, exponent):
            probs_ref[0, s, h] = exponent
            values = jnp.concatenate([qkv[place_of(s, h, 2)], one], 0)
            mixed = dot(values, exponent)
            inverse = 1.0 / mixed[head : head + 1]
            inv_ref[side, group, pl.ds(s * side_heads + h, 1), :] = inverse
            to = pl.ds(pl.multiple_of(side * side_rows + h * head, head), head)
            ct_ref[group, to, seq * s : seq * (s + 1)] = (mixed[:head] * inverse).astype(BF)
            if last and h == 0:
                attended(jnp.maximum(group - 1, 0), s)

        pipelined(items, 3, 2, score, soften, mix)

    pl.when((stage > 0) & (stage < sides))(lambda: heads(stage - 1, False))
    pl.when(stage == sides)(lambda: heads(sides - 1, True))

    @pl.when(stage > sides)
    def _():
        for s in range(many):
            attended(groups - 1, s)


    if gathers:

        @pl.when(step == pl.num_programs(0) - 1)
        def _():
            for whole, to in ((early, early_ref), (late, late_ref), (wo, wo_ref)):
                to[...] = whole[...]
            for action in after:
                action()
            for last_gather, whole, to in ((up, wu, wu_ref), (down, wd, wd_ref)):
                last_gather.finish()
                to[...] = whole[...]


def plan_forward(enter, first, late, out, up, down):
    plan = {
        0: [enter],
        2: [first.relay, late.start, out.start],
        3: [late.spread, out.spread],
        4: [first.cross, late.relay, first.share, out.relay, up.start, first.finish],
        5: [late.cross, out.cross, up.spread, down.start],
        6: [late.share, out.share, down.spread, up.relay],
        8: [late.finish, out.finish, down.relay],
        9: [up.cross],
        10: [up.share, down.cross],
        12: [down.share],
    }
    return plan, []


def forward_kernel(
    r1_ref, a2_ref, gt_ref, norm2_ref, gsum_ref, early_ref, wu_ref, wd_ref,
    out_ref, do_ref, dwu_ref, dwd_ref, small_ref,
    wu_t, wd_t, total_wu, total_wd, total_out, total_a2, u_s, dh_s, h_s, du_s, sums, sums_up, up_bias, *, block,
):
    step = pl.program_id(0)
    d, tokens = r1_ref.shape[1:]
    hidden = wu_t.shape[0]
    n_dev = dwd_ref.shape[0] * 2
    rows = d // n_dev
    seqs, seq = out_ref.shape[:2]
    cols = early_ref.shape[-1] - LANES
    column = early_ref[..., cols:].reshape(d, LANES).astype(F32)
    blocks = hidden // block
    slots = h_s.shape[0]
    a2, gt = a2_ref.at[0], gt_ref.at[0]

    @pl.when(step == 0)
    def _():
        wu_t[...] = wu_ref[...].reshape(d, hidden).T
        wd_t[...] = wd_ref[...].reshape(hidden, d).T
        sums[...] = jnp.zeros_like(sums)
        sums_up[...] = jnp.zeros_like(sums_up)
        for r in range(hidden // d):
            up_bias[:, r * rows : (r + 1) * rows, :] = jnp.broadcast_to(
                column[:, 8 + r : 9 + r].reshape(n_dev, rows, 1), (n_dev, rows, LANES)
            )

    per = block // (hidden // n_dev)

    def span(j):
        return slice(j * block, (j + 1) * block)

    def down_rows(j):
        if len(wd_ref.shape) == 2:
            return wd_ref[span(j)]
        unit = block // (2 * wd_ref.shape[2])
        return wd_ref[j * unit : (j + 1) * unit].reshape(block, d)

    def enter(j):
        bias = up_bias[j * per : (j + 1) * per].reshape(block, LANES)[:, 0:1]
        u_s[j % 2] = dot(wu_t[span(j)], a2[...]) + bias
        dh_s[j % 2] = dot(down_rows(j), gt[...])

    def bend(j):
        u = u_s[j % 2]
        square = u * u
        part = 0.5 + 0.5 * jnp.tanh(u * (C0 + C1 * square))
        h = (u * part).astype(BF)
        h_s[j % slots] = h
        part = part.astype(BF)
        slope = part + h * (1.0 - part) * (2 * C0 + 6 * C1 * square).astype(BF)
        du = dh_s[j % 2].astype(BF) * slope
        du_s[j % slots] = du
        sums_up[span(j)] += lane_sums(du.astype(F32))

    def leave(j):
        term = dot(wd_t[:, span(j)], h_s[j % slots])
        total_out[...] = term if j == 0 else total_out[...] + term
        term = dot(wu_ref[..., span(j)].reshape(d, block), du_s[j % slots])
        total_a2[...] = term if j == 0 else total_a2[...] + term

    def weights(j):
        unit = block // (2 * dwd_ref.shape[2])
        at = slice(j * unit, (j + 1) * unit)
        term = dot(h_s[j % slots], gt[...], NT)
        term = jnp.where(step == 0, term, total_wd[span(j)] + term)
        total_wd[span(j)] = term
        dwd_ref[at] = term.astype(BF).reshape(unit, *dwd_ref.shape[1:])
        term = dot(a2[...], du_s[j % slots], NT)
        term = jnp.where(step == 0, term, total_wu[:, span(j)] + term)
        total_wu[:, span(j)] = term
        dwu_ref[..., span(j)] = term.astype(BF).reshape(*dwu_ref.shape[:3], block)

    def close():
        for s in range(seqs):
            at = slice(seq * s, seq * (s + 1))
            r1, g = r1_ref[0, :, at].astype(F32), gt[:, at].astype(F32)
            out_ref[s] = (r1 + total_out[:, at] + column[:, 7:8]).astype(BF).T
            da2, inverse = total_a2[:, at], norm2_ref[step, 8:9, at]
            n = (r1 - norm2_ref[step, 0:1, at]) * inverse
            dr1 = g + normalize_back(da2, n, inverse, column[:, 1:2])
            do_ref[step, :, at] = dr1.astype(BF)
            sums[0] += lane_sums(da2 * n)
            sums[1] += lane_sums(da2)

    enter(0)
    for j in range(blocks):
        if j + 1 < blocks:
            enter(j + 1)
        if j:
            leave(j - 1)
        bend(j)
        if 0 < j < blocks - 1:
            weights(j - 1)
    leave(blocks - 1)
    weights(blocks - 2)
    close()
    weights(blocks - 1)

    @pl.when(step == pl.num_programs(0) - 1)
    def _():
        lane = lax.broadcasted_iota(jnp.int32, (d, LANES), 1)
        small = jnp.zeros((d, LANES), F32)
        for total, at in ((sums[0], 1), (sums[1], 6), (gsum_ref[...], 7)):
            small = jnp.where(lane == at, jnp.sum(total, 1, keepdims=True), small)
        up = jnp.sum(sums_up[...], 1, keepdims=True).reshape(n_dev, hidden // n_dev, 1)
        for r in range(hidden // d):
            part = up[:, r * rows : (r + 1) * rows].reshape(d, 1)
            small = jnp.where(lane == 8 + r, part, small)
        small_ref[...] = small


class Scatter:
    def __init__(self, place, part, result, bufs, send, recv, flip=False):
        self.p, self.part, self.result = place, part, result
        self.sum1, self.got1, self.got2, self.sum2, self.got3 = bufs
        self.send, self.recv = send, recv
        p = place
        by_z = (p.n_z, p.z_peer, lambda far, near: p.dp_of(near) * p.n_z + p.z_of(far))
        by_dp = (p.n_dp, p.dp_peer, lambda far, near: p.dp_of(far) * p.n_z + p.z_of(near))
        (self.far, self.far_peer, self.slot), (self.near, self.near_peer, _) = (
            (by_z, by_dp) if flip else (by_dp, by_z)
        )

    @staticmethod
    def scratch(n_dp, n_z, rows, width, kind, flip=False):
        far, near = (n_z, n_dp) if flip else (n_dp, n_z)
        return [
            pltpu.VMEM((n_dp * n_z, rows, width), kind),
            pltpu.VMEM((n_dp * n_z, rows, width), kind),
            pltpu.VMEM((far - 1, near, rows, width), kind),
            pltpu.VMEM((near, rows, width), kind),
            pltpu.VMEM((near - 1, rows, width), kind),
        ]

    @staticmethod
    def sems(n_dp, n_z):
        return 1 + (max(n_dp, n_z) - 1) * max(n_dp, n_z) + max(n_dp, n_z) - 1

    def copy(self, src, dst, at, peer):
        return pltpu.make_async_remote_copy(
            src_ref=src,
            dst_ref=dst,
            send_sem=self.send.at[at],
            recv_sem=self.recv.at[at],
            device_id=peer,
            device_id_type=MESH,
        )

    def to_mate(self):
        return self.copy(self.sum1, self.got1, 0, self.p.mate)

    def afar(self):
        return [
            self.copy(
                self.sum1.at[self.slot(k, m)],
                self.got2.at[k - 1, m],
                1 + (k - 1) * self.near + m,
                self.far_peer(k),
            )
            for k in range(1, self.far)
            for m in range(self.near)
        ]

    def nearby(self):
        return [
            self.copy(
                self.sum2.at[m],
                self.got3.at[m - 1],
                1 + (self.far - 1) * self.near + m - 1,
                self.near_peer(m),
            )
            for m in range(1, self.near)
        ]

    def step1(self):
        def cast(s, _):
            self.sum1[s] = self.part[s, 1 - self.p.core].astype(self.sum1.dtype)
            return 0

        lax.fori_loop(0, self.p.n_dp * self.p.n_z, cast, 0)
        self.to_mate().start()

    def step2(self):
        self.to_mate().wait()

        def add(s, _):
            total = self.part[s, self.p.core].astype(F32) + self.got1[s].astype(F32)
            self.sum1[s] = total.astype(self.sum1.dtype)
            return 0

        lax.fori_loop(0, self.p.n_dp * self.p.n_z, add, 0)
        for copy in self.afar():
            copy.start()

    def step3(self):
        for copy in self.afar():
            copy.wait()
        for m in range(self.near):
            total = self.sum1[self.slot(0, m)].astype(F32)
            for k in range(self.far - 1):
                total = total + self.got2[k, m].astype(F32)
            self.sum2[m] = total.astype(self.sum2.dtype)
        for copy in self.nearby():
            copy.start()

    def step4(self):
        for copy in self.nearby():
            copy.wait()
        total = self.sum2[0].astype(F32)
        for m in range(self.near - 1):
            total = total + self.got3[m].astype(F32)
        self.result[...] = total


def backward_kernel(mesh_sizes, scatters, sides, groups, *refs):
    n_dp, n_z = mesh_sizes
    (do_ref, ct_ref, qkv_ref, probs_ref, inv_ref, n1_ref, inv1_ref,
     early_ref, late_ref, wo_ref, part_ref) = refs[:11]
    refs = refs[11:]
    if scatters:
        (dwu_ref, dwd_ref, tg_ref, gqkv_ref, gout_ref, gup_ref, gdown_ref, gsmall_ref,
         dp_s, total_qkv, total_out, sum_dp, dc_s, sums, part_small, gqkv_side) = refs[:16]
        buffers, (send, recv) = refs[16:-2], refs[-2:]
    else:
        (tg_ref, gqkv_ref, gout_ref, gsmall_ref, dp_s, total_qkv, total_out, sum_dp, dc_s, sums) = refs
    step = pl.program_id(0)
    last = pl.num_programs(0) - 1
    stage, group = step // groups, lax.rem(step, groups)
    d, width = do_ref.shape[1:]
    many, seq = tg_ref.shape[:2]
    head = d // HEADS
    side_rows, side_heads = d // sides, HEADS // sides
    cols = 3 * side_rows
    scale = head**-0.5
    opening = group == 0

    def columns():
        return early_ref[..., cols:].reshape(d, LANES).astype(F32)

    def side_weights(side):
        w = late_ref[side - 1] if side else early_ref[..., :cols]
        return w.reshape(d, cols)

    @pl.when(step == 0)
    def _():
        sums[...] = jnp.zeros_like(sums)

    def pack(side):
        n_slots, _, rows, _ = total_qkv.shape[1:]
        column, w = columns(), side_weights(side)
        row = sum_dp[side, 0:1]
        for slot in range(n_slots):
            at = slice(slot * 2 * rows, (slot + 1) * 2 * rows)
            product = total_qkv[side, slot].reshape(2 * rows, cols)
            piece = w[at].astype(F32)
            sums[0, at] += lane_sums(piece * product)
            sums[1, at] += lane_sums(piece * row)
            whole = column[at, 0:1] * product + column[at, 2:3] * row
            total_qkv[side, slot] = whole.reshape(2, rows, cols)

    def vectors():
        lane = lax.broadcasted_iota(jnp.int32, (d, LANES), 1)
        small = part_ref[...]
        for s, at in enumerate((0, 2, 3, 4, 5)):
            small = jnp.where(lane == at, jnp.sum(sums[s], 1, keepdims=True), small)
        return small

    if scatters:
        place = Place(n_dp, n_z)
        cut = dwd_ref.shape[2] // 2
        parts = [
            (dwu_ref, gup_ref, False),
            (dwd_ref.at[:, :, :cut], gdown_ref.at[:cut], False),
            (dwd_ref.at[:, :, cut:], gdown_ref.at[cut:], True),
            (total_out, gout_ref, False),
            (part_small, gsmall_ref, False),
        ]
        parts += [(total_qkv.at[i], gqkv_side.at[i], False) for i in range(sides)]
        up, down, down2, out, small, *qkvs = [
            Scatter(place, part, result, buffers[5 * i : 5 * i + 5], send.at[i], recv.at[i], flip)
            for i, (part, result, flip) in enumerate(parts)
        ]

        def pack_small():
            part_small[...] = vectors().reshape(part_small.shape)

        packs = [functools.partial(pack, i) for i in range(sides)]
        plan, after = plan_backward(place.greet, up, down, down2, out, small, qkvs, packs, pack_small)
        for at, actions in plan.items():

            @pl.when(step == at)
            def _(actions=actions):
                for action in actions:
                    action()

    @pl.when(stage == 0)
    def _():
        n_slots = total_out.shape[0]
        for part in range(2):
            at = slice(part * n_slots // 2, (part + 1) * n_slots // 2)
            term = dot(ct_ref[group, part * d // 2 : (part + 1) * d // 2], do_ref[group], NT)
            term = term.reshape(n_slots // 2, *total_out.shape[1:])
            total_out[at] = jnp.where(opening, term, total_out[at] + term)
        sums[4] += lane_sums(do_ref[group].astype(F32))

    def heads(side):
        mine = pl.ds(pl.multiple_of(side * side_rows, side_rows), side_rows)
        qkv, to = qkv_ref.at[0], dp_s.at[side, group]
        if len(wo_ref.shape) == 4:
            part = wo_ref.shape[0] // sides
            wo = wo_ref[pl.ds(side * part, part)].reshape(side_rows, d)
        else:
            wo = wo_ref[mine, :]
        dc_s[...] = dot(wo, do_ref[group])
        items = [(s, h) for s in range(many) for h in range(side_heads)]

        def place_of(s, h, part):
            at = part * side_rows + h * head
            return slice(at, at + head), slice(seq * s, seq * (s + 1))

        def grad_probs(s, h):
            inverse = inv_ref[side, group, pl.ds(s * side_heads + h, 1), :]
            dc = (dc_s[place_of(s, h, 0)] * inverse).astype(BF)
            return dc, dot(qkv[place_of(s, h, 2)], dc, TN)

        def grad_scores(s, h, begun):
            dc, term = begun
            there = pl.ds(pl.multiple_of(side * side_rows + h * head, head), head)
            delta = dc.astype(F32) * ct_ref[group, there, seq * s : seq * (s + 1)].astype(F32)
            delta = jnp.sum(delta, 0, keepdims=True)
            return dc, (probs_ref[0, s, h].astype(F32) * (term - delta)).astype(BF)

        def finish(s, h, done):
            dc, ds = done
            q, k, v = (place_of(s, h, part) for part in range(3))
            to[v] = dot(dc, probs_ref[0, s, h], NT).astype(BF)
            to[k] = dot(qkv[q], ds, NT).astype(BF)
            to[q] = (dot(qkv[k], ds) * scale).astype(BF)

        pipelined(items, 2, 1, grad_probs, grad_scores, finish)
        n_slots = total_qkv.shape[1]
        for part in range(2):
            at = slice(part * n_slots // 2, (part + 1) * n_slots // 2)
            term = dot(n1_ref[0, part * d // 2 : (d // 2, d + 16)[part]], to[...], NT)
            product = term[: d // 2].reshape(n_slots // 2, *total_qkv.shape[2:])
            total_qkv[side, at] = jnp.where(opening, product, total_qkv[side, at] + product)
        row = term[d // 2 : d // 2 + 8]
        sum_dp[side] = jnp.where(opening, row, sum_dp[side] + row)
        sums[2, mine, :] += lane_sums(to[:side_rows].astype(F32))
        sums[3, mine, :] += lane_sums(to[2 * side_rows :].astype(F32))

    pl.when(stage < sides)(lambda: heads(stage))

    @pl.when(stage == sides)
    def _():
        gain = columns()[:, 0:1]

        def product(s):
            at = slice(seq * s, seq * (s + 1))
            total = dot(side_weights(0), dp_s[0, group, :, at])
            for side in range(1, sides):
                total = total + dot(side_weights(side), dp_s[side, group, :, at])
            return total

        def finish(s, _, da1):
            at = slice(seq * s, seq * (s + 1))
            normed = n1_ref[0, :d, at].astype(F32)
            dv = normalize_back(da1, normed, inv1_ref[group, 0:1, at], gain)
            tg_ref[s] = (do_ref[group, :, at].astype(F32) + dv).astype(BF).T

        ahead = product(0)
        for s in range(many):
            da1, ahead = ahead, product(s + 1) if s + 1 < many else None
            finish(s, None, da1)

    @pl.when(step == last)
    def _():
        if scatters:
            for action in after:
                action()
            shards = gqkv_side
        else:
            for side in range(sides):
                pack(side)
            gout_ref[...] = total_out[...].reshape(d, d)
            gsmall_ref[...] = vectors()
            shards = total_qkv
        for side in range(sides):
            whole = shards[side].reshape(gqkv_ref.shape[0], cols)
            for part in range(3):
                at = part * d + side * side_rows
                gqkv_ref[:, at : at + side_rows] = whole[:, part * side_rows : (part + 1) * side_rows]


def plan_backward(greet, up, down, down2, out, small, qkvs, packs, pack_small):
    qkv0, qkv1 = qkvs
    plan = {
        0: [greet, up.step1, down2.step1, down.step1],
        1: [up.step2, down2.step2, down.step2],
        4: [packs[0], qkv0.step1, out.step1],
        5: [up.step3, down2.step3, qkv0.step2, out.step2],
        7: [down.step3],
        8: [packs[1], qkv1.step1, pack_small, small.step1, up.step4, down2.step4],
        9: [qkv1.step2, small.step2],
        10: [qkv0.step3, out.step3, down.step4],
    }
    return plan, [qkv1.step3, small.step3, qkv0.step4, out.step4, qkv1.step4, small.step4]


def finish_kernel(tg, qkv, out, up, down, small, tg_to, qkv_to, out_to, up_to, down_to, gains, biases, upb, held, turn, sems):
    pieces = range(tg.shape[0])
    inward = [pltpu.make_async_copy(tg.at[s], held.at[s], sems.at[0, s]) for s in pieces]
    outward = [pltpu.make_async_copy(held.at[s], tg_to.at[s], sems.at[1, s]) for s in pieces]
    for copy in inward:
        copy.start()
    for source, to in ((qkv, qkv_to), (out, out_to), (up, up_to), (down, down_to)):
        to[...] = source[...]
    rows = small.shape[0]
    turn[...] = jnp.zeros_like(turn)
    turn[:rows] = small[...]
    turned = turn[...].T
    gains[...] = turned[0:2, :rows]
    biases[...] = turned[2:8, :rows]
    for r in range(upb.shape[1] // rows):
        upb[:, r * rows : (r + 1) * rows] = turned[8 + r : 9 + r, :rows]
    for copy, then in zip(inward, outward):
        copy.wait()
        then.start()
    for copy in outward:
        copy.wait()


def in_hbm(*arrays):
    return tuple(pltpu.with_memory_space_constraint(array, pltpu.HBM) for array in arrays)


def per_device(n_dp, n_fsdp, tokens, lengths, cotangent, qkv_w, out_w, up_w, down_w, gains, biases, up_bias):
    tokens, lengths, cotangent = in_hbm(tokens, lengths, cotangent)
    seqs, seq, d = tokens.shape
    n_z, n_dev = n_fsdp // 2, n_dp * n_fsdp
    rows, rows_down = qkv_w.shape[0], down_w.shape[0]
    hidden = up_w.shape[1]
    slots = n_dp * n_z
    axes = ("dp", "fsdp")
    direct = rows % 16 == 0 and n_dp == 4
    cut = n_dev if direct else 32
    quarter = hidden // d
    many = next(m for m in (3, 2, 1) if seqs % m == 0)
    groups, width = seqs // many, many * seq
    sides = 2
    side_rows, side_heads = d // sides, HEADS // sides
    cols = 3 * side_rows
    wide = cols + LANES

    def whole(shape):
        return pl.BlockSpec(shape, lambda i: (0,) * len(shape), pipeline_mode=pl.Buffered(1))

    def shape(dims, kind):
        return jax.ShapeDtypeStruct(dims, kind)

    anywhere = pl.BlockSpec(memory_space=pl.ANY)
    smem = pl.BlockSpec(memory_space=pltpu.SMEM)
    vmem = pl.BlockSpec(memory_space=pltpu.VMEM)
    probs_block = (1, many, side_heads, seq, seq)

    def params(mib, **more):
        return pltpu.CompilerParams(vmem_limit_bytes=int(mib * 2**20), **more)

    held = [
        pltpu.HBM((sides * groups, cols, width), BF),
        pltpu.HBM((sides * groups, *probs_block[1:]), BF),
        pltpu.VMEM((sides, groups, many * side_heads, seq), F32),
        pltpu.VMEM((groups, d, width), BF),
        pltpu.HBM((groups, d + 16, width), BF),
        pltpu.VMEM((groups, 8, width), F32),
        pltpu.HBM((groups, d, width), BF),
        pltpu.HBM((groups, d, width), BF),
        pltpu.HBM((groups, d, width), BF),
        pltpu.VMEM((groups, 16, width), F32),
        pltpu.VMEM((d, LANES), F32),
    ]
    held_specs = [vmem] * len(held)
    def working(i):
        return jnp.clip(i - groups, 0, sides * groups - 1)

    held_specs[0] = pl.BlockSpec((1, cols, width), lambda i: (working(i), 0, 0))
    held_specs[4] = pl.BlockSpec(
        (1, d + 16, width), lambda i: (jnp.minimum(i, groups - 1), 0, 0)
    )
    closing = pl.BlockSpec(
        (1, d, width), lambda i: (jnp.maximum(i - sides * groups - 1, 0), 0, 0)
    )
    held_specs[6] = held_specs[7] = closing
    held_specs[8] = pl.BlockSpec((1, d, width), lambda i: (jnp.minimum(i, groups - 1), 0, 0))
    held_specs[1] = pl.BlockSpec(
        probs_block, lambda i: (working(i), 0, 0, 0, 0)
    )
    in_specs = [
        smem,
    ] + [pl.BlockSpec((many, seq, d), lambda i: (jnp.minimum(i, groups - 1), 0, 0))] * 2
    scratch = [
        pltpu.VMEM((cols, d), BF),
        pltpu.VMEM((d, d), BF),
        pltpu.VMEM((groups, d, width), BF),
        pltpu.VMEM((groups, d, width), F32),
        pltpu.VMEM((groups, d, width), BF),
    ]
    steps = (1 + sides) * groups
    if direct:
        n_sends = Gather.sends(n_z)
        shards = in_hbm(qkv_w, out_w, up_w, down_w, gains, biases, up_bias.reshape(1, -1))
        qkv, probs, inv, ct, n1, inv1, r1, a2, gt, norm2, gsum, early, late, wo, wu, wd = pl.pallas_call(
            functools.partial(attention_kernel, (n_dp, n_z), True, sides, groups),
            grid=(steps + 1,),
            in_specs=in_specs + [whole(s.shape) for s in shards],
            out_specs=held_specs + [vmem] * 5,
            out_shape=held
            + [
                pltpu.VMEM((slots, 2, rows, wide), BF),
                pltpu.VMEM((sides - 1, slots, 2, rows, cols), BF),
                pltpu.VMEM((slots, 2, rows, d), BF),
                pltpu.VMEM((slots, 2, rows, hidden), BF),
                pltpu.VMEM((slots, 2, rows_down, d), BF),
            ],
            scratch_shapes=scratch
            + [
                pltpu.VMEM((slots, 2, rows, wide), BF),
                pltpu.VMEM((sides - 1, slots, 2, rows, cols), BF),
                pltpu.VMEM((slots, 2, rows, d), BF),
                pltpu.VMEM((slots, 2, rows, hidden), BF),
                pltpu.VMEM((slots, 2, rows_down, d), BF),
                pltpu.VMEM((rows, wide), BF),
                pltpu.VMEM((sides - 1, rows, cols), BF),
                pltpu.VMEM((rows, d), BF),
                pltpu.VMEM((rows, hidden), BF),
                pltpu.VMEM((rows_down, d), BF),
                pltpu.VMEM((LANES, LANES), F32),
                pltpu.SemaphoreType.DMA((sides + 3, n_sends)),
                pltpu.SemaphoreType.DMA((sides + 3, slots, 2)),
            ],
            compiler_params=params(VMEM_FORWARD, collective_id=0, has_side_effects=True),
            name="attention_forward",
        )(lengths, tokens, cotangent, *shards)
    else:
        split = [
            jnp.concatenate([qkv_w[:, p * d + i * side_rows :][:, :side_rows] for p in range(3)], 1)
            for i in range(sides)
        ]
        early = jnp.concatenate([split[0], gains.T, biases.T], 1).astype(BF)
        early = lax.all_gather(early, axes, axis=0, tiled=True)
        up_all = lax.all_gather(up_bias.astype(BF), axes, axis=0, tiled=True)
        up_all = up_all.reshape(cut, quarter, d // cut).swapaxes(1, 2).reshape(d, quarter)
        early = jnp.concatenate([early, up_all], 1)
        early = jnp.pad(early, ((0, 0), (0, wide - early.shape[1])))
        late = lax.all_gather(jnp.stack(split[1:]).astype(BF), axes, axis=1, tiled=True)
        wo = lax.all_gather(out_w.astype(BF), axes, axis=0, tiled=True)
        wu = lax.all_gather(up_w.astype(BF), axes, axis=0, tiled=True)
        wd = lax.all_gather(down_w.astype(BF), axes, axis=0, tiled=True)
        qkv, probs, inv, ct, n1, inv1, r1, a2, gt, norm2, gsum = pl.pallas_call(
            functools.partial(attention_kernel, (n_dp, n_z), False, sides, groups),
            grid=(steps + 1,),
            in_specs=in_specs + [whole(early.shape), whole(late.shape), whole(wo.shape)],
            out_specs=held_specs,
            out_shape=held,
            scratch_shapes=scratch,
            compiler_params=params(VMEM_FORWARD),
            name="attention_forward",
        )(lengths, tokens, cotangent, early, late, wo)

    r1, a2, gt, n1, qkv, probs = in_hbm(r1, a2, gt, n1, qkv, probs)

    def weight(array):
        return vmem if direct else whole(array.shape)

    block = d
    lag = 2
    parts = [
        pltpu.VMEM((cut // 2, 2, d // cut, hidden), BF),
        pltpu.VMEM((cut // 2, 2, hidden // cut, d), BF),
    ]
    part_specs = [vmem] * 2
    if not direct:
        parts = [shape(part.shape, BF) for part in parts]
        part_specs = [whole(part.shape) for part in parts]
    out, do, dwu, dwd, small = pl.pallas_call(
        functools.partial(forward_kernel, block=block),
        grid=(groups,),
        in_specs=[pl.BlockSpec((1, d, width), lambda i: (i, 0, 0))] * 3
        + [vmem] * 2
        + [weight(early), weight(wu), weight(wd)],
        out_specs=[pl.BlockSpec((many, seq, d), lambda i: (i, 0, 0)), vmem]
        + part_specs
        + [whole((d, LANES))],
        out_shape=[pltpu.HBM(tokens.shape, BF), pltpu.VMEM((groups, d, width), BF)]
        + parts
        + [shape((d, LANES), F32)],
        scratch_shapes=[pltpu.VMEM((hidden, d), BF), pltpu.VMEM((d, hidden), BF)]
        + [pltpu.VMEM((d, hidden), F32), pltpu.VMEM((hidden, d), F32)]
        + [pltpu.VMEM((d, width), F32)] * 2
        + [pltpu.VMEM((2, block, width), F32)] * 2
        + [pltpu.VMEM((lag, block, width), BF)] * 2
        + [
            pltpu.VMEM((2, d, LANES), F32),
            pltpu.VMEM((hidden, LANES), F32),
            pltpu.VMEM((cut, hidden // cut, LANES), F32),
        ],
        compiler_params=params(VMEM_MIDDLE if direct else VMEM_MIDDLE + 16),
        name="feed_forward",
    )(r1, a2, gt, norm2, gsum, early, wu, wd)

    seq_block = pl.BlockSpec((many, seq, d), lambda i: (jnp.maximum(i - sides * groups, 0), 0, 0))
    acts = (do, ct, qkv, probs, inv, n1, inv1, early, late, wo, small)
    acts_in = [vmem] * 7 + [weight(early), weight(late), weight(wo), whole((d, LANES))]
    acts_in[5] = pl.BlockSpec((1, d + 16, width), lambda i: (lax.rem(i, groups), 0, 0))
    acts_in[2] = pl.BlockSpec(
        (1, cols, width), lambda i: (jnp.minimum(i, sides * groups - 1), 0, 0)
    )
    acts_in[3] = pl.BlockSpec(
        probs_block, lambda i: (jnp.minimum(i, sides * groups - 1), 0, 0, 0, 0)
    )
    base = [
        pltpu.VMEM((sides, groups, cols, width), BF),
        pltpu.VMEM((sides, cut // 2, 2, d // cut, cols), F32),
        pltpu.VMEM((cut // 2, 2, d // cut, d), F32),
        pltpu.VMEM((sides, 8, cols), F32),
        pltpu.VMEM((side_rows, width), F32),
        pltpu.VMEM((5, d, LANES), F32),
    ]
    if direct:
        n_sems = Scatter.sems(n_dp, n_z)
        plan = [(rows, hidden, False), (rows_down // 2, d, False), (rows_down // 2, d, True), (rows, d, False), (rows, LANES, False)]
        plan += [(rows, cols, False)] * sides
        outs = [(rows, 3 * d), (rows, d), (rows, hidden), (rows_down, d), (rows, LANES)]
        scratch = base + [
            pltpu.VMEM((slots, 2, rows, LANES), F32),
            pltpu.VMEM((sides, rows, cols), F32),
        ]
        for height, across, flip in plan:
            scratch += Scatter.scratch(n_dp, n_z, height, across, BF, flip)
        scratch += [pltpu.SemaphoreType.DMA((len(plan), n_sems))] * 2
        grads = pl.pallas_call(
            functools.partial(backward_kernel, (n_dp, n_z), True, sides, groups),
            grid=(steps,),
            in_specs=acts_in + [vmem, vmem],
            out_specs=[seq_block] + [whole(o) for o in outs],
            out_shape=[pltpu.HBM(o, BF if i == 0 else F32) for i, o in enumerate([tokens.shape] + outs)],
            scratch_shapes=scratch,
            compiler_params=params(VMEM_BACKWARD, collective_id=1, has_side_effects=True),
            name="attention_backward",
        )(*acts, dwu, dwd)
        ends = [shape(tokens.shape, BF)] + [shape(o, F32) for o in outs[:4]]
        vectors = [shape(v, F32) for v in (gains.shape, biases.shape, (1, quarter * rows))]
        token_grad, gqkv, gout, gup, gdown, ggains, gbiases, gupb = pl.pallas_call(
            finish_kernel,
            in_specs=[anywhere] + [vmem] * 5,
            out_specs=[anywhere] + [vmem] * 7,
            out_shape=ends + vectors,
            scratch_shapes=[
                pltpu.VMEM(tokens.shape, BF),
                pltpu.VMEM((LANES, LANES), F32),
                pltpu.SemaphoreType.DMA((2, seqs)),
            ],
            compiler_params=params(60),
            name="hand_over",
        )(*grads)
        return out, token_grad, gqkv, gout, gup, gdown, ggains, gbiases, gupb.reshape(-1)

    token_grad, gqkv, gout, gsmall = pl.pallas_call(
        functools.partial(backward_kernel, (n_dp, n_z), False, sides, groups),
        grid=(steps,),
        in_specs=acts_in,
        out_specs=[seq_block, whole((d, 3 * d)), whole((d, d)), whole((d, LANES))],
        out_shape=[shape(tokens.shape, BF), shape((d, 3 * d), F32), shape((d, d), F32), shape((d, LANES), F32)],
        scratch_shapes=base,
        compiler_params=params(VMEM_BACKWARD),
        name="attention_backward",
    )(*acts)

    def scatter(term):
        return lax.psum_scatter(term.astype(F32), axes, scatter_dimension=0, tiled=True)

    up_sums = gsmall[:, 8 : 8 + quarter].reshape(cut, d // cut, quarter).swapaxes(1, 2)
    gsmall = scatter(gsmall[:, :8]).T
    return (
        out,
        token_grad,
        scatter(gqkv),
        scatter(gout),
        scatter(dwu.reshape(d, hidden)),
        scatter(dwd.reshape(hidden, d)),
        gsmall[:2],
        gsmall[2:8],
        scatter(up_sums.reshape(hidden)),
    )


def solution(mesh):
    axes = ("dp", "fsdp")
    rows, cols, flat = P(axes, None), P(None, axes), P(axes)
    data = P(axes, None, None)
    return jax.shard_map(
        functools.partial(per_device, mesh.shape["dp"], mesh.shape["fsdp"]),
        mesh=mesh,
        in_specs=(data, flat, data, rows, rows, rows, rows, cols, cols, flat),
        out_specs=(data, data, rows, rows, rows, rows, cols, cols, flat),
        check_vma=False,
    )
```
